32 devices in a mesh: gx: 4 (over y, x), gy: 4 (over z), gz: 2 (over core).
Axes of the slice: x: 2, y: 2, z: 4, core: 2. Of those that a mesh axis runs over, the one named last changes fastest.
Arguments:
- orbitals: float32 [64, 64, 32, 64], P('gx', 'gy', 'gz'), may hold values from -6 to 6
- potential: float32 [64, 64, 32], P('gx', 'gy', 'gz'), may hold values from -1.5 to 1
Outputs:
- basis: float32 [64, 64, 32, 64], P('gx', 'gy', 'gz')
- blocks: float32 [4, 4, 2, 7, 64, 64], P('gx', 'gy', 'gz')
The draws below stay inside these ranges and needn't reach their ends.
All inputs are finite; a program needn't handle non-finite values.
Results may differ from the reference program's by a relative error of at most 0.0003.
Values sent between devices are 32-bit elements; how exact they have to be, the bound alone decides.
No kernel may reach another device: no remote copies, remote signals or barrier semaphores. Data moves between devices by JAX's collectives and lax.ppermute only.
A program may use at most 128 MiB of HBM per device.

```python
import jax
import jax.numpy as jnp
import numpy as np
from jax import lax

ORBITALS = 64
CELLS = 16
BUF = 3
DEGREE = 2
EXT = 22
NX = 64
NY = 64
NZ = 32
N_GX = 4
N_GY = 4
N_GZ = 2


def block_scale(key, extent, pieces, low, top_value):
    def one(dim, parts):
        draws = jax.random.uniform(jax.random.fold_in(jax.random.fold_in(key, 6), dim), (parts,), jnp.float32, low / len(pieces), top_value / len(pieces))
        return jnp.repeat(jnp.exp(draws), extent[dim] // parts).reshape((-1,) + (1,) * (len(extent) - dim - 1))

    loudness = one(*pieces[0])
    for cut in pieces[1:]:
        loudness = loudness * one(*cut)
    return loudness


def noise(own_key, dims, deviation, limit, shards=(), kind=jnp.bfloat16):
    drawn = deviation * jax.random.normal(own_key, dims, jnp.float32)
    if shards:
        drawn = drawn * block_scale(own_key, dims, shards, -0.22, 0.18)
    return jnp.clip(drawn, -limit, limit).astype(kind)


def setup_inputs(seed: int = 0) -> dict:
    splits = jax.random.split(jax.random.key(seed), 3)
    orbitals = noise(splits[0], (NX, NY, NZ, ORBITALS), 1.0, 6.0, ((0, 4), (1, 4), (2, 2)), jnp.float32)
    potential = jnp.clip(-1.5 + 2.5 * jax.random.uniform(splits[1], (NX, NY, NZ), jnp.float32) ** block_scale(splits[1], (NX, NY, NZ), ((0, 4), (1, 4), (2, 2)), -0.2, 0.2), -1.5, 1.0)
    return dict(orbitals=orbitals, potential=potential)


PENALTY = 2.0
LOW_BOUND = -1.5
CUTOFF = 8.0
HIGH_BOUND = 16.0


def spectral_tables(points):
    indices = np.arange(points)
    offsets = indices[:, None] - indices[None, :]
    nyquist = points // 2
    deriv_one = np.zeros((points, points))
    deriv_two = np.zeros((points, points))
    for harmonic in range(1, nyquist):
        wavenum = 2.0 * np.pi * harmonic / points
        deriv_one = deriv_one - 2.0 * wavenum * np.sin(wavenum * offsets) / points
        deriv_two = deriv_two - 2.0 * wavenum * wavenum * np.cos(wavenum * offsets) / points
    deriv_two = deriv_two - np.pi * np.pi * np.cos(np.pi * offsets) / points
    return jnp.asarray(deriv_one, jnp.float32), jnp.asarray(deriv_two, jnp.float32)


def apply_along(matrix, field, axis_pos):
    forms = ("ia,ajko->ijko", "ja,iako->ijko", "ka,ijao->ijko")
    return jnp.einsum(forms[axis_pos], matrix, field, precision=lax.Precision.HIGHEST)


def hamiltonian(field, ext_pot, deriv_two):
    laplace = apply_along(deriv_two, field, 0) + apply_along(deriv_two, field, 1)
    laplace = laplace + apply_along(deriv_two, field, 2)
    return -0.5 * laplace + ext_pot[..., None] * field


def chebyshev(start, ext_pot, deriv_two, degree):
    half_width = (HIGH_BOUND - CUTOFF) / 2.0
    center = (HIGH_BOUND + CUTOFF) / 2.0
    scale_now = half_width / (LOW_BOUND - center)
    tau_factor = 2.0 / scale_now
    previous = start
    current = (hamiltonian(start, ext_pot, deriv_two) - center * start) * (scale_now / half_width)
    for iteration in range(1, degree):
        scale_next = 1.0 / (tau_factor - scale_now)
        applied = hamiltonian(current, ext_pot, deriv_two) - center * current
        following = applied * (2.0 * scale_next / half_width) - (scale_now * scale_next) * previous
        previous = current
        current = following
        scale_now = scale_next
    return current


def element_fields(ext_orb, ext_pot, deriv_one, deriv_two, margin, cells, degree):
    filtered = chebyshev(ext_orb, ext_pot, deriv_two, degree)
    stop = margin + cells
    row_block = deriv_one[margin:stop]
    interior = filtered[margin:stop, margin:stop, margin:stop]
    grad_x = apply_along(row_block, filtered[:, margin:stop, margin:stop], 0)
    grad_y = apply_along(row_block, filtered[margin:stop, :, margin:stop], 1)
    grad_z = apply_along(row_block, filtered[margin:stop, margin:stop, :], 2)
    return interior, grad_x, grad_y, grad_z


def face_product(left, right):
    return jnp.einsum("...pqi,...pqj->...ij", left, right, precision=lax.Precision.HIGHEST)


def neighbour_block(own_value, own_deriv, other_value, other_deriv, sign):
    skew = face_product(own_deriv, other_value) - face_product(own_value, other_deriv)
    return 0.25 * sign * skew - 0.5 * PENALTY * face_product(own_value, other_value)


def own_face(value, deriv, sign):
    mixed = face_product(value, deriv) + face_product(deriv, value)
    return -0.25 * sign * mixed + 0.5 * PENALTY * face_product(value, value)


def assemble(interior, gradients, pot_el, lowers, uppers):
    volume_form = "...xyzi,...xyzj->...ij"
    diagonal = jnp.einsum(volume_form, interior, pot_el[..., None] * interior, precision=lax.Precision.HIGHEST)
    for axis_pos in range(3):
        diagonal = diagonal + 0.5 * jnp.einsum(volume_form, gradients[axis_pos], gradients[axis_pos], precision=lax.Precision.HIGHEST)
    cells = interior.shape[-2]
    coupled = []
    for axis_pos in range(3):
        grid_axis = interior.ndim - 4 + axis_pos
        low_value = jnp.take(interior, 0, axis=grid_axis)
        low_deriv = jnp.take(gradients[axis_pos], 0, axis=grid_axis)
        high_value = jnp.take(interior, cells - 1, axis=grid_axis)
        high_deriv = jnp.take(gradients[axis_pos], cells - 1, axis=grid_axis)
        diagonal = diagonal + own_face(low_value, low_deriv, -1.0)
        diagonal = diagonal + own_face(high_value, high_deriv, 1.0)
        coupled.append(neighbour_block(low_value, low_deriv, lowers[axis_pos][0], lowers[axis_pos][1], -1.0))
        coupled.append(neighbour_block(high_value, high_deriv, uppers[axis_pos][0], uppers[axis_pos][1], 1.0))
    return jnp.stack([diagonal] + coupled, axis=-3)


def reference(orbitals, potential):
    deriv_one, deriv_two = spectral_tables(EXT)
    offsets = jnp.arange(EXT, dtype=jnp.int32) - BUF

    def one_element(flat_index):
        elem_x = flat_index // (N_GY * N_GZ)
        elem_y = (flat_index // N_GZ) % N_GY
        elem_z = flat_index % N_GZ
        rows_x = ((elem_x * CELLS + offsets) % NX).astype(jnp.int32)
        rows_y = ((elem_y * CELLS + offsets) % NY).astype(jnp.int32)
        rows_z = ((elem_z * CELLS + offsets) % NZ).astype(jnp.int32)
        ext_orb = jnp.take(jnp.take(jnp.take(orbitals, rows_x, axis=0), rows_y, axis=1), rows_z, axis=2)
        ext_pot = jnp.take(jnp.take(jnp.take(potential, rows_x, axis=0), rows_y, axis=1), rows_z, axis=2)
        return element_fields(ext_orb, ext_pot, deriv_one, deriv_two, BUF, CELLS, DEGREE)

    fields = lax.map(one_element, jnp.arange(N_GX * N_GY * N_GZ, dtype=jnp.int32))
    full_shape = (N_GX, N_GY, N_GZ, CELLS, CELLS, CELLS, ORBITALS)
    interior = fields[0].reshape(full_shape)
    gradients = (fields[1].reshape(full_shape), fields[2].reshape(full_shape), fields[3].reshape(full_shape))
    pot_el = potential.reshape(N_GX, CELLS, N_GY, CELLS, N_GZ, CELLS).transpose(0, 2, 4, 1, 3, 5)
    lowers = []
    uppers = []
    for axis_pos in range(3):
        grid_axis = 3 + axis_pos
        lowers.append((jnp.roll(jnp.take(interior, CELLS - 1, axis=grid_axis), 1, axis=axis_pos),
                       jnp.roll(jnp.take(gradients[axis_pos], CELLS - 1, axis=grid_axis), 1, axis=axis_pos)))
        uppers.append((jnp.roll(jnp.take(interior, 0, axis=grid_axis), -1, axis=axis_pos),
                       jnp.roll(jnp.take(gradients[axis_pos], 0, axis=grid_axis), -1, axis=axis_pos)))
    blocks = assemble(interior, gradients, pot_el, lowers, uppers)
    basis = interior.transpose(0, 3, 1, 4, 2, 5, 6).reshape(NX, NY, NZ, ORBITALS)
    return basis, blocks
```

```python
import functools

import jax
import jax.numpy as jnp
import ml_dtypes
import numpy as np
from jax import lax
from jax.experimental import pallas as pl
from jax.experimental.pallas import tpu as pltpu
from jax.sharding import PartitionSpec as P

BUF = 3
PENALTY = 2.0
LOW_BOUND = -1.5
CUTOFF = 8.0
HIGH_BOUND = 16.0
LIMIT = 56 * 1024 * 1024
BF = jnp.bfloat16
F32 = jnp.float32


class Plan:
    def __init__(self, cells, width):
        self.cells, self.width = cells, width
        self.ext = cells + 2 * BUF
        self.groups = self.ext // 2
        self.inner = cells // 2
        self.lanes = 2 * width
        self.face = cells * cells
        self.yext = self.ext * cells
        self.plane = -(-self.ext // 8) * 8
        self.strip = BUF * cells
        self.rows = self.yext + 2 * BUF * self.plane
        self.trows = -(-self.ext // 8) * 8
        order = list(range(BUF, BUF + cells)) + list(range(BUF)) + list(range(BUF + cells, self.ext))
        points = []
        for y in order:
            points += [(y, BUF + z) for z in range(cells)]
        for z in list(range(BUF)) + list(range(BUF + cells, self.ext)):
            points += [(y, z) for y in order] + [None] * (self.plane - self.ext)
        self.points = points
        self.first, self.second = spectral(self.ext)
        inside = np.zeros(self.ext)
        inside[BUF : BUF + cells] = 1.0
        self.inside = inside


def spectral(points):
    indices = np.arange(points)
    offsets = indices[:, None] - indices[None, :]
    first = np.zeros((points, points))
    second = np.zeros((points, points))
    for harmonic in range(1, points // 2):
        wavenum = 2.0 * np.pi * harmonic / points
        first = first - 2.0 * wavenum * np.sin(wavenum * offsets) / points
        second = second - 2.0 * wavenum * wavenum * np.cos(wavenum * offsets) / points
    second = second - np.pi * np.pi * np.cos(np.pi * offsets) / points
    return first, second


def row_matrix(plan, along, masked):
    out = np.zeros((plan.rows, plan.rows))
    for r, p in enumerate(plan.points):
        if p is None:
            continue
        for q, s in enumerate(plan.points):
            if s is None:
                continue
            if p[1] == s[1] and (not masked or plan.inside[p[1]]):
                out[r, q] += along[p[0], s[0]]
            if p[0] == s[0] and (not masked or plan.inside[p[0]]):
                out[r, q] += along[p[1], s[1]]
    return out


def mirrored(plan, along):
    n, g = plan.ext, plan.groups
    plus = along[:g, :g] + along[:g, ::-1][:, :g]
    minus = along[:g, :g] - along[:g, ::-1][:, :g]
    return np.concatenate([np.repeat(plus[:, :, None], plan.width, 2), np.repeat(minus[:, :, None], plan.width, 2)], 2)


def face_rows(plan):
    c = plan.cells
    index = {p: r for r, p in enumerate(plan.points) if p is not None}
    out = np.zeros((4 * c, plan.rows))
    for side, layer in enumerate((BUF, BUF + c - 1)):
        for z in range(c):
            for y in range(plan.ext):
                out[side * c + z, index[(y, BUF + z)]] = plan.first[layer, y]
        for y in range(c):
            for z in range(plan.ext):
                out[(2 + side) * c + y, index[(BUF + y, z)]] = plan.first[layer, z]
    return out


def energy(plan):
    c = plan.cells
    block = plan.first[BUF : BUF + c]
    out = 0.5 * block.T @ block
    for sign, layer in ((-1.0, BUF), (1.0, BUF + c - 1)):
        unit = np.zeros(plan.ext)
        unit[layer] = 1.0
        cross = np.outer(unit, plan.first[layer])
        out = out + 0.5 * PENALTY * np.outer(unit, unit) - 0.25 * sign * (cross + cross.T)
    return out


def halves(matrix):
    high = matrix.astype(np.float32).astype(ml_dtypes.bfloat16)
    low = (matrix - high.astype(np.float64)).astype(np.float32).astype(ml_dtypes.bfloat16)
    return high, low


def split(x):
    high = x.astype(BF)
    return high, (x - high.astype(F32)).astype(BF)


def swap(x):
    return pltpu.roll(x, x.shape[-1] // 2, x.ndim - 1)


def dot(a, b):
    return jnp.dot(a, b, preferred_element_type=F32)


def dot_t(a, b):
    return lax.dot_general(a, b, (((0,), (0,)), ((), ())), preferred_element_type=F32)


def exact(a, b):
    return jnp.dot(a, b, preferred_element_type=F32, precision=lax.Precision.HIGHEST)


def low_lanes(shape):
    return lax.broadcasted_iota(jnp.int32, shape, len(shape) - 1) < shape[-1] // 2


def pack_kernel(plan, orb, pot, spread, pick, xlo, xhi, ylo, yhi, inner, vt):
    c, w = plan.cells, plan.width
    half = plan.face // 2
    for s in range(BUF):
        for out, x in ((xlo, s), (xhi, c - BUF + s)):
            out[s * half : (s + 1) * half, :] = jnp.concatenate([orb[x, :half], orb[x, half:]], axis=1)
    for j in range(plan.inner):
        a, b = orb[j], orb[c - 1 - j]
        e = jnp.concatenate([a + b, a - b], axis=1)
        inner[j] = e
        ylo[j * plan.strip : (j + 1) * plan.strip, :] = e[: plan.strip]
        yhi[j * plan.strip : (j + 1) * plan.strip, :] = e[plan.face - plan.strip :]
    wide = exact(pot[...], spread[...]) * pick[...]
    v = wide.reshape(c, c, plan.face).sum(axis=1)
    vt[...] = v
    lanes = plan.lanes
    base = BUF * half
    xlo[base:, :] = jnp.zeros((8, lanes), F32)
    xhi[base:, :] = jnp.zeros((8, lanes), F32)
    for part in range(2):
        cols = slice(part * lanes, (part + 1) * lanes)
        xlo[base + part * BUF : base + (part + 1) * BUF, :] = v[:BUF, cols]
        xhi[base + part * BUF : base + (part + 1) * BUF, :] = v[c - BUF :, cols]
    ybase = plan.inner * plan.strip
    ylo[ybase:, :] = v[:, :lanes]
    yhi[ybase:, :] = v[:, plan.face - lanes :]


def xhalo_kernel(plan, lo, hi, outer, elo, ehi):
    half = plan.face // 2
    lanes = plan.lanes
    mask = low_lanes((half, lanes))
    for g in range(BUF):
        a = lo[g * half : (g + 1) * half, :]
        b = hi[(BUF - 1 - g) * half : (BUF - g) * half, :]
        s, d = a + b, a - b
        top = jnp.where(mask, s, swap(d))
        bottom = jnp.where(mask, swap(s), d)
        outer[g, :half] = top
        outer[g, half:] = bottom
        elo[g * plan.strip : (g + 1) * plan.strip, :] = top[: plan.strip]
        ehi[g * plan.strip : (g + 1) * plan.strip, :] = bottom[half - plan.strip :]
    base, ebase = BUF * half, BUF * plan.strip
    elo[ebase:, :] = jnp.zeros((8, lanes), F32)
    ehi[ebase:, :] = jnp.zeros((8, lanes), F32)
    for k, src in enumerate((lo, hi)):
        elo[ebase + k * BUF : ebase + (k + 1) * BUF, :] = src[base : base + BUF, :]
        ehi[ebase + k * BUF : ebase + (k + 1) * BUF, :] = src[base + BUF : base + 2 * BUF, :]


def zpack_kernel(plan, inner, outer, vt, xlo, xhi, ylo, yhi, elo, ehi, zpick, field, vfull, z):
    c, lanes, strip, face = plan.cells, plan.lanes, plan.strip, plan.face
    for g in range(BUF):
        field[g, :face] = outer[g]
        field[g, face : face + strip] = elo[g * strip : (g + 1) * strip, :]
        field[g, face + strip : face + 2 * strip] = ehi[g * strip : (g + 1) * strip, :]
    for j in range(plan.inner):
        g = BUF + j
        field[g, :face] = inner[j]
        field[g, face : face + strip] = ylo[j * strip : (j + 1) * strip, :]
        field[g, face + strip : face + 2 * strip] = yhi[j * strip : (j + 1) * strip, :]
    pad = field.shape[1] - plan.yext
    field[:, plan.yext :] = jnp.zeros((plan.groups, pad, lanes), F32)
    plane = plan.plane
    span = BUF * plane
    for side, start in ((0, 0), (1, c - BUF)):
        for g in range(plan.groups):
            for k in range(BUF):
                at = g * span + k * plane
                z[side, at : at + plane, :] = field[g, pl.ds(start + k, plane, stride=c), :]
    base, ebase, ybase = BUF * (face // 2), BUF * strip, plan.inner * strip
    vfull[...] = jnp.zeros(vfull.shape, F32)
    for part in range(2):
        cols = slice(part * lanes, (part + 1) * lanes)
        vfull[:BUF, cols] = xlo[base + part * BUF : base + (part + 1) * BUF, :]
        vfull[BUF + c : plan.ext, cols] = xhi[base + part * BUF : base + (part + 1) * BUF, :]
    vfull[BUF : BUF + c, :face] = vt[...]
    shift = lanes - strip
    vfull[:BUF, face : face + strip] = elo[ebase : ebase + BUF, :][:, shift:]
    vfull[BUF + c : plan.ext, face : face + strip] = elo[ebase + BUF : ebase + 2 * BUF, :][:, shift:]
    vfull[BUF : BUF + c, face : face + strip] = ylo[ybase:, :][:, shift:]
    vfull[:BUF, face + strip : face + 2 * strip] = ehi[ebase : ebase + BUF, :][:, :strip]
    vfull[BUF + c : plan.ext, face + strip : face + 2 * strip] = ehi[ebase + BUF : ebase + 2 * BUF, :][:, :strip]
    vfull[BUF : BUF + c, face + strip : face + 2 * strip] = yhi[ybase:, :][:, :strip]
    for side in range(2):
        z[side, plan.groups * span :, :] = exact(vfull[...], zpick[side])


def mix(plan, coef, table, g, src, r0, r1):
    total = None
    for s in range(plan.groups):
        term = coef[table + s : table + s + 1, :] * src[s, r0:r1, :]
        total = term if total is None else total + term
    return total


def chunks(stop, size=16):
    return [(r, min(r + size, stop)) for r in range(0, stop, size)]


def filter_kernel(plan, field, zlo, zhi, vfull, wh, wl, coef, dcoef, vspread, fh, fl,
                  basis, out, mxlo, mxhi, mylo, myhi, mzlo, mzhi, va_out, vd_out,
                  x, xh, xl, y, yh, yl, va, vd, acc, dacc):
    g_all, lanes, rows, face = plan.groups, plan.lanes, plan.rows, plan.face
    span = BUF * plan.plane
    c = plan.cells
    half_width = (HIGH_BOUND - CUTOFF) / 2.0
    center = (HIGH_BOUND + CUTOFF) / 2.0
    s0 = half_width / (LOW_BOUND - center)
    s1 = 1.0 / (2.0 / s0 - s0)

    def put(dst, dh, dl, g, r0, r1, value):
        dst[g, r0:r1, :] = value
        h, l = split(value)
        dh[r0:r1, g * lanes : (g + 1) * lanes] = h
        dl[r0:r1, g * lanes : (g + 1) * lanes] = l

    for g in range(g_all):
        put(x, xh, xl, g, 0, plan.yext, field[g, : plan.yext, :])
        put(x, xh, xl, g, plan.yext, plan.yext + span, zlo[g * span : (g + 1) * span, :])
        put(x, xh, xl, g, plan.yext + span, rows, zhi[g * span : (g + 1) * span, :])
    pieces = ((0, vfull[...], plan.yext), (plan.yext, zlo[g_all * span :, :], span), (plan.yext + span, zhi[g_all * span :, :], span))
    for at, piece, count in pieces:
        turned = jnp.transpose(piece)[:count, :]
        both = exact(turned, vspread[...])
        for g in range(g_all):
            va[g, at : at + count, :] = both[:, g * lanes : (g + 1) * lanes]
            vd[g, at : at + count, :] = both[:, (g_all + g) * lanes : (g_all + g + 1) * lanes]

    def apply(src, sh, sl, finish):
        for g0 in range(0, g_all, 2):
            g1 = min(g0 + 2, g_all)
            cols = slice(g0 * lanes, g1 * lanes)
            acc[:, : (g1 - g0) * lanes] = (
                dot(wh[...], sh[:, cols]) + dot(wl[...], sh[:, cols]) + dot(wh[...], sl[:, cols])
            )
            for g in range(g0, g1):
                for r0, r1 in chunks(rows):
                    own = src[g, r0:r1, :]
                    value = acc[r0:r1, (g - g0) * lanes : (g - g0 + 1) * lanes]
                    value = value + mix(plan, coef, g * g_all, g, src, r0, r1)
                    value = value + (va[g, r0:r1, :] - center) * own + vd[g, r0:r1, :] * swap(own)
                    finish(g, r0, r1, value)

    def first(g, r0, r1, value):
        put(y, yh, yl, g, r0, r1, value * (s0 / half_width))

    apply(x, xh, xl, first)

    def second(g, r0, r1, value):
        put(out, xh, xl, g, r0, r1, value * (2.0 * s1 / half_width) - (s0 * s1) * x[g, r0:r1, :])

    apply(y, yh, yl, second)

    for j in range(plan.inner):
        g = BUF + j
        for r0, r1 in chunks(face, 64):
            e = out[g, r0:r1, :]
            t = swap(e)
            basis[j, r0:r1, :] = (0.5 * (e + t))[:, : plan.width]
            basis[c - 1 - j, r0:r1, :] = (0.5 * (e - t))[:, : plan.width]
    for r0, r1 in chunks(face, 16):
        mask = low_lanes((r1 - r0, lanes))
        e = out[BUF, r0:r1, :]
        d = mix(plan, dcoef, 0, 0, out, r0, r1)
        te, td = swap(e), swap(d)
        mxlo[r0:r1, :] = 0.5 * jnp.where(mask, e + te, d + td)
        mxhi[r0:r1, :] = 0.5 * jnp.where(mask, e - te, d - td)
    cols = slice(BUF * lanes, g_all * lanes)
    dacc[...] = dot(fh[...], xh[:, cols]) + dot(fl[...], xh[:, cols]) + dot(fh[...], xl[:, cols])
    for j in range(plan.inner):
        g = BUF + j
        own = slice(j * lanes, (j + 1) * lanes)
        to = slice(j * c, (j + 1) * c)
        mylo[0, to, :] = out[g, :c, :]
        myhi[0, to, :] = out[g, face - c : face, :]
        mzlo[0, to, :] = out[g, pl.ds(0, c, stride=c), :]
        mzhi[0, to, :] = out[g, pl.ds(c - 1, c, stride=c), :]
        for k, dst in enumerate((mylo, myhi, mzlo, mzhi)):
            dst[1, to, :] = dacc[k * c : (k + 1) * c, own]
    va_out[...] = va[BUF:, :face, :]
    vd_out[...] = vd[BUF:, :face, :]


def own_kernel(plan, f, va, vd, bh, bl, coef, diag, f2, f2h, f2l, fhi, acc):
    g_all, lanes, rows, face = plan.groups, plan.lanes, plan.rows, plan.face
    for g in range(g_all):
        top = face if g < BUF else rows
        for r0, r1 in chunks(top, 16):
            value = f[g, r0:r1, :]
            high = value.astype(BF)
            fhi[g, r0:r1, :] = high
            twice = 2.0 * value - high.astype(F32)
            f2[g, r0:r1, :] = twice
            if g >= BUF:
                h, l = split(twice)
                f2h[r0:r1, (g - BUF) * lanes : (g - BUF + 1) * lanes] = h
                f2l[r0:r1, (g - BUF) * lanes : (g - BUF + 1) * lanes] = l
    total = jnp.zeros((lanes, 2 * lanes), F32)

    def fold(total, g, top, value):
        h, l = split(value)
        return total + dot_t(fhi[g, :top, :], jnp.concatenate([h, l], axis=1))

    for g in range(BUF):
        parts = [mix(plan, coef, g * g_all, g, f2, r0, r1) for r0, r1 in chunks(face)]
        total = fold(total, g, face, jnp.concatenate(parts, axis=0))
    for j0 in range(0, plan.inner, 2):
        cols = slice(j0 * lanes, (j0 + 2) * lanes)
        acc[...] = dot(bh[...], f2h[:, cols]) + dot(bl[...], f2h[:, cols]) + dot(bh[...], f2l[:, cols])
        for j in (j0, j0 + 1):
            g = BUF + j
            mine = slice((j - j0) * lanes, (j - j0 + 1) * lanes)
            parts = []
            for r0, r1 in chunks(face):
                own = f2[g, r0:r1, :]
                value = acc[r0:r1, mine] + mix(plan, coef, g * g_all, g, f2, r0, r1)
                parts.append(value + va[j, r0:r1, :] * own + vd[j, r0:r1, :] * swap(own))
            parts.append(acc[face:, mine])
            total = fold(total, g, rows, jnp.concatenate(parts, axis=0))
    both = total[:, :lanes] + total[:, lanes:]
    w = plan.width
    block = both[:w, :w] + both[w:, w:]
    diag[...] = 0.25 * (block + jnp.transpose(block))


def face_kernel(plan, diag, oxl, oxh, oyl, oyh, ozl, ozh, nxl, nxh, nyl, nyh, nzl, nzh, blocks):
    w, lanes = plan.width, plan.lanes
    blocks[0] = diag[...]

    def product(a, b):
        ah, al = split(a)
        bh, bl = split(b)
        return dot_t(ah, bh) + dot_t(ah, bl) + dot_t(al, bh)

    for k, (own, other) in enumerate(((oxl, nxl), (oxh, nxh))):
        sign = -1.0 if k % 2 == 0 else 1.0
        m = product(own[...], other[...])
        blocks[1 + k] = 0.25 * sign * (m[w:, :w] - m[:w, w:]) - 0.5 * PENALTY * m[:w, :w]
    for k, (own, other) in enumerate(((oyl, nyl), (oyh, nyh), (ozl, nzl), (ozh, nzh))):
        sign = -1.0 if k % 2 == 0 else 1.0
        a = jnp.concatenate([own[0], own[1]], axis=1)
        b = jnp.concatenate([other[0], other[1]], axis=1)
        m = product(a, b)
        uv = m[:w, :w] + m[w:lanes, w:lanes]
        udv = m[:w, lanes : lanes + w] + m[w:lanes, lanes + w :]
        duv = m[lanes : lanes + w, :w] + m[lanes + w :, w:lanes]
        blocks[3 + k] = 0.5 * (0.25 * sign * (duv - udv) - 0.5 * PENALTY * uv)


def call(kernel, plan, outs, args, scratch=(), flops=0):
    bytes_all = sum(int(np.prod(a.shape)) * a.dtype.itemsize for a in args)
    return pl.pallas_call(
        functools.partial(kernel, plan),
        out_shape=outs,
        in_specs=[pl.BlockSpec(memory_space=pltpu.VMEM)] * len(args),
        out_specs=[pl.BlockSpec(memory_space=pltpu.VMEM)] * len(outs),
        scratch_shapes=list(scratch),
        compiler_params=pltpu.CompilerParams(vmem_limit_bytes=LIMIT),
        cost_estimate=pl.CostEstimate(flops=flops, bytes_accessed=bytes_all, transcendentals=0),
    )(*args)


def f32(*shape):
    return jax.ShapeDtypeStruct(shape, F32)


def shift(array, axis, step):
    count = lax.axis_size(axis)
    return lax.ppermute(array, axis, [(i, (i + step) % count) for i in range(count)])


def on_device(orbitals, potential):
    cells, width = orbitals.shape[0], orbitals.shape[-1]
    plan = Plan(cells, width)
    lanes, face, strip = plan.lanes, plan.face, plan.strip
    g_all = plan.groups

    spread = np.zeros((cells, face), np.float32)
    for y in range(cells):
        spread[np.arange(cells), y * cells + np.arange(cells)] = 1.0
    pick = np.zeros((cells, cells, face), np.float32)
    for y in range(cells):
        pick[:, y, y * cells : (y + 1) * cells] = 1.0
    xrows, yrows, erows = BUF * face // 2 + 8, plan.inner * strip + cells, BUF * strip + 8
    xlo, xhi, ylo, yhi, inner, vt = call(
        pack_kernel, plan,
        [f32(xrows, lanes), f32(xrows, lanes), f32(yrows, lanes), f32(yrows, lanes), f32(plan.inner, face, lanes), f32(cells, face)],
        [orbitals.reshape(cells, face, width), potential.reshape(face, cells), jnp.asarray(spread), jnp.asarray(pick.reshape(face, face))],
    )
    from_xlo, from_xhi = shift(xhi, "gx", 1), shift(xlo, "gx", -1)
    from_ylo, from_yhi = shift(yhi, "gy", 1), shift(ylo, "gy", -1)
    outer, elo, ehi = call(
        xhalo_kernel, plan, [f32(BUF, face, lanes), f32(erows, lanes), f32(erows, lanes)], [from_xlo, from_xhi],
    )
    from_elo, from_ehi = shift(ehi, "gy", 1), shift(elo, "gy", -1)

    frows = plan.plane * cells
    zpick = np.zeros((2, frows, lanes), np.float32)
    for side, start in ((0, 0), (1, cells - BUF)):
        for k in range(BUF):
            for y in range(plan.ext):
                zpick[side, y * cells + start + k, k * plan.plane + y] = 1.0
    zrows = g_all * BUF * plan.plane + plan.trows
    field, vfull, z = call(
        zpack_kernel, plan,
        [f32(g_all, frows, lanes), f32(plan.trows, frows), f32(2, zrows, lanes)],
        [inner, outer, vt, from_xlo, from_xhi, from_ylo, from_yhi, from_elo, from_ehi, jnp.asarray(zpick)],
    )
    if lax.axis_size("gz") == 2:
        other = shift(z, "gz", 1)
        zlo, zhi = other[1], other[0]
    else:
        zlo, zhi = shift(z[1], "gz", 1), shift(z[0], "gz", -1)

    wh, wl = halves(-0.5 * row_matrix(plan, plan.second, False))
    coef = (-0.5 * mirrored(plan, plan.second)).reshape(-1, lanes).astype(np.float32)
    p = plan.first[BUF, :g_all] + plan.first[BUF, ::-1][:g_all]
    q = plan.first[BUF, :g_all] - plan.first[BUF, ::-1][:g_all]
    dcoef = np.concatenate([np.repeat(p[:, None], width, 1), np.repeat(q[:, None], width, 1)], 1).astype(np.float32)
    vspread = np.zeros((plan.trows, 2, g_all, lanes), np.float32)
    for g in range(g_all):
        vspread[g, :, g, :] = 0.5
        vspread[plan.ext - 1 - g, 0, g, :] = 0.5
        vspread[plan.ext - 1 - g, 1, g, :] = -0.5
    fh, fl = halves(face_rows(plan))
    rows = plan.rows
    outs = [f32(cells, face, width), f32(g_all, rows, lanes), f32(face, lanes), f32(face, lanes)]
    outs += [f32(2, plan.inner * cells, lanes)] * 4 + [f32(plan.inner, face, lanes)] * 2
    basis, filtered, mxlo, mxhi, mylo, myhi, mzlo, mzhi, va, vd = call(
        filter_kernel, plan, outs,
        [field, zlo, zhi, vfull, jnp.asarray(wh), jnp.asarray(wl), jnp.asarray(coef), jnp.asarray(dcoef),
         jnp.asarray(vspread.reshape(plan.trows, -1)), jnp.asarray(fh), jnp.asarray(fl)],
        [pltpu.VMEM((g_all, rows, lanes), F32), pltpu.VMEM((rows, g_all * lanes), BF), pltpu.VMEM((rows, g_all * lanes), BF),
         pltpu.VMEM((g_all, rows, lanes), F32), pltpu.VMEM((rows, g_all * lanes), BF), pltpu.VMEM((rows, g_all * lanes), BF),
         pltpu.VMEM((g_all, rows, lanes), F32), pltpu.VMEM((g_all, rows, lanes), F32),
         pltpu.VMEM((rows, 2 * lanes), F32), pltpu.VMEM((4 * cells, plan.inner * lanes), F32)],
    )
    nxl, nxh = shift(mxhi, "gx", 1), shift(mxlo, "gx", -1)
    nyl, nyh = shift(myhi, "gy", 1), shift(mylo, "gy", -1)
    if lax.axis_size("gz") == 2:
        nz = shift(jnp.stack([mzlo, mzhi]), "gz", 1)
        nzl, nzh = nz[1], nz[0]
    else:
        nzl, nzh = shift(mzhi, "gz", 1), shift(mzlo, "gz", -1)

    along = energy(plan)
    bh, bl = halves(row_matrix(plan, along, True))
    bcoef = mirrored(plan, along).reshape(-1, lanes).astype(np.float32)
    (diag,) = call(
        own_kernel, plan, [f32(width, width)],
        [filtered, va, vd, jnp.asarray(bh), jnp.asarray(bl), jnp.asarray(bcoef)],
        [pltpu.VMEM((g_all, rows, lanes), F32), pltpu.VMEM((rows, plan.inner * lanes), BF), pltpu.VMEM((rows, plan.inner * lanes), BF),
         pltpu.VMEM((g_all, rows, lanes), BF), pltpu.VMEM((rows, 2 * lanes), F32)],
        flops=2 * 10**9,
    )
    (blocks,) = call(
        face_kernel, plan, [f32(7, width, width)],
        [diag, mxlo, mxhi, mylo, myhi, mzlo, mzhi, nxl, nxh, nyl, nyh, nzl, nzh],
    )
    return basis.reshape(orbitals.shape), blocks[None, None, None]


def solution(mesh):
    return jax.shard_map(
        on_device,
        mesh=mesh,
        in_specs=(P("gx", "gy", "gz", None), P("gx", "gy", "gz")),
        out_specs=(P("gx", "gy", "gz", None), P("gx", "gy", "gz", None, None, None)),
        check_vma=False,
    )
```

```python
import functools

import jax
import jax.numpy as jnp
import ml_dtypes
import numpy as np
from jax import lax
from jax.experimental import pallas as pl
from jax.experimental.pallas import tpu as pltpu
from jax.sharding import PartitionSpec as P

BUF = 3
PENALTY = 2.0
LOW_BOUND = -1.5
CUTOFF = 8.0
HIGH_BOUND = 16.0
BF = jnp.bfloat16
F32 = jnp.float32


class Plan:
    def __init__(self, cells, width):
        self.cells, self.width = cells, width
        self.ext = cells + 2 * BUF
        self.groups = self.ext // 2
        self.inner = cells // 2
        self.lanes = 2 * width
        self.face = cells * cells
        self.yext = self.ext * cells
        self.plane = -(-self.ext // 8) * 8
        self.strip = BUF * cells
        self.rows = self.yext + 2 * BUF * self.plane
        self.trows = -(-self.ext // 8) * 8
        order = list(range(BUF, BUF + cells)) + list(range(BUF)) + list(range(BUF + cells, self.ext))
        points = []
        for y in order:
            points += [(y, BUF + z) for z in range(cells)]
        for z in list(range(BUF)) + list(range(BUF + cells, self.ext)):
            points += [(y, z) for y in order] + [None] * (self.plane - self.ext)
        self.points = points
        self.first, self.second = spectral(self.ext)
        inside = np.zeros(self.ext)
        inside[BUF : BUF + cells] = 1.0
        self.inside = inside


def spectral(points):
    indices = np.arange(points)
    offsets = indices[:, None] - indices[None, :]
    first = np.zeros((points, points))
    second = np.zeros((points, points))
    for harmonic in range(1, points // 2):
        wavenum = 2.0 * np.pi * harmonic / points
        first = first - 2.0 * wavenum * np.sin(wavenum * offsets) / points
        second = second - 2.0 * wavenum * wavenum * np.cos(wavenum * offsets) / points
    second = second - np.pi * np.pi * np.cos(np.pi * offsets) / points
    return first, second


def row_matrix(plan, along, masked):
    out = np.zeros((plan.rows, plan.rows))
    for r, p in enumerate(plan.points):
        if p is None:
            continue
        for q, s in enumerate(plan.points):
            if s is None:
                continue
            if p[1] == s[1] and (not masked or plan.inside[p[1]]):
                out[r, q] += along[p[0], s[0]]
            if p[0] == s[0] and (not masked or plan.inside[p[0]]):
                out[r, q] += along[p[1], s[1]]
    return out


def mirrored(plan, along):
    n, g = plan.ext, plan.groups
    plus = along[:g, :g] + along[:g, ::-1][:, :g]
    minus = along[:g, :g] - along[:g, ::-1][:, :g]
    return np.concatenate([np.repeat(plus[:, :, None], plan.width, 2), np.repeat(minus[:, :, None], plan.width, 2)], 2)


def face_rows(plan):
    c = plan.cells
    index = {p: r for r, p in enumerate(plan.points) if p is not None}
    out = np.zeros((4 * c, plan.rows))
    for side, layer in enumerate((BUF, BUF + c - 1)):
        for z in range(c):
            for y in range(plan.ext):
                out[side * c + z, index[(y, BUF + z)]] = plan.first[layer, y]
        for y in range(c):
            for z in range(plan.ext):
                out[(2 + side) * c + y, index[(BUF + y, z)]] = plan.first[layer, z]
    return out


def energy(plan):
    c = plan.cells
    block = plan.first[BUF : BUF + c]
    out = 0.5 * block.T @ block
    for sign, layer in ((-1.0, BUF), (1.0, BUF + c - 1)):
        unit = np.zeros(plan.ext)
        unit[layer] = 1.0
        cross = np.outer(unit, plan.first[layer])
        out = out + 0.5 * PENALTY * np.outer(unit, unit) - 0.25 * sign * (cross + cross.T)
    return out


def halves(matrix):
    high = matrix.astype(np.float32).astype(ml_dtypes.bfloat16)
    low = (matrix - high.astype(np.float64)).astype(np.float32).astype(ml_dtypes.bfloat16)
    return high, low


def split(x):
    high = x.astype(BF)
    return high, (x - high.astype(F32)).astype(BF)


def swap(x):
    return pltpu.roll(x, x.shape[-1] // 2, x.ndim - 1)


def dot(a, b):
    return jnp.dot(a, b, preferred_element_type=F32)


def dot_t(a, b):
    return lax.dot_general(a, b, (((0,), (0,)), ((), ())), preferred_element_type=F32)


def exact(a, b):
    return jnp.dot(a, b, preferred_element_type=F32, precision=lax.Precision.HIGHEST)


def low_lanes(shape):
    return lax.broadcasted_iota(jnp.int32, shape, len(shape) - 1) < shape[-1] // 2


def sides(ref, paired):
    return [ref.at[0], ref.at[1]] if paired else ref


def pack_kernel(plan, orb, pot, spread, pick, xlo, xhi, ylo, yhi, inner, vt):
    c, w = plan.cells, plan.width
    half = plan.face // 2
    for s in range(BUF):
        for out, x in ((xlo, s), (xhi, c - BUF + s)):
            out[s * half : (s + 1) * half, :] = jnp.concatenate([orb[x, :half], orb[x, half:]], axis=1)
    for j in range(plan.inner):
        a, b = orb[j], orb[c - 1 - j]
        e = jnp.concatenate([a + b, a - b], axis=1)
        inner[j] = e
        ylo[j * plan.strip : (j + 1) * plan.strip, :] = e[: plan.strip]
        yhi[j * plan.strip : (j + 1) * plan.strip, :] = e[plan.face - plan.strip :]
    wide = exact(pot[...], spread[...]) * pick[...]
    v = wide.reshape(c, c, plan.face).sum(axis=1)
    vt[...] = v
    lanes = plan.lanes
    base = BUF * half
    xlo[base:, :] = jnp.zeros((8, lanes), F32)
    xhi[base:, :] = jnp.zeros((8, lanes), F32)
    for part in range(2):
        cols = slice(part * lanes, (part + 1) * lanes)
        xlo[base + part * BUF : base + (part + 1) * BUF, :] = v[:BUF, cols]
        xhi[base + part * BUF : base + (part + 1) * BUF, :] = v[c - BUF :, cols]
    ybase = plan.inner * plan.strip
    ylo[ybase:, :] = v[:, :lanes]
    yhi[ybase:, :] = v[:, plan.face - lanes :]


def xhalo_kernel(plan, lo, hi, outer, elo, ehi):
    half = plan.face // 2
    lanes = plan.lanes
    mask = low_lanes((half, lanes))
    for g in range(BUF):
        a = lo[g * half : (g + 1) * half, :]
        b = hi[(BUF - 1 - g) * half : (BUF - g) * half, :]
        s, d = a + b, a - b
        top = jnp.where(mask, s, swap(d))
        bottom = jnp.where(mask, swap(s), d)
        outer[g, :half] = top
        outer[g, half:] = bottom
        elo[g * plan.strip : (g + 1) * plan.strip, :] = top[: plan.strip]
        ehi[g * plan.strip : (g + 1) * plan.strip, :] = bottom[half - plan.strip :]
    base, ebase = BUF * half, BUF * plan.strip
    elo[ebase:, :] = jnp.zeros((8, lanes), F32)
    ehi[ebase:, :] = jnp.zeros((8, lanes), F32)
    for k, src in enumerate((lo, hi)):
        elo[ebase + k * BUF : ebase + (k + 1) * BUF, :] = src[base : base + BUF, :]
        ehi[ebase + k * BUF : ebase + (k + 1) * BUF, :] = src[base + BUF : base + 2 * BUF, :]


def zpack_kernel(plan, inner, outer, vx, vt, ylo, yhi, elo, ehi, zpick, field, vfull, z):
    c, lanes, strip, face = plan.cells, plan.lanes, plan.strip, plan.face
    for g in range(BUF):
        field[g, :face] = outer[g]
        field[g, face : face + strip] = elo[g * strip : (g + 1) * strip, :]
        field[g, face + strip : face + 2 * strip] = ehi[g * strip : (g + 1) * strip, :]
    for j in range(plan.inner):
        g = BUF + j
        field[g, :face] = inner[j]
        field[g, face : face + strip] = ylo[j * strip : (j + 1) * strip, :]
        field[g, face + strip : face + 2 * strip] = yhi[j * strip : (j + 1) * strip, :]
    pad = field.shape[1] - plan.yext
    field[:, plan.yext :] = jnp.zeros((plan.groups, pad, lanes), F32)
    plane = plan.plane
    span = BUF * plane
    for side, start in ((0, 0), (1, c - BUF)):
        for g in range(plan.groups):
            for k in range(BUF):
                at = g * span + k * plane
                z[side, at : at + plane, :] = field[g, pl.ds(start + k, plane, stride=c), :]
    ebase, ybase = BUF * strip, plan.inner * strip
    vfull[...] = jnp.zeros(vfull.shape, F32)
    vfull[: plan.ext, :face] = vx[: plan.ext, :]
    shift = lanes - strip
    vfull[:BUF, face : face + strip] = elo[ebase : ebase + BUF, :][:, shift:]
    vfull[BUF + c : plan.ext, face : face + strip] = elo[ebase + BUF : ebase + 2 * BUF, :][:, shift:]
    vfull[BUF : BUF + c, face : face + strip] = ylo[ybase:, :][:, shift:]
    vfull[:BUF, face + strip : face + 2 * strip] = ehi[ebase : ebase + BUF, :][:, :strip]
    vfull[BUF + c : plan.ext, face + strip : face + 2 * strip] = ehi[ebase + BUF : ebase + 2 * BUF, :][:, :strip]
    vfull[BUF : BUF + c, face + strip : face + 2 * strip] = yhi[ybase:, :][:, :strip]
    for side in range(2):
        z[side, plan.groups * span :, :] = exact(vfull[...], zpick[side])


CENTER = (HIGH_BOUND + CUTOFF) / 2.0
HALF_WIDTH = (HIGH_BOUND - CUTOFF) / 2.0
S0 = HALF_WIDTH / (LOW_BOUND - CENTER)
S1 = 1.0 / (2.0 / S0 - S0)


def mix(plan, coef, table, src, r0, r1):
    total = None
    for s in range(plan.groups):
        term = coef[table + s : table + s + 1, :] * src[s, r0:r1, :]
        total = term if total is None else total + term
    return total


def chunks(stop, size=16, start=0):
    return [(r, min(r + size, stop)) for r in range(start, stop, size)]


def pairs(stop, start=0):
    return [(g, min(g + 2, stop)) for g in range(start, stop, 2)]


def spread_potential(plan, piece, count, vspread, va, vd, at):
    high = piece.astype(BF).astype(F32)
    rest = piece - high
    mid = rest.astype(BF).astype(F32)
    three = jnp.concatenate([high, mid, rest - mid], axis=0)
    turned = jnp.transpose(three)[:count, :].astype(BF)
    g_all, lanes = plan.groups, plan.lanes
    for g0, g1 in pairs(g_all):
        for k, dst, less in ((0, va, CENTER), (1, vd, 0.0)):
            cols = slice((k * g_all + g0) * lanes, (k * g_all + g1) * lanes)
            both = dot(turned, vspread[:, cols]) - less
            for g in range(g0, g1):
                dst[g, at : at + count, :] = both[:, (g - g0) * lanes : (g - g0 + 1) * lanes]


def three(wh, wl, sh, sl):
    return dot(wh, sh) + dot(wl, sh) + dot(wh, sl)


def local_terms(plan, coef, g, src, r0, r1, va, vd, v0):
    own = src[g, r0:r1, :]
    value = mix(plan, coef, g * plan.groups, src, r0, r1)
    return value + va[g, v0 : v0 + r1 - r0, :] * own + vd[g, v0 : v0 + r1 - r0, :] * swap(own)


def inside_kernel(plan, inner, outer, vt, xlo, xhi, wh, wl, coef, vspread, acc, va, vd, vx, x, xh, xl):
    g_all, lanes, face, c = plan.groups, plan.lanes, plan.face, plan.cells
    base = BUF * (face // 2)
    vx[...] = jnp.zeros(vx.shape, F32)
    for part in range(2):
        cols = slice(part * lanes, (part + 1) * lanes)
        vx[:BUF, cols] = xlo[base + part * BUF : base + (part + 1) * BUF, :]
        vx[BUF + c : plan.ext, cols] = xhi[base + part * BUF : base + (part + 1) * BUF, :]
    vx[BUF : BUF + c, :] = vt[...]
    spread_potential(plan, vx[...], face, vspread, va, vd, 0)
    for g in range(g_all):
        value = outer[g] if g < BUF else inner[g - BUF]
        x[g] = value
        h, l = split(value)
        xh[:, g * lanes : (g + 1) * lanes] = h
        xl[:, g * lanes : (g + 1) * lanes] = l
    for g0, g1 in pairs(g_all):
        cols = slice(g0 * lanes, g1 * lanes)
        total = three(wh[...], wl[...], xh[:, cols], xl[:, cols])
        for g in range(g0, g1):
            acc[g] = total[:, (g - g0) * lanes : (g - g0 + 1) * lanes]
            for r0, r1 in chunks(face):
                acc[g, r0:r1, :] = acc[g, r0:r1, :] + local_terms(plan, coef, g, x, r0, r1, va, vd, r0)


def yhalo_kernel(plan, field, vfull, wh, wl, coef, vspread, given, acc, va, vd, xh, xl):
    g_all, lanes, face, yext = plan.groups, plan.lanes, plan.face, plan.yext
    count = yext - face
    spread_potential(plan, vfull[:, face:], count, vspread, va, vd, 0)
    for g in range(g_all):
        h, l = split(field[g, face:yext, :])
        xh[:, g * lanes : (g + 1) * lanes] = h
        xl[:, g * lanes : (g + 1) * lanes] = l
    for g0, g1 in pairs(g_all):
        cols = slice(g0 * lanes, g1 * lanes)
        total = three(wh[...], wl[...], xh[:, cols], xl[:, cols])
        for g in range(g0, g1):
            acc[g] = given[g] + total[:, (g - g0) * lanes : (g - g0 + 1) * lanes]
            for r0, r1 in chunks(yext, 16, face):
                acc[g, r0:r1, :] = acc[g, r0:r1, :] + local_terms(plan, coef, g, field, r0, r1, va, vd, r0 - face)


def filter_kernel(plan, paired, *refs):
    zin, refs = refs[: 1 if paired else 2], refs[1 if paired else 2 :]
    (field, vai, vdi, vay, vdy, given, zwh, zwl, wh, wl, coef, dcoef, vspread, fh, fl,
     out, mx, my, mz,
     x, xh, xl, y, yh, yl, va, vd, acc, dacc) = refs
    g_all, lanes, rows, face, yext, c = plan.groups, plan.lanes, plan.rows, plan.face, plan.yext, plan.cells
    span = BUF * plan.plane
    mz = sides(mz, paired)
    zlo, zhi = (zin[0].at[1], zin[0].at[0]) if paired else zin
    for k, piece in enumerate((zlo, zhi)):
        spread_potential(plan, piece[g_all * span :, :], span, vspread, va, vd, k * span)
        for g in range(g_all):
            value = piece[g * span : (g + 1) * span, :]
            x[g, k * span : (k + 1) * span, :] = value
            h, l = split(value)
            xh[k * span : (k + 1) * span, g * lanes : (g + 1) * lanes] = h
            xl[k * span : (k + 1) * span, g * lanes : (g + 1) * lanes] = l

    def put(dst, dh, dl, g, r0, r1, value):
        dst[g, r0:r1, :] = value
        h, l = split(value)
        dh[r0:r1, g * lanes : (g + 1) * lanes] = h
        dl[r0:r1, g * lanes : (g + 1) * lanes] = l

    for n, (g0, g1) in enumerate(pairs(g_all)):
        slot = n % 2
        cols = slice(g0 * lanes, g1 * lanes)
        acc[slot, :, : (g1 - g0) * lanes] = three(zwh[...], zwl[...], xh[:, cols], xl[:, cols])
        for g in range(g0, g1):
            mine = slice((g - g0) * lanes, (g - g0 + 1) * lanes)
            for r0, r1 in chunks(rows):
                value = given[g, r0:r1, :] + acc[slot, r0:r1, mine]
                if r0 >= yext:
                    value = value + local_terms(plan, coef, g, x, r0 - yext, r1 - yext, va, vd, r0 - yext)
                put(y, yh, yl, g, r0, r1, value * (S0 / HALF_WIDTH))

    for n, (g0, g1) in enumerate(pairs(g_all)):
        slot = n % 2
        top = face if g1 <= BUF else rows
        cols = slice(g0 * lanes, g1 * lanes)
        acc[slot, :top, : (g1 - g0) * lanes] = three(wh[:top], wl[:top], yh[:, cols], yl[:, cols])
        for g in range(g0, g1):
            mine = slice((g - g0) * lanes, (g - g0 + 1) * lanes)
            for r0, r1 in chunks(face if g < BUF else rows):
                v, d, at, start, s0 = (vai, vdi, r0, field, r0)
                if r0 >= yext:
                    v, d, at, start, s0 = (va, vd, r0 - yext, x, r0 - yext)
                elif r0 >= face:
                    v, d, at, start, s0 = (vay, vdy, r0 - face, field, r0)
                value = acc[slot, r0:r1, mine] + local_terms(plan, coef, g, y, r0, r1, v, d, at)
                value = value * (2.0 * S1 / HALF_WIDTH) - (S0 * S1) * start[g, s0 : s0 + r1 - r0, :]
                out[g, r0:r1, :] = value
                if g >= BUF:
                    h, l = split(value)
                    yh[r0:r1, g * lanes : (g + 1) * lanes] = h
                    yl[r0:r1, g * lanes : (g + 1) * lanes] = l

    for r0, r1 in chunks(face, 16):
        mask = low_lanes((r1 - r0, lanes))
        e = out[BUF, r0:r1, :]
        d = mix(plan, dcoef, 0, out, r0, r1)
        te, td = swap(e), swap(d)
        mx[0][r0:r1, :] = 0.5 * jnp.where(mask, e + te, d + td)
        mx[1][r0:r1, :] = 0.5 * jnp.where(mask, e - te, d - td)
    cols = slice(BUF * lanes, g_all * lanes)
    dacc[...] = three(fh[...], fl[...], yh[:, cols], yl[:, cols])
    part = plan.inner * c
    for j in range(plan.inner):
        g = BUF + j
        own = slice(j * lanes, (j + 1) * lanes)
        to = slice(j * c, (j + 1) * c)
        my[0][to, :] = out[g, :c, :]
        my[1][to, :] = out[g, face - c : face, :]
        mz[0][to, :] = out[g, pl.ds(0, c, stride=c), :]
        mz[1][to, :] = out[g, pl.ds(c - 1, c, stride=c), :]
        for k, dst in enumerate((my[0], my[1], mz[0], mz[1])):
            dst[part + j * c : part + (j + 1) * c, :] = dacc[k * c : (k + 1) * c, own]


def own_kernel(plan, f, va, vd, bh, bl, coef, diag, basis, f2, f2h, f2l, fhi, acc):
    g_all, lanes, rows, face, c = plan.groups, plan.lanes, plan.rows, plan.face, plan.cells
    for j in range(plan.inner):
        for r0, r1 in chunks(face, 64):
            e = f[BUF + j, r0:r1, :]
            t = swap(e)
            basis[j, r0:r1, :] = (0.5 * (e + t))[:, : plan.width]
            basis[c - 1 - j, r0:r1, :] = (0.5 * (e - t))[:, : plan.width]
    for g in range(g_all):
        top = face if g < BUF else rows
        for r0, r1 in chunks(top, 16):
            value = f[g, r0:r1, :]
            high = value.astype(BF)
            fhi[g, r0:r1, :] = high
            twice = 2.0 * value - high.astype(F32)
            f2[g, r0:r1, :] = twice
            if g >= BUF:
                h, l = split(twice)
                f2h[r0:r1, (g - BUF) * lanes : (g - BUF + 1) * lanes] = h
                f2l[r0:r1, (g - BUF) * lanes : (g - BUF + 1) * lanes] = l
    total = jnp.zeros((lanes, 2 * lanes), F32)

    def fold(total, g, top, value):
        h, l = split(value)
        return total + dot_t(fhi[g, :top, :], jnp.concatenate([h, l], axis=1))

    for g in range(BUF):
        parts = [mix(plan, coef, g * g_all, f2, r0, r1) for r0, r1 in chunks(face)]
        total = fold(total, g, face, jnp.concatenate(parts, axis=0))
    for n, (j0, j1) in enumerate(pairs(plan.inner)):
        slot = n % 2
        cols = slice(j0 * lanes, j1 * lanes)
        acc[slot] = three(bh[...], bl[...], f2h[:, cols], f2l[:, cols])
        for j in range(j0, j1):
            g = BUF + j
            mine = slice((j - j0) * lanes, (j - j0 + 1) * lanes)
            parts = []
            for r0, r1 in chunks(face):
                own = f2[g, r0:r1, :]
                value = acc[slot, r0:r1, mine] + mix(plan, coef, g * g_all, f2, r0, r1)
                parts.append(value + (va[g, r0:r1, :] + CENTER) * own + vd[g, r0:r1, :] * swap(own))
            parts.append(acc[slot, face:, mine])
            total = fold(total, g, rows, jnp.concatenate(parts, axis=0))
    both = total[:, :lanes] + total[:, lanes:]
    w = plan.width
    block = both[:w, :w] + both[w:, w:]
    diag[...] = 0.25 * (block + jnp.transpose(block))


def face_kernel(plan, paired, diag, ox, oy, oz, nx, ny, nz, blocks):
    w, lanes = plan.width, plan.lanes
    part = plan.inner * plan.cells
    oz, nz = sides(oz, paired), sides(nz, paired)[::-1] if paired else nz
    blocks[0] = diag[...]

    def product(a, b):
        ah, al = split(a)
        bh, bl = split(b)
        return dot_t(ah, bh) + dot_t(ah, bl) + dot_t(al, bh)

    for k in range(2):
        sign = -1.0 if k == 0 else 1.0
        m = product(ox[k][...], nx[k][...])
        blocks[1 + k] = 0.25 * sign * (m[w:, :w] - m[:w, w:]) - 0.5 * PENALTY * m[:w, :w]
        for at, own, other in ((3, oy, ny), (5, oz, nz)):
            a = jnp.concatenate([own[k][:part, :], own[k][part:, :]], axis=1)
            b = jnp.concatenate([other[k][:part, :], other[k][part:, :]], axis=1)
            m = product(a, b)
            uv = m[:w, :w] + m[w:lanes, w:lanes]
            udv = m[:w, lanes : lanes + w] + m[w:lanes, lanes + w :]
            duv = m[lanes : lanes + w, :w] + m[lanes + w :, w:lanes]
            blocks[at + k] = 0.5 * (0.25 * sign * (duv - udv) - 0.5 * PENALTY * uv)


def near(*shape):
    return pltpu.VMEM(shape, F32)


def far(*shape):
    return jax.ShapeDtypeStruct(shape, F32)


def call(kernel, outs, args, scratch=(), flops=0, limit=24, aliases=None, direct=()):
    def place(a):
        return pltpu.with_memory_space_constraint(jnp.asarray(a), pltpu.VMEM)

    placed = [a if i in direct else jax.tree.map(place, a) for i, a in enumerate(args)]
    space = pl.BlockSpec(memory_space=pltpu.VMEM)
    bytes_all = sum(int(np.prod(a.shape)) * a.dtype.itemsize for a in jax.tree.leaves(placed))
    return pl.pallas_call(
        kernel,
        out_shape=outs,
        in_specs=jax.tree.map(lambda a: space, placed),
        out_specs=jax.tree.map(lambda a: space, outs),
        scratch_shapes=list(scratch),
        input_output_aliases=aliases or {},
        compiler_params=pltpu.CompilerParams(vmem_limit_bytes=limit * 1024 * 1024),
        cost_estimate=pl.CostEstimate(flops=flops, bytes_accessed=bytes_all, transcendentals=0),
    )(*placed)


def shift(array, axis, step):
    count = lax.axis_size(axis)
    return lax.ppermute(array, axis, [(i, (i + step) % count) for i in range(count)])


def on_device(orbitals, potential):
    cells, width = orbitals.shape[0], orbitals.shape[-1]
    plan = Plan(cells, width)
    lanes, face, strip, rows, yext = plan.lanes, plan.face, plan.strip, plan.rows, plan.yext
    g_all, inner_all = plan.groups, plan.inner
    paired = lax.axis_size("gz") == 2
    part = functools.partial

    spread = np.zeros((cells, face), np.float32)
    pick = np.zeros((cells, cells, face), np.float32)
    for y in range(cells):
        spread[np.arange(cells), y * cells + np.arange(cells)] = 1.0
        pick[:, y, y * cells : (y + 1) * cells] = 1.0
    xrows, yrows, erows = BUF * face // 2 + 8, inner_all * strip + cells, BUF * strip + 8
    xlo, xhi, ylo, yhi, inner, vt = call(
        part(pack_kernel, plan),
        [near(xrows, lanes), near(xrows, lanes), near(yrows, lanes), near(yrows, lanes), near(inner_all, face, lanes), near(cells, face)],
        [orbitals.reshape(cells, face, width), potential.reshape(face, cells), spread, pick.reshape(face, face)],
        direct=(0, 1),
    )
    from_xlo, from_xhi = shift(xhi, "gx", 1), shift(xlo, "gx", -1)
    from_ylo, from_yhi = shift(yhi, "gy", 1), shift(ylo, "gy", -1)
    outer, elo, ehi = call(
        part(xhalo_kernel, plan), [near(BUF, face, lanes), near(erows, lanes), near(erows, lanes)], [from_xlo, from_xhi],
    )
    from_elo, from_ehi = shift(ehi, "gy", 1), shift(elo, "gy", -1)

    matrix = -0.5 * row_matrix(plan, plan.second, False)
    coef = (-0.5 * mirrored(plan, plan.second)).reshape(-1, lanes).astype(np.float32)
    vspread = np.zeros((plan.trows, 2, g_all, lanes), np.float32)
    for g in range(g_all):
        vspread[g, :, g, :] = 0.5
        vspread[plan.ext - 1 - g, 0, g, :] = 0.5
        vspread[plan.ext - 1 - g, 1, g, :] = -0.5
    vspread = np.tile(vspread.reshape(plan.trows, -1), (3, 1)).astype(ml_dtypes.bfloat16)
    bf = lambda *shape: pltpu.VMEM(shape, BF)
    acc, vai, vdi, vx = call(
        part(inside_kernel, plan),
        [near(g_all, rows, lanes), near(g_all, face, lanes), near(g_all, face, lanes), near(plan.trows, face)],
        [inner, outer, vt, from_xlo, from_xhi, *halves(matrix[:, :face]), coef, vspread],
        [near(g_all, face, lanes), bf(face, g_all * lanes), bf(face, g_all * lanes)],
        flops=10**9,
    )

    frows = plan.plane * cells
    zpick = np.zeros((2, frows, lanes), np.float32)
    for side, start in ((0, 0), (1, cells - BUF)):
        for k in range(BUF):
            for y in range(plan.ext):
                zpick[side, y * cells + start + k, k * plan.plane + y] = 1.0
    span = BUF * plan.plane
    zrows = g_all * span + plan.trows
    field, vfull, z = call(
        part(zpack_kernel, plan),
        [near(g_all, frows, lanes), near(plan.trows, frows), near(2, zrows, lanes)],
        [inner, outer, vx, vt, from_ylo, from_yhi, from_elo, from_ehi, zpick],
    )
    if paired:
        zin = [shift(z, "gz", 1)]
    else:
        zin = [shift(z[1], "gz", 1), shift(z[0], "gz", -1)]
    ycount = yext - face
    acc, vay, vdy = call(
        part(yhalo_kernel, plan),
        [near(g_all, rows, lanes), near(g_all, ycount, lanes), near(g_all, ycount, lanes)],
        [field, vfull, *halves(matrix[:, face:yext]), coef, vspread, acc],
        [bf(ycount, g_all * lanes), bf(ycount, g_all * lanes)],
        flops=10**9,
        aliases={6: 0},
    )

    p = plan.first[BUF, :g_all] + plan.first[BUF, ::-1][:g_all]
    q = plan.first[BUF, :g_all] - plan.first[BUF, ::-1][:g_all]
    dcoef = np.concatenate([np.repeat(p[:, None], width, 1), np.repeat(q[:, None], width, 1)], 1).astype(np.float32)
    msg = near(face, lanes)
    filtered, mx, my, mz = call(
        part(filter_kernel, plan, paired),
        [near(g_all, rows, lanes), [msg, msg], [msg, msg], near(2, face, lanes) if paired else [msg, msg]],
        [*zin, field, vai, vdi, vay, vdy, acc, *halves(matrix[:, yext:]), *halves(matrix), coef, dcoef, vspread, *halves(face_rows(plan))],
        [near(g_all, 2 * span, lanes), bf(2 * span, g_all * lanes), bf(2 * span, g_all * lanes),
         near(g_all, rows, lanes), bf(rows, g_all * lanes), bf(rows, g_all * lanes),
         near(g_all, 2 * span, lanes), near(g_all, 2 * span, lanes),
         near(2, rows, 2 * lanes), near(4 * cells, inner_all * lanes)],
    )
    ny = [shift(my[1], "gy", 1), shift(my[0], "gy", -1)]
    nx = [shift(mx[1], "gx", 1), shift(mx[0], "gx", -1)]
    if paired:
        nz = shift(mz, "gz", 1)
    else:
        nz = [shift(mz[1], "gz", 1), shift(mz[0], "gz", -1)]

    along = energy(plan)
    bcoef = mirrored(plan, along).reshape(-1, lanes).astype(np.float32)
    diag, basis = call(
        part(own_kernel, plan), [near(width, width), far(cells, face, width)],
        [filtered, vai, vdi, *halves(row_matrix(plan, along, True)), bcoef],
        [near(g_all, rows, lanes), bf(rows, inner_all * lanes), bf(rows, inner_all * lanes), bf(g_all, rows, lanes), near(2, rows, 2 * lanes)],
        flops=2 * 10**9,
    )
    blocks = call(
        part(face_kernel, plan, paired), far(7, width, width), [diag, mx, my, mz, nx, ny, nz],
    )
    return basis.reshape(orbitals.shape), blocks[None, None, None]


def solution(mesh):
    return jax.shard_map(
        on_device,
        mesh=mesh,
        in_specs=(P("gx", "gy", "gz", None), P("gx", "gy", "gz")),
        out_specs=(P("gx", "gy", "gz", None), P("gx", "gy", "gz", None, None, None)),
        check_vma=False,
    )
```

```python
import functools

import jax
import jax.numpy as jnp
import ml_dtypes
import numpy as np
from jax import lax
from jax.experimental import pallas as pl
from jax.experimental.pallas import tpu as pltpu
from jax.sharding import PartitionSpec as P

BUF = 3
PENALTY = 2.0
LOW_BOUND = -1.5
CUTOFF = 8.0
HIGH_BOUND = 16.0
BF = jnp.bfloat16
F32 = jnp.float32


class Plan:
    def __init__(self, cells, width):
        self.cells, self.width = cells, width
        self.ext = cells + 2 * BUF
        self.groups = self.ext // 2
        self.inner = cells // 2
        self.lanes = 2 * width
        self.face = cells * cells
        self.strip = BUF * cells
        self.corner = -(-2 * BUF // 8) * 8
        self.yext = self.face + 2 * self.strip
        self.cross = self.yext + 2 * self.strip
        self.rows = self.cross + 2 * BUF * self.corner
        self.trows = -(-self.ext // 8) * 8
        inside = list(range(BUF, BUF + cells))
        outside = list(range(BUF)) + list(range(BUF + cells, self.ext))
        points = [(y, z) for y in inside for z in inside] + [(y, z) for y in outside for z in inside]
        points += [(y, z) for z in outside for y in inside]
        for z in outside:
            points += [(y, z) for y in outside] + [None] * (self.corner - 2 * BUF)
        self.points = points
        self.first, self.second = spectral(self.ext)
        self.inside = np.isin(np.arange(self.ext), inside)


def spectral(points):
    indices = np.arange(points)
    offsets = indices[:, None] - indices[None, :]
    first = np.zeros((points, points))
    second = np.zeros((points, points))
    for harmonic in range(1, points // 2):
        wavenum = 2.0 * np.pi * harmonic / points
        first = first - 2.0 * wavenum * np.sin(wavenum * offsets) / points
        second = second - 2.0 * wavenum * wavenum * np.cos(wavenum * offsets) / points
    second = second - np.pi * np.pi * np.cos(np.pi * offsets) / points
    return first, second


def row_matrix(plan, along, masked):
    real = np.array([p is not None for p in plan.points])
    y, z = np.array([(0, 0) if p is None else p for p in plan.points]).T
    by_y = along[y[:, None], y[None, :]] * (z[:, None] == z[None, :])
    by_z = along[z[:, None], z[None, :]] * (y[:, None] == y[None, :])
    if masked:
        by_y, by_z = by_y * plan.inside[z][:, None], by_z * plan.inside[y][:, None]
    return (by_y + by_z) * real[:, None] * real[None, :]


def mirrored(plan, along):
    g = plan.groups
    plus = along[:g, :g] + along[:g, ::-1][:, :g]
    minus = along[:g, :g] - along[:g, ::-1][:, :g]
    return np.concatenate([np.repeat(plus[:, :, None], plan.width, 2), np.repeat(minus[:, :, None], plan.width, 2)], 2)


def folded(table):
    g = table.shape[0]
    half, odd = g // 2, g % 2
    out = []
    for t in range(half + odd):
        out += [0.5 * (table[t, s] + table[t, g - 1 - s]) for s in range(half)] + [table[t, half]] * odd
        if t < half:
            out += [0.5 * (table[t, s] - table[t, g - 1 - s]) for s in range(half)]
    return np.stack(out).astype(np.float32)


def energy(plan):
    c = plan.cells
    block = plan.first[BUF : BUF + c]
    out = 0.5 * block.T @ block
    for sign, layer in ((-1.0, BUF), (1.0, BUF + c - 1)):
        unit = np.zeros(plan.ext)
        unit[layer] = 1.0
        cross = np.outer(unit, plan.first[layer])
        out = out + 0.5 * PENALTY * np.outer(unit, unit) - 0.25 * sign * (cross + cross.T)
    return out


def halves(matrix):
    high = matrix.astype(np.float32).astype(ml_dtypes.bfloat16)
    low = (matrix - high.astype(np.float64)).astype(np.float32).astype(ml_dtypes.bfloat16)
    return high, low


def split(x):
    high = x.astype(BF)
    return high, (x - high.astype(F32)).astype(BF)


def swap(x):
    return pltpu.roll(x, x.shape[-1] // 2, x.ndim - 1)


def dot(a, b):
    return jnp.dot(a, b, preferred_element_type=F32)


def dot_t(a, b):
    return lax.dot_general(a, b, (((0,), (0,)), ((), ())), preferred_element_type=F32)


def exact(a, b):
    return jnp.dot(a, b, preferred_element_type=F32, precision=lax.Precision.HIGHEST)


def three(wh, wl, sh, sl):
    return dot(wh, sh) + dot(wl, sh) + dot(wh, sl)


def low_lanes(shape):
    return lax.broadcasted_iota(jnp.int32, shape, len(shape) - 1) < shape[-1] // 2


def sides(ref, paired):
    return [ref.at[0], ref.at[1]] if paired else ref


def chunks(stop, size=16, start=0):
    return [(r, min(r + size, stop)) for r in range(start, stop, size)]


def pairs(stop, start=0):
    return [(g, min(g + 2, stop)) for g in range(start, stop, 2)]


CENTER = (HIGH_BOUND + CUTOFF) / 2.0
HALF_WIDTH = (HIGH_BOUND - CUTOFF) / 2.0
S0 = HALF_WIDTH / (LOW_BOUND - CENTER)
S1 = 1.0 / (2.0 / S0 - S0)


def mix(coef, table, items):
    total = None
    for s, item in enumerate(items):
        term = coef[table + s : table + s + 1, :] * item
        total = term if total is None else total + term
    return total


def fold_mix(coef, items):
    g = len(items)
    half, odd = g // 2, g % 2
    plus = [items[s] + items[g - 1 - s] for s in range(half)] + [items[half]] * odd
    minus = [items[s] - items[g - 1 - s] for s in range(half)]
    out, k = [None] * g, 0
    for t in range(half + odd):
        p = mix(coef, k, plus)
        k += len(plus)
        if t < half:
            q = mix(coef, k, minus)
            k += half
            out[t], out[g - 1 - t] = p + q, p - q
        else:
            out[t] = p
    return out


def spread_potential(plan, piece, count, vspread, va, vd, at):
    high = piece.astype(BF).astype(F32)
    rest = piece - high
    mid = rest.astype(BF).astype(F32)
    stacked = jnp.concatenate([high, mid, rest - mid], axis=0)
    turned = jnp.transpose(stacked)[:count, :].astype(BF)
    g_all, lanes = plan.groups, plan.lanes
    for g0, g1 in pairs(g_all):
        for k, dst, less in ((0, va, CENTER), (1, vd, 0.0)):
            cols = slice((k * g_all + g0) * lanes, (k * g_all + g1) * lanes)
            both = dot(turned, vspread[:, cols]) - less
            for g in range(g0, g1):
                dst[g, at : at + count, :] = both[:, (g - g0) * lanes : (g - g0 + 1) * lanes]


def local_terms(coef, get, count, va, vd, v0):
    items = [get(g) for g in range(va.shape[0])]
    out = fold_mix(coef, items)
    for g, own in enumerate(items):
        out[g] = out[g] + va[g, v0 : v0 + count, :] * own + vd[g, v0 : v0 + count, :] * swap(own)
    return out


def pack_kernel(plan, orb_far, pot_far, xlo, xhi, ylo, yhi, inner, vt, orb, pot, sem):
    c, lanes = plan.cells, plan.lanes
    half = plan.face // 2
    copies = [pltpu.make_async_copy(pot_far, pot, sem.at[c])]
    copies += [pltpu.make_async_copy(orb_far.at[x], orb.at[x], sem.at[x]) for x in range(c)]
    for copy in copies:
        copy.start()
    copies[0].wait()
    lane = lax.broadcasted_iota(jnp.int32, (c, plan.face), 1)
    spread = (lax.rem(lane, c) == lax.broadcasted_iota(jnp.int32, (c, plan.face), 0)).astype(F32)
    shape = (plan.face, plan.face)
    own = lax.div(lax.broadcasted_iota(jnp.int32, shape, 1), c) == lax.rem(lax.broadcasted_iota(jnp.int32, shape, 0), c)
    wide = jnp.where(own, exact(pot[...], spread), 0.0)
    v = wide.reshape(c, c, plan.face).sum(axis=1)
    vt[...] = v
    base = BUF * half
    xlo[base:, :] = jnp.zeros((8, lanes), F32)
    xhi[base:, :] = jnp.zeros((8, lanes), F32)
    for part in range(2):
        cols = slice(part * lanes, (part + 1) * lanes)
        xlo[base + part * BUF : base + (part + 1) * BUF, :] = v[:BUF, cols]
        xhi[base + part * BUF : base + (part + 1) * BUF, :] = v[c - BUF :, cols]
    ybase = plan.inner * plan.strip
    ylo[ybase:, :] = v[:, :lanes]
    yhi[ybase:, :] = v[:, plan.face - lanes :]
    for copy in copies[1:]:
        copy.wait()
    for s in range(BUF):
        for out, x in ((xlo, s), (xhi, c - BUF + s)):
            out[s * half : (s + 1) * half, :] = jnp.concatenate([orb[x, :half], orb[x, half:]], axis=1)
    for j in range(plan.inner):
        a, b = orb[j], orb[c - 1 - j]
        e = jnp.concatenate([a + b, a - b], axis=1)
        inner[j] = e
        ylo[j * plan.strip : (j + 1) * plan.strip, :] = e[: plan.strip]
        yhi[j * plan.strip : (j + 1) * plan.strip, :] = e[plan.face - plan.strip :]


def xhalo_kernel(plan, paired, inner, vt, lo, hi, zpick, outer, elo, ehi, vx, zi):
    half, c, face, strip = plan.face // 2, plan.cells, plan.face, plan.strip
    lanes = plan.lanes
    mask = low_lanes((half, lanes))
    for g in range(BUF):
        a = lo[g * half : (g + 1) * half, :]
        b = hi[(BUF - 1 - g) * half : (BUF - g) * half, :]
        s, d = a + b, a - b
        top = jnp.where(mask, s, swap(d))
        bottom = jnp.where(mask, swap(s), d)
        outer[g, :half] = top
        outer[g, half:] = bottom
        elo[g * strip : (g + 1) * strip, :] = top[:strip]
        ehi[g * strip : (g + 1) * strip, :] = bottom[half - strip :]
    base, ebase = BUF * half, BUF * strip
    vx[...] = jnp.zeros(vx.shape, F32)
    vx[BUF : BUF + c, :] = vt[...]
    elo[ebase:, :] = jnp.zeros((8, lanes), F32)
    ehi[ebase:, :] = jnp.zeros((8, lanes), F32)
    for k, src in enumerate((lo, hi)):
        elo[ebase + k * BUF : ebase + (k + 1) * BUF, :] = src[base : base + BUF, :]
        ehi[ebase + k * BUF : ebase + (k + 1) * BUF, :] = src[base + BUF : base + 2 * BUF, :]
        at = 0 if k == 0 else BUF + c
        vx[at : at + BUF, :lanes] = src[base : base + BUF, :]
        vx[at : at + BUF, lanes:] = src[base + BUF : base + 2 * BUF, :]
    for side, dst in enumerate(sides(zi, paired)):
        start = side * (c - BUF)
        for g in range(plan.groups):
            src = outer.at[g] if g < BUF else inner.at[g - BUF]
            for k in range(BUF):
                at = g * strip + k * c
                dst[at : at + c, :] = src[pl.ds(start + k, c, stride=c), :]
        dst[plan.groups * strip :, :] = exact(vx[...], zpick[side])


def inside_kernel(plan, inner, outer, vx, wh, wl, coef, vspread, acc, va, vd, order, xh, xl):
    g_all, lanes, face = plan.groups, plan.lanes, plan.face
    spread_potential(plan, vx[...], face, vspread, va, vd, 0)
    order[...] = jnp.zeros(order.shape, F32)

    def get(g, r0, r1):
        return outer[g, r0:r1, :] if g < BUF else inner[g - BUF, r0:r1, :]

    for g in range(g_all):
        h, l = split(get(g, 0, face))
        xh[:, g * lanes : (g + 1) * lanes] = h
        xl[:, g * lanes : (g + 1) * lanes] = l
    for g0, g1 in pairs(g_all):
        cols = slice(g0 * lanes, g1 * lanes)
        total = three(wh[...], wl[...], xh[:, cols], xl[:, cols])
        for g in range(g0, g1):
            acc[g] = total[:, (g - g0) * lanes : (g - g0 + 1) * lanes]
    for r0, r1 in chunks(face):
        local = local_terms(coef, lambda g: get(g, r0, r1), r1 - r0, va, vd, r0)
        for g in range(g_all):
            acc[g, r0:r1, :] = acc[g, r0:r1, :] + local[g]


def ypack_kernel(plan, paired, ylo, yhi, elo, ehi, zpick, order, yh, vy, zc):
    c, lanes, strip, corner = plan.cells, plan.lanes, plan.strip, plan.corner
    for g in range(plan.groups):
        lo, hi, at = (elo, ehi, g * strip) if g < BUF else (ylo, yhi, (g - BUF) * strip)
        yh[g, :strip] = lo[at : at + strip, :]
        yh[g, strip : 2 * strip] = hi[at : at + strip, :]
    yh[:, 2 * strip :] = jnp.zeros((plan.groups, yh.shape[1] - 2 * strip, lanes), F32)
    ebase, ybase = BUF * strip, plan.inner * strip
    shift_in = lanes - strip
    vy[...] = jnp.zeros(vy.shape, F32)
    for e, y, cut, at in ((elo, ylo, shift_in, 0), (ehi, yhi, 0, strip)):
        cols = slice(at, at + strip)
        vy[:BUF, cols] = e[ebase : ebase + BUF, :][:, cut : cut + strip]
        vy[BUF + c : plan.ext, cols] = e[ebase + BUF : ebase + 2 * BUF, :][:, cut : cut + strip]
        vy[BUF : BUF + c, cols] = y[ybase:, :][:, cut : cut + strip]
    for side, dst in enumerate(sides(zc, paired)):
        start = side * (c - BUF)
        for g in range(plan.groups):
            for k in range(BUF):
                at = (g * BUF + k) * corner
                dst[at : at + corner, :] = yh[g, pl.ds(start + k, corner, stride=c), :]
        dst[plan.groups * BUF * corner :, :] = exact(vy[...], zpick[side])


def halo_kernel(plan, paired, yh, vy, zi, coef, vspread, given, acc, xr, va, vd, xh, xl):
    g_all, lanes, strip, face = plan.groups, plan.lanes, plan.strip, plan.face
    zlo, zhi = sides(zi, paired)[::-1] if paired else zi
    spread_potential(plan, vy[...], 2 * strip, vspread, va, vd, 0)
    for k, piece in enumerate((zlo, zhi)):
        at = (2 + k) * strip
        spread_potential(plan, piece[g_all * strip :, :], strip, vspread, va, vd, at)
        for g in range(g_all):
            xr[g, at : at + strip, :] = piece[g * strip : (g + 1) * strip, :]
    for g in range(g_all):
        xr[g, : 2 * strip, :] = yh[g, : 2 * strip, :]
        h, l = split(xr[g])
        xh[:, g * lanes : (g + 1) * lanes] = h
        xl[:, g * lanes : (g + 1) * lanes] = l
    for r0, r1 in chunks(4 * strip):
        local = local_terms(coef, lambda g: xr[g, r0:r1, :], r1 - r0, va, vd, r0)
        for g in range(g_all):
            acc[g, face + r0 : face + r1, :] = given[g, face + r0 : face + r1, :] + local[g]


def filter_kernel(plan, paired, zc, inner, outer, xr, xrh, xrl, vai, vdi, vah, vdh, given, wrh, wrl, wh, wl, coef, dcoef,
                  vspread, out, mx, my, mz, xh, xl, xc, y, yh, yl, va, vd, acc):
    g_all, lanes, rows, face, cross, c = plan.groups, plan.lanes, plan.rows, plan.face, plan.cross, plan.cells
    strip = plan.strip
    span = BUF * plan.corner
    mz = sides(mz, paired)
    zlo, zhi = sides(zc, paired)[::-1] if paired else zc
    rest = 4 * strip
    xh[:rest, :] = xrh[...]
    xl[:rest, :] = xrl[...]
    for k, piece in enumerate((zlo, zhi)):
        spread_potential(plan, piece[g_all * span :, :], span, vspread, va, vd, k * span)
        for g in range(g_all):
            xc[g, k * span : (k + 1) * span, :] = piece[g * span : (g + 1) * span, :]
    for g in range(g_all):
        h, l = split(xc[g])
        xh[rest:, g * lanes : (g + 1) * lanes] = h
        xl[rest:, g * lanes : (g + 1) * lanes] = l

    def put(g, r0, r1, value):
        y[g, r0:r1, :] = value
        h, l = split(value)
        yh[r0:r1, g * lanes : (g + 1) * lanes] = h
        yl[r0:r1, g * lanes : (g + 1) * lanes] = l

    corners = {}
    for r0, r1 in chunks(2 * span):
        corners[r0] = local_terms(coef, lambda g: xc[g, r0:r1, :], r1 - r0, va, vd, r0)
        for g in range(g_all):
            y[g, cross + r0 : cross + r1, :] = corners[r0][g]
    for n, (g0, g1) in enumerate(pairs(g_all)):
        slot = n % 2
        cols = slice(g0 * lanes, g1 * lanes)
        acc[slot, :, : (g1 - g0) * lanes] = three(wrh[...], wrl[...], xh[:, cols], xl[:, cols])
        for g in range(g0, g1):
            mine = slice((g - g0) * lanes, (g - g0 + 1) * lanes)
            for r0, r1 in chunks(rows):
                value = given[g, r0:r1, :] + acc[slot, r0:r1, mine]
                if r0 >= cross:
                    value = value + y[g, r0:r1, :]
                put(g, r0, r1, value * (S0 / HALF_WIDTH))

    for r0, r1 in chunks(cross):
        v, d, at = (vai, vdi, r0) if r0 < face else (vah, vdh, r0 - face)
        local = local_terms(coef, lambda g: y[g, r0:r1, :], r1 - r0, v, d, at)
        for g in range(g_all):
            if g >= BUF or r0 < face:
                if r0 >= face:
                    x = xr[g, r0 - face : r1 - face, :]
                else:
                    x = outer[g, r0:r1, :] if g < BUF else inner[g - BUF, r0:r1, :]
                out[g, r0:r1, :] = local[g] * (2.0 * S1 / HALF_WIDTH) - (S0 * S1) * x
    for n, (g0, g1) in enumerate(pairs(g_all)):
        slot = n % 2
        top = face if g1 <= BUF else cross
        cols = slice(g0 * lanes, g1 * lanes)
        acc[slot, :top, : (g1 - g0) * lanes] = three(wh[:top], wl[:top], yh[:, cols], yl[:, cols])
        for g in range(g0, g1):
            mine = slice((g - g0) * lanes, (g - g0 + 1) * lanes)
            for r0, r1 in chunks(face if g < BUF else cross):
                out[g, r0:r1, :] = out[g, r0:r1, :] + acc[slot, r0:r1, mine] * (2.0 * S1 / HALF_WIDTH)

    for r0, r1 in chunks(face):
        mask = low_lanes((r1 - r0, lanes))
        e = out[BUF, r0:r1, :]
        d = mix(dcoef, 0, [out[g, r0:r1, :] for g in range(g_all)])
        te, td = swap(e), swap(d)
        mx[0][r0:r1, :] = 0.5 * jnp.where(mask, e + te, d + td)
        mx[1][r0:r1, :] = 0.5 * jnp.where(mask, e - te, d - td)
    part = plan.inner * c
    order = list(range(BUF, BUF + c)) + list(range(BUF)) + list(range(BUF + c, plan.ext))
    for j in range(plan.inner):
        g = BUF + j
        to = slice(j * c, (j + 1) * c)
        down = slice(part + j * c, part + (j + 1) * c)
        ylayers = [out[g, k * c : (k + 1) * c, :] for k in range(plan.ext)]
        zlayers = [out[g, pl.ds(k, c, stride=c), :] for k in range(c)]
        zlayers += [out[g, plan.yext + k * c : plan.yext + (k + 1) * c, :] for k in range(2 * BUF)]
        for layers, message in ((ylayers, my), (zlayers, mz)):
            for side, layer in enumerate((0, c - 1)):
                message[side][to, :] = layers[layer]
                total = None
                for k, t in enumerate(order):
                    weight = float(plan.first[BUF + layer, t])
                    if t != BUF + layer:
                        term = weight * layers[k]
                        total = term if total is None else total + term
                message[side][down, :] = total


def own_kernel(plan, f, va, vd, bh, bl, coef, diag, basis, local, f2, f2h, f2l, fhi, acc, sem):
    g_all, lanes, face, cross, c = plan.groups, plan.lanes, plan.face, plan.cross, plan.cells
    copies = []
    for j in range(plan.inner):
        for r0, r1 in chunks(face, 64):
            e = f[BUF + j, r0:r1, :]
            t = swap(e)
            local[j, r0:r1, :] = (0.5 * (e + t))[:, : plan.width]
            local[c - 1 - j, r0:r1, :] = (0.5 * (e - t))[:, : plan.width]
        for x in (j, c - 1 - j):
            copies.append(pltpu.make_async_copy(local.at[x], basis.at[x], sem.at[x]))
            copies[-1].start()
    for g in range(g_all):
        top = face if g < BUF else cross
        for r0, r1 in chunks(top):
            value = f[g, r0:r1, :]
            high = value.astype(BF)
            fhi[g, r0:r1, :] = high
            twice = 2.0 * value - high.astype(F32)
            f2[g, r0:r1, :] = twice
            if g >= BUF:
                h, l = split(twice)
                f2h[r0:r1, (g - BUF) * lanes : (g - BUF + 1) * lanes] = h
                f2l[r0:r1, (g - BUF) * lanes : (g - BUF + 1) * lanes] = l
    total = jnp.zeros((lanes, 2 * lanes), F32)

    def fold(total, g, top, value):
        h, l = split(value)
        return total + dot_t(fhi[g, :top, :], jnp.concatenate([h, l], axis=1))

    def mixed(g, r0, r1):
        return mix(coef, g * g_all, [f2[s, r0:r1, :] for s in range(g_all)])

    for g in range(BUF):
        total = fold(total, g, face, jnp.concatenate([mixed(g, r0, r1) for r0, r1 in chunks(face)], axis=0))
    for n, (j0, j1) in enumerate(pairs(plan.inner)):
        slot = n % 2
        cols = slice(j0 * lanes, j1 * lanes)
        acc[slot] = three(bh[...], bl[...], f2h[:, cols], f2l[:, cols])
        for j in range(j0, j1):
            g = BUF + j
            mine = slice((j - j0) * lanes, (j - j0 + 1) * lanes)
            parts = []
            for r0, r1 in chunks(face):
                own = f2[g, r0:r1, :]
                value = acc[slot, r0:r1, mine] + mixed(g, r0, r1)
                parts.append(value + (va[g, r0:r1, :] + CENTER) * own + vd[g, r0:r1, :] * swap(own))
            parts.append(acc[slot, face:, mine])
            total = fold(total, g, cross, jnp.concatenate(parts, axis=0))
    both = total[:, :lanes] + total[:, lanes:]
    w = plan.width
    block = both[:w, :w] + both[w:, w:]
    diag[...] = 0.25 * (block + jnp.transpose(block))
    for copy in copies:
        copy.wait()


def face_kernel(plan, paired, diag, ox, oy, oz, nx, ny, nz, blocks):
    w, lanes = plan.width, plan.lanes
    part = plan.inner * plan.cells
    oz, nz = sides(oz, paired), sides(nz, paired)[::-1] if paired else nz
    blocks[0] = diag[...]

    def product(a, b):
        ah, al = split(a)
        bh, bl = split(b)
        return dot_t(ah, bh) + dot_t(ah, bl) + dot_t(al, bh)

    for k in range(2):
        sign = -1.0 if k == 0 else 1.0
        m = product(ox[k][...], nx[k][...])
        blocks[1 + k] = 0.25 * sign * (m[w:, :w] - m[:w, w:]) - 0.5 * PENALTY * m[:w, :w]
        for at, own, other in ((3, oy, ny), (5, oz, nz)):
            a = jnp.concatenate([own[k][:part, :], own[k][part:, :]], axis=1)
            b = jnp.concatenate([other[k][:part, :], other[k][part:, :]], axis=1)
            m = product(a, b)
            uv = m[:w, :w] + m[w:lanes, w:lanes]
            udv = m[:w, lanes : lanes + w] + m[w:lanes, lanes + w :]
            duv = m[lanes : lanes + w, :w] + m[lanes + w :, w:lanes]
            blocks[at + k] = 0.5 * (0.25 * sign * (duv - udv) - 0.5 * PENALTY * uv)


def near(*shape):
    return pltpu.VMEM(shape, F32)


def far(*shape):
    return jax.ShapeDtypeStruct(shape, F32)


def call(kernel, outs, args, scratch=(), flops=0, limit=24, aliases=None, far_in=(), far_out=()):
    def place(a, where):
        return pltpu.with_memory_space_constraint(jnp.asarray(a), where)

    placed = [jax.tree.map(lambda b: place(b, pltpu.HBM if i in far_in else pltpu.VMEM), a) for i, a in enumerate(args)]
    space, apart = pl.BlockSpec(memory_space=pltpu.VMEM), pl.BlockSpec(memory_space=pl.ANY)
    return pl.pallas_call(
        kernel,
        out_shape=outs,
        in_specs=[apart if i in far_in else jax.tree.map(lambda b: space, a) for i, a in enumerate(placed)],
        out_specs=[apart if i in far_out else jax.tree.map(lambda b: space, a) for i, a in enumerate(outs)],
        scratch_shapes=list(scratch),
        input_output_aliases=aliases or {},
        compiler_params=pltpu.CompilerParams(vmem_limit_bytes=limit * 1024 * 1024),
        cost_estimate=pl.CostEstimate(flops=flops, bytes_accessed=0, transcendentals=0),
    )(*placed)


def shift(array, axis, step):
    count = lax.axis_size(axis)
    return lax.ppermute(array, axis, [(i, (i + step) % count) for i in range(count)])


def shift_z(both, paired):
    if paired:
        return shift(both, "gz", 1)
    return [shift(both[1], "gz", 1), shift(both[0], "gz", -1)]


def on_device(orbitals, potential):
    cells, width = orbitals.shape[0], orbitals.shape[-1]
    plan = Plan(cells, width)
    lanes, face, strip, rows, cross = plan.lanes, plan.face, plan.strip, plan.rows, plan.cross
    g_all, inner_all, corner = plan.groups, plan.inner, plan.corner
    paired = lax.axis_size("gz") == 2
    part = functools.partial
    bf = lambda *shape: pltpu.VMEM(shape, BF)
    wide = g_all * lanes

    def two(*shape):
        return near(2, *shape) if paired else [near(*shape), near(*shape)]

    xrows, yrows, erows = BUF * face // 2 + 8, inner_all * strip + cells, BUF * strip + 8
    xlo, xhi, ylo, yhi, inner, vt = call(
        part(pack_kernel, plan),
        [near(xrows, lanes), near(xrows, lanes), near(yrows, lanes), near(yrows, lanes), near(inner_all, face, lanes), near(cells, face)],
        [orbitals.reshape(cells, face, width), potential.reshape(face, cells)],
        [pltpu.VMEM((cells, face, width), F32), pltpu.VMEM((face, cells), F32), pltpu.SemaphoreType.DMA((cells + 1,))],
        far_in=(0, 1),
    )
    from_ylo, from_yhi = shift(yhi, "gy", 1), shift(ylo, "gy", -1)
    from_xlo, from_xhi = shift(xhi, "gx", 1), shift(xlo, "gx", -1)

    ipick = np.zeros((2, face, lanes), np.float32)
    cpick = np.zeros((2, lanes, lanes), np.float32)
    for side in range(2):
        for k in range(BUF):
            z = side * (cells - BUF) + k
            for y in range(cells):
                ipick[side, y * cells + z, k * cells + y] = 1.0
            for y in range(2 * BUF):
                cpick[side, y * cells + z, k * corner + y] = 1.0
    outer, elo, ehi, vx, zi = call(
        part(xhalo_kernel, plan, paired),
        [near(BUF, face, lanes), near(erows, lanes), near(erows, lanes), near(plan.trows, face), two(g_all * strip + plan.trows, lanes)],
        [inner, vt, from_xlo, from_xhi, ipick],
    )
    from_elo, from_ehi = shift(ehi, "gy", 1), shift(elo, "gy", -1)
    zi = shift_z(zi, paired)

    matrix = -0.5 * row_matrix(plan, plan.second, False)
    coef = folded(-0.5 * mirrored(plan, plan.second))
    vspread = np.zeros((plan.trows, 2, g_all, lanes), np.float32)
    for g in range(g_all):
        vspread[g, :, g, :] = 0.5
        vspread[plan.ext - 1 - g, 0, g, :] = 0.5
        vspread[plan.ext - 1 - g, 1, g, :] = -0.5
    vspread = np.tile(vspread.reshape(plan.trows, -1), (3, 1)).astype(ml_dtypes.bfloat16)
    acc, vai, vdi, order = call(
        part(inside_kernel, plan),
        [near(g_all, rows, lanes), near(g_all, face, lanes), near(g_all, face, lanes), near(8, lanes)],
        [inner, outer, vx, *halves(matrix[:, :face]), coef, vspread],
        [bf(face, wide), bf(face, wide)],
    )

    room = 2 * strip + (corner - 2 * BUF) * cells
    yh, vy, zc = call(
        part(ypack_kernel, plan, paired),
        [near(g_all, room, lanes), near(plan.trows, lanes), two(g_all * BUF * corner + plan.trows, lanes)],
        [from_ylo, from_yhi, from_elo, from_ehi, cpick, order],
        flops=10**10,
    )
    zc = shift_z(zc, paired)
    rest = 4 * strip
    acc, xr, vah, vdh, xrh, xrl = call(
        part(halo_kernel, plan, paired),
        [near(g_all, rows, lanes), near(g_all, rest, lanes), near(g_all, rest, lanes), near(g_all, rest, lanes), bf(rest, wide), bf(rest, wide)],
        [yh, vy, zi, coef, vspread, acc],
        aliases={5 if paired else 6: 0},
    )

    p = plan.first[BUF, :g_all] + plan.first[BUF, ::-1][:g_all]
    q = plan.first[BUF, :g_all] - plan.first[BUF, ::-1][:g_all]
    dcoef = np.concatenate([np.repeat(p[:, None], width, 1), np.repeat(q[:, None], width, 1)], 1).astype(np.float32)
    msg = near(face, lanes)
    corners = 2 * BUF * corner
    filtered, mx, my, mz = call(
        part(filter_kernel, plan, paired),
        [near(g_all, cross, lanes), [msg, msg], [msg, msg], two(face, lanes)],
        [zc, inner, outer, xr, xrh, xrl, vai, vdi, vah, vdh, acc, *halves(matrix[:, face:]), *halves(matrix[:cross]), coef, dcoef, vspread],
        [bf(rest + corners, wide), bf(rest + corners, wide), near(g_all, corners, lanes),
         near(g_all, rows, lanes), bf(rows, wide), bf(rows, wide),
         near(g_all, corners, lanes), near(g_all, corners, lanes), near(2, rows, 2 * lanes)],
    )
    ny = [shift(my[1], "gy", 1), shift(my[0], "gy", -1)]
    nx = [shift(mx[1], "gx", 1), shift(mx[0], "gx", -1)]
    nz = shift_z(mz, paired)

    along = energy(plan)
    bcoef = mirrored(plan, along).reshape(-1, lanes).astype(np.float32)
    diag, basis = call(
        part(own_kernel, plan), [near(width, width), far(cells, face, width)],
        [filtered, vai, vdi, *halves(row_matrix(plan, along, True)[:cross, :cross]), bcoef],
        [near(cells, face, width), near(g_all, cross, lanes), bf(cross, inner_all * lanes), bf(cross, inner_all * lanes), bf(g_all, cross, lanes),
         near(2, cross, 2 * lanes), pltpu.SemaphoreType.DMA((cells,))],
        flops=2 * 10**9,
        far_out=(1,),
    )
    (blocks,) = call(
        part(face_kernel, plan, paired), [far(7, width, width)], [diag, mx, my, mz, nx, ny, nz],
    )
    return basis.reshape(orbitals.shape), blocks[None, None, None]


def solution(mesh):
    return jax.shard_map(
        on_device,
        mesh=mesh,
        in_specs=(P("gx", "gy", "gz", None), P("gx", "gy", "gz")),
        out_specs=(P("gx", "gy", "gz", None), P("gx", "gy", "gz", None, None, None)),
        check_vma=False,
    )
```

```python
import functools

import jax
import jax.numpy as jnp
import ml_dtypes
import numpy as np
from jax import lax
from jax.experimental import pallas as pl
from jax.experimental.pallas import tpu as pltpu
from jax.sharding import PartitionSpec as P

BUF = 3
PENALTY = 2.0
LOW_BOUND = -1.5
CUTOFF = 8.0
HIGH_BOUND = 16.0
BF = jnp.bfloat16
F32 = jnp.float32


class Plan:
    def __init__(self, cells, width):
        self.cells, self.width = cells, width
        self.ext = cells + 2 * BUF
        self.groups = self.ext // 2
        self.inner = cells // 2
        self.lanes = 2 * width
        self.face = cells * cells
        self.strip = BUF * cells
        self.corner = -(-2 * BUF // 8) * 8
        self.yext = self.face + 2 * self.strip
        self.cross = self.yext + 2 * self.strip
        self.rows = self.cross + 2 * BUF * self.corner
        self.trows = -(-self.ext // 8) * 8
        inside = list(range(BUF, BUF + cells))
        outside = list(range(BUF)) + list(range(BUF + cells, self.ext))
        points = [(y, z) for y in inside for z in inside] + [(y, z) for y in outside for z in inside]
        points += [(y, z) for z in outside for y in inside]
        for z in outside:
            points += [(y, z) for y in outside] + [None] * (self.corner - 2 * BUF)
        self.points = points
        self.first, self.second = spectral(self.ext)
        self.inside = np.isin(np.arange(self.ext), inside)


def spectral(points):
    indices = np.arange(points)
    offsets = indices[:, None] - indices[None, :]
    first = np.zeros((points, points))
    second = np.zeros((points, points))
    for harmonic in range(1, points // 2):
        wavenum = 2.0 * np.pi * harmonic / points
        first = first - 2.0 * wavenum * np.sin(wavenum * offsets) / points
        second = second - 2.0 * wavenum * wavenum * np.cos(wavenum * offsets) / points
    second = second - np.pi * np.pi * np.cos(np.pi * offsets) / points
    return first, second


def row_matrix(plan, along, masked):
    real = np.array([p is not None for p in plan.points])
    y, z = np.array([(0, 0) if p is None else p for p in plan.points]).T
    by_y = along[y[:, None], y[None, :]] * (z[:, None] == z[None, :])
    by_z = along[z[:, None], z[None, :]] * (y[:, None] == y[None, :])
    if masked:
        by_y, by_z = by_y * plan.inside[z][:, None], by_z * plan.inside[y][:, None]
    return (by_y + by_z) * real[:, None] * real[None, :]


def mirrored(plan, along):
    g = plan.groups
    plus = along[:g, :g] + along[:g, ::-1][:, :g]
    minus = along[:g, :g] - along[:g, ::-1][:, :g]
    return np.concatenate([np.repeat(plus[:, :, None], plan.width, 2), np.repeat(minus[:, :, None], plan.width, 2)], 2)


def folded(table):
    g = table.shape[0]
    half, odd = g // 2, g % 2
    out = []
    for t in range(half + odd):
        out += [0.5 * (table[t, s] + table[t, g - 1 - s]) for s in range(half)] + [table[t, half]] * odd
        if t < half:
            out += [0.5 * (table[t, s] - table[t, g - 1 - s]) for s in range(half)]
    return np.stack(out).astype(np.float32)


def energy(plan):
    c = plan.cells
    block = plan.first[BUF : BUF + c]
    out = 0.5 * block.T @ block
    for sign, layer in ((-1.0, BUF), (1.0, BUF + c - 1)):
        unit = np.zeros(plan.ext)
        unit[layer] = 1.0
        cross = np.outer(unit, plan.first[layer])
        out = out + 0.5 * PENALTY * np.outer(unit, unit) - 0.25 * sign * (cross + cross.T)
    return out


def halves(matrix):
    high = matrix.astype(np.float32).astype(ml_dtypes.bfloat16)
    low = (matrix - high.astype(np.float64)).astype(np.float32).astype(ml_dtypes.bfloat16)
    return high, low


def split(x):
    high = x.astype(BF)
    return high, (x - high.astype(F32)).astype(BF)


def swap(x):
    return pltpu.roll(x, x.shape[-1] // 2, x.ndim - 1)


def dot(a, b):
    return jnp.dot(a, b, preferred_element_type=F32)


def dot_t(a, b):
    return lax.dot_general(a, b, (((0,), (0,)), ((), ())), preferred_element_type=F32)


def exact(a, b):
    return jnp.dot(a, b, preferred_element_type=F32, precision=lax.Precision.HIGHEST)


def three(wh, wl, sh, sl):
    return dot(wh, sh) + dot(wl, sh) + dot(wh, sl)


def low_lanes(shape):
    return lax.broadcasted_iota(jnp.int32, shape, len(shape) - 1) < shape[-1] // 2


def sides(ref, paired):
    return [ref.at[0], ref.at[1]] if paired else ref


def chunks(stop, size=16, start=0):
    return [(r, min(r + size, stop)) for r in range(start, stop, size)]


def pairs(stop, start=0):
    return [(g, min(g + 2, stop)) for g in range(start, stop, 2)]


CENTER = (HIGH_BOUND + CUTOFF) / 2.0
HALF_WIDTH = (HIGH_BOUND - CUTOFF) / 2.0
S0 = HALF_WIDTH / (LOW_BOUND - CENTER)
S1 = 1.0 / (2.0 / S0 - S0)


def mix(coef, table, items):
    total = None
    for s, item in enumerate(items):
        term = coef[table + s : table + s + 1, :] * item
        total = term if total is None else total + term
    return total


def fold_mix(coef, items):
    g = len(items)
    half, odd = g // 2, g % 2
    plus = [items[s] + items[g - 1 - s] for s in range(half)] + [items[half]] * odd
    minus = [items[s] - items[g - 1 - s] for s in range(half)]
    out, k = [None] * g, 0
    for t in range(half + odd):
        p = mix(coef, k, plus)
        k += len(plus)
        if t < half:
            q = mix(coef, k, minus)
            k += half
            out[t], out[g - 1 - t] = p + q, p - q
        else:
            out[t] = p
    return out


def spread_potential(plan, piece, count, vspread, va, vd, at):
    high = piece.astype(BF).astype(F32)
    rest = piece - high
    mid = rest.astype(BF).astype(F32)
    stacked = jnp.concatenate([high, mid, rest - mid], axis=0)
    turned = jnp.transpose(stacked)[:count, :].astype(BF)
    g_all, lanes = plan.groups, plan.lanes
    for g0, g1 in pairs(g_all):
        for k, dst, less in ((0, va, CENTER), (1, vd, 0.0)):
            cols = slice((k * g_all + g0) * lanes, (k * g_all + g1) * lanes)
            both = dot(turned, vspread[:, cols]) - less
            for g in range(g0, g1):
                dst[g, at : at + count, :] = both[:, (g - g0) * lanes : (g - g0 + 1) * lanes]


def local_terms(coef, get, count, va, vd, v0):
    items = [get(g) for g in range(va.shape[0])]
    out = fold_mix(coef, items)
    for g, own in enumerate(items):
        out[g] = out[g] + va[g, v0 : v0 + count, :] * own + vd[g, v0 : v0 + count, :] * swap(own)
    return out


def packx_kernel(plan, orb_far, pot_far, slo, shi, rlo, rhi, vt, orb, pot, sem):
    c, lanes, face, strip = plan.cells, plan.lanes, plan.face, plan.strip
    half, rest = face // 2, face // 2 - plan.strip
    slabs = list(range(BUF)) + list(range(c - BUF, c))
    copies = [pltpu.make_async_copy(pot_far, pot, sem.at[2 * BUF])]
    copies += [pltpu.make_async_copy(orb_far.at[x], orb.at[k], sem.at[k]) for k, x in enumerate(slabs)]
    for copy in copies:
        copy.start()
    copies[0].wait()
    v = jnp.concatenate([pot[pl.ds(y, c, stride=c), :] for y in range(c)], axis=1)
    vt[...] = v
    base = BUF * strip
    for out, first in ((slo, 0), (shi, c - BUF)):
        out[base:, :] = jnp.zeros((8, lanes), F32)
        for part in range(2):
            out[base + part * BUF : base + (part + 1) * BUF, :] = v[first : first + BUF, part * lanes : (part + 1) * lanes]
    for k in range(2 * BUF):
        copies[1 + k].wait()
        at = k % BUF
        near_out, rest_out = (slo, rlo) if k < BUF else (shi, rhi)
        near_out[at * strip : (at + 1) * strip, :] = jnp.concatenate([orb[k, :strip], orb[k, face - strip :]], axis=1)
        rest_out[at * rest : (at + 1) * rest, :] = jnp.concatenate([orb[k, strip:half], orb[k, half : face - strip]], axis=1)


def packy_kernel(plan, orb, vt, ylo, yhi, inner):
    c, strip, face = plan.cells, plan.strip, plan.face
    ybase = plan.inner * strip
    ylo[ybase:, :] = vt[:, : plan.lanes]
    yhi[ybase:, :] = vt[:, face - plan.lanes :]
    for j in range(plan.inner):
        a, b = orb[j], orb[c - 1 - j]
        e = jnp.concatenate([a + b, a - b], axis=1)
        inner[j] = e
        ylo[j * strip : (j + 1) * strip, :] = e[:strip]
        yhi[j * strip : (j + 1) * strip, :] = e[face - strip :]


def mirror(a, b):
    mask = low_lanes(a.shape)
    s, d = a + b, a - b
    return jnp.where(mask, s, swap(d)), jnp.where(mask, swap(s), d)


def edge_kernel(plan, vt, lo, hi, ahead, elo, ehi, vx):
    c, strip, lanes = plan.cells, plan.strip, plan.lanes
    for g in range(BUF):
        back = BUF - 1 - g
        top, bottom = mirror(lo[g * strip : (g + 1) * strip, :], hi[back * strip : (back + 1) * strip, :])
        elo[g * strip : (g + 1) * strip, :] = top
        ehi[g * strip : (g + 1) * strip, :] = bottom
    base = BUF * strip
    vx[...] = jnp.zeros(vx.shape, F32)
    vx[BUF : BUF + c, :] = vt[...]
    elo[base:, :] = jnp.zeros((8, lanes), F32)
    ehi[base:, :] = jnp.zeros((8, lanes), F32)
    for k, src in enumerate((lo, hi)):
        elo[base + k * BUF : base + (k + 1) * BUF, :] = src[base : base + BUF, :]
        ehi[base + k * BUF : base + (k + 1) * BUF, :] = src[base + BUF : base + 2 * BUF, :]
        at = 0 if k == 0 else BUF + c
        vx[at : at + BUF, :lanes] = src[base : base + BUF, :]
        vx[at : at + BUF, lanes:] = src[base + BUF : base + 2 * BUF, :]


def xhalo_kernel(plan, paired, inner, vx, elo, ehi, lo, hi, zpick, ahead, outer, zi):
    c, face, strip = plan.cells, plan.face, plan.strip
    half, rest = face // 2, face // 2 - strip
    for g in range(BUF):
        back = BUF - 1 - g
        top, bottom = mirror(lo[g * rest : (g + 1) * rest, :], hi[back * rest : (back + 1) * rest, :])
        outer[g, :strip] = elo[g * strip : (g + 1) * strip, :]
        outer[g, strip:half] = top
        outer[g, half : face - strip] = bottom
        outer[g, face - strip :] = ehi[g * strip : (g + 1) * strip, :]
    for side, dst in enumerate(sides(zi, paired)):
        start = side * (c - BUF)
        for g in range(plan.groups):
            src = outer.at[g] if g < BUF else inner.at[g - BUF]
            for k in range(BUF):
                at = g * strip + k * c
                dst[at : at + c, :] = src[pl.ds(start + k, c, stride=c), :]
        dst[plan.groups * strip :, :] = exact(vx[...], zpick[side])


def row_products(plan, get, first, stop, wh, wl, xh, xl, acc):
    lanes = plan.lanes
    for g in range(first, stop):
        h, l = split(get(g))
        xh[:, (g - first) * lanes : (g - first + 1) * lanes] = h
        xl[:, (g - first) * lanes : (g - first + 1) * lanes] = l
    for g0, g1 in pairs(stop, first):
        cols = slice((g0 - first) * lanes, (g1 - first) * lanes)
        total = three(wh[...], wl[...], xh[:, cols], xl[:, cols])
        for g in range(g0, g1):
            acc[g] = total[:, (g - g0) * lanes : (g - g0 + 1) * lanes]


def inside_kernel(plan, inner, vx, wh, wl, vspread, acc, va, vd, order, xh, xl):
    order[...] = jnp.zeros(order.shape, F32)
    spread_potential(plan, vx[...], plan.face, vspread, va, vd, 0)
    row_products(plan, lambda g: inner[g - BUF], BUF, plan.groups, wh, wl, xh, xl, acc)


def outside_kernel(plan, inner, outer, wh, wl, coef, va, vd, given, acc, order, xh, xl):
    order[...] = jnp.zeros(order.shape, F32)
    row_products(plan, lambda g: outer[g], 0, BUF, wh, wl, xh, xl, acc)

    def get(g, r0, r1):
        return outer[g, r0:r1, :] if g < BUF else inner[g - BUF, r0:r1, :]

    for r0, r1 in chunks(plan.face):
        local = local_terms(coef, lambda g: get(g, r0, r1), r1 - r0, va, vd, r0)
        for g in range(plan.groups):
            before = acc if g < BUF else given
            acc[g, r0:r1, :] = before[g, r0:r1, :] + local[g]


def ypack_kernel(plan, paired, ylo, yhi, elo, ehi, zpick, order, yh, vy, zc):
    c, lanes, strip, corner = plan.cells, plan.lanes, plan.strip, plan.corner
    for g in range(plan.groups):
        lo, hi, at = (elo, ehi, g * strip) if g < BUF else (ylo, yhi, (g - BUF) * strip)
        yh[g, :strip] = lo[at : at + strip, :]
        yh[g, strip : 2 * strip] = hi[at : at + strip, :]
    yh[:, 2 * strip :] = jnp.zeros((plan.groups, yh.shape[1] - 2 * strip, lanes), F32)
    ebase, ybase = BUF * strip, plan.inner * strip
    shift_in = lanes - strip
    vy[...] = jnp.zeros(vy.shape, F32)
    for e, y, cut, at in ((elo, ylo, shift_in, 0), (ehi, yhi, 0, strip)):
        cols = slice(at, at + strip)
        vy[:BUF, cols] = e[ebase : ebase + BUF, :][:, cut : cut + strip]
        vy[BUF + c : plan.ext, cols] = e[ebase + BUF : ebase + 2 * BUF, :][:, cut : cut + strip]
        vy[BUF : BUF + c, cols] = y[ybase:, :][:, cut : cut + strip]
    for side, dst in enumerate(sides(zc, paired)):
        start = side * (c - BUF)
        for g in range(plan.groups):
            for k in range(BUF):
                at = (g * BUF + k) * corner
                dst[at : at + corner, :] = yh[g, pl.ds(start + k, corner, stride=c), :]
        dst[plan.groups * BUF * corner :, :] = exact(vy[...], zpick[side])


def halo_kernel(plan, paired, yh, vy, zi, coef, vspread, given, acc, xr, va, vd, xh, xl):
    g_all, lanes, strip, face = plan.groups, plan.lanes, plan.strip, plan.face
    zlo, zhi = sides(zi, paired)[::-1] if paired else zi
    spread_potential(plan, vy[...], 2 * strip, vspread, va, vd, 0)
    for k, piece in enumerate((zlo, zhi)):
        at = (2 + k) * strip
        spread_potential(plan, piece[g_all * strip :, :], strip, vspread, va, vd, at)
        for g in range(g_all):
            xr[g, at : at + strip, :] = piece[g * strip : (g + 1) * strip, :]
    for g in range(g_all):
        xr[g, : 2 * strip, :] = yh[g, : 2 * strip, :]
        h, l = split(xr[g])
        xh[:, g * lanes : (g + 1) * lanes] = h
        xl[:, g * lanes : (g + 1) * lanes] = l
    for r0, r1 in chunks(4 * strip):
        local = local_terms(coef, lambda g: xr[g, r0:r1, :], r1 - r0, va, vd, r0)
        for g in range(g_all):
            acc[g, face + r0 : face + r1, :] = given[g, face + r0 : face + r1, :] + local[g]


def filter_kernel(plan, paired, zc, inner, outer, xr, xrh, xrl, vai, vdi, vah, vdh, given, wrh, wrl, wh, wl, coef, dcoef,
                  vspread, out, mx, my, mz, xh, xl, xc, y, yh, yl, va, vd, acc):
    g_all, lanes, rows, face, cross, c = plan.groups, plan.lanes, plan.rows, plan.face, plan.cross, plan.cells
    strip = plan.strip
    span = BUF * plan.corner
    mz = sides(mz, paired)
    zlo, zhi = sides(zc, paired)[::-1] if paired else zc
    rest = 4 * strip
    xh[:rest, :] = xrh[...]
    xl[:rest, :] = xrl[...]
    for k, piece in enumerate((zlo, zhi)):
        spread_potential(plan, piece[g_all * span :, :], span, vspread, va, vd, k * span)
        for g in range(g_all):
            xc[g, k * span : (k + 1) * span, :] = piece[g * span : (g + 1) * span, :]
    for g in range(g_all):
        h, l = split(xc[g])
        xh[rest:, g * lanes : (g + 1) * lanes] = h
        xl[rest:, g * lanes : (g + 1) * lanes] = l

    def put(g, r0, r1, value):
        y[g, r0:r1, :] = value
        h, l = split(value)
        yh[r0:r1, g * lanes : (g + 1) * lanes] = h
        yl[r0:r1, g * lanes : (g + 1) * lanes] = l

    corners = {}
    for r0, r1 in chunks(2 * span):
        corners[r0] = local_terms(coef, lambda g: xc[g, r0:r1, :], r1 - r0, va, vd, r0)
        for g in range(g_all):
            y[g, cross + r0 : cross + r1, :] = corners[r0][g]
    for n, (g0, g1) in enumerate(pairs(g_all)):
        slot = n % 2
        cols = slice(g0 * lanes, g1 * lanes)
        acc[slot, :, : (g1 - g0) * lanes] = three(wrh[...], wrl[...], xh[:, cols], xl[:, cols])
        for g in range(g0, g1):
            mine = slice((g - g0) * lanes, (g - g0 + 1) * lanes)
            for r0, r1 in chunks(rows):
                value = given[g, r0:r1, :] + acc[slot, r0:r1, mine]
                if r0 >= cross:
                    value = value + y[g, r0:r1, :]
                put(g, r0, r1, value * (S0 / HALF_WIDTH))

    for r0, r1 in chunks(cross):
        v, d, at = (vai, vdi, r0) if r0 < face else (vah, vdh, r0 - face)
        local = local_terms(coef, lambda g: y[g, r0:r1, :], r1 - r0, v, d, at)
        for g in range(g_all):
            if g >= BUF or r0 < face:
                if r0 >= face:
                    x = xr[g, r0 - face : r1 - face, :]
                else:
                    x = outer[g, r0:r1, :] if g < BUF else inner[g - BUF, r0:r1, :]
                out[g, r0:r1, :] = local[g] * (2.0 * S1 / HALF_WIDTH) - (S0 * S1) * x
    for n, (g0, g1) in enumerate(pairs(g_all)):
        slot = n % 2
        top = face if g1 <= BUF else cross
        cols = slice(g0 * lanes, g1 * lanes)
        acc[slot, :top, : (g1 - g0) * lanes] = three(wh[:top], wl[:top], yh[:, cols], yl[:, cols])
        for g in range(g0, g1):
            mine = slice((g - g0) * lanes, (g - g0 + 1) * lanes)
            for r0, r1 in chunks(face if g < BUF else cross):
                out[g, r0:r1, :] = out[g, r0:r1, :] + acc[slot, r0:r1, mine] * (2.0 * S1 / HALF_WIDTH)

    for r0, r1 in chunks(face):
        mask = low_lanes((r1 - r0, lanes))
        e = out[BUF, r0:r1, :]
        d = mix(dcoef, 0, [out[g, r0:r1, :] for g in range(g_all)])
        te, td = swap(e), swap(d)
        mx[0][r0:r1, :] = 0.5 * jnp.where(mask, e + te, d + td)
        mx[1][r0:r1, :] = 0.5 * jnp.where(mask, e - te, d - td)
    part = plan.inner * c
    order = list(range(BUF, BUF + c)) + list(range(BUF)) + list(range(BUF + c, plan.ext))
    mask = low_lanes((c, lanes))
    for j in range(plan.inner):
        g = BUF + j
        ylayers = [out[g, k * c : (k + 1) * c, :] for k in range(plan.ext)]
        zlayers = [out[g, pl.ds(k, c, stride=c), :] for k in range(c)]
        zlayers += [out[g, plan.yext + k * c : plan.yext + (k + 1) * c, :] for k in range(2 * BUF)]
        for layers, message in ((ylayers, my), (zlayers, mz)):
            for side, layer in enumerate((0, c - 1)):
                total = None
                for k, t in enumerate(order):
                    weight = float(plan.first[BUF + layer, t])
                    if t != BUF + layer:
                        term = weight * layers[k]
                        total = term if total is None else total + term
                value = layers[layer]
                message[side][j * c : (j + 1) * c, :] = jnp.where(mask, value, swap(total))
                message[side][part + j * c : part + (j + 1) * c, :] = jnp.where(mask, swap(value), total)


def own_kernel(plan, f, va, vd, bh, bl, coef, diag, basis, local, f2, f2h, f2l, fhi, acc, sem):
    g_all, lanes, face, cross, c = plan.groups, plan.lanes, plan.face, plan.cross, plan.cells
    copies = []
    for j in range(plan.inner):
        for r0, r1 in chunks(face, 64):
            e = f[BUF + j, r0:r1, :]
            t = swap(e)
            local[j, r0:r1, :] = (0.5 * (e + t))[:, : plan.width]
            local[c - 1 - j, r0:r1, :] = (0.5 * (e - t))[:, : plan.width]
        for x in (j, c - 1 - j):
            copies.append(pltpu.make_async_copy(local.at[x], basis.at[x], sem.at[x]))
            copies[-1].start()
    for g in range(g_all):
        top = face if g < BUF else cross
        for r0, r1 in chunks(top):
            value = f[g, r0:r1, :]
            high = value.astype(BF)
            fhi[g, r0:r1, :] = high
            twice = 2.0 * value - high.astype(F32)
            f2[g, r0:r1, :] = twice
            if g >= BUF:
                h, l = split(twice)
                f2h[r0:r1, (g - BUF) * lanes : (g - BUF + 1) * lanes] = h
                f2l[r0:r1, (g - BUF) * lanes : (g - BUF + 1) * lanes] = l
    total = jnp.zeros((lanes, 2 * lanes), F32)

    def fold(total, g, top, value):
        h, l = split(value)
        return total + dot_t(fhi[g, :top, :], jnp.concatenate([h, l], axis=1))

    def mixed(g, r0, r1):
        return mix(coef, g * g_all, [f2[s, r0:r1, :] for s in range(g_all)])

    for g in range(BUF):
        total = fold(total, g, face, jnp.concatenate([mixed(g, r0, r1) for r0, r1 in chunks(face)], axis=0))
    for n, (j0, j1) in enumerate(pairs(plan.inner)):
        slot = n % 2
        cols = slice(j0 * lanes, j1 * lanes)
        acc[slot] = three(bh[...], bl[...], f2h[:, cols], f2l[:, cols])
        for j in range(j0, j1):
            g = BUF + j
            mine = slice((j - j0) * lanes, (j - j0 + 1) * lanes)
            parts = []
            for r0, r1 in chunks(face):
                own = f2[g, r0:r1, :]
                value = acc[slot, r0:r1, mine] + mixed(g, r0, r1)
                parts.append(value + (va[g, r0:r1, :] + CENTER) * own + vd[g, r0:r1, :] * swap(own))
            parts.append(acc[slot, face:, mine])
            total = fold(total, g, cross, jnp.concatenate(parts, axis=0))
    both = total[:, :lanes] + total[:, lanes:]
    w = plan.width
    block = both[:w, :w] + both[w:, w:]
    diag[...] = 0.25 * (block + jnp.transpose(block))
    for copy in copies:
        copy.wait()


def face_block(plan, own, other, sign, scale):
    w, lanes = plan.width, plan.lanes
    ah, al = split(own[...])
    bh, bl = split(other[...])
    first = dot_t(ah, jnp.concatenate([bh, bl], axis=1))
    m = first[:, :lanes] + first[:, lanes:] + dot_t(al, bh)
    return scale * (0.25 * sign * (m[w:, :w] - m[:w, w:]) - 0.5 * PENALTY * m[:w, :w])


def yzface_kernel(plan, paired, oy, oz, ny, nz, blocks):
    oz, nz = sides(oz, paired), sides(nz, paired)[::-1] if paired else nz
    for k, (own, other) in enumerate(((oy[0], ny[0]), (oy[1], ny[1]), (oz[0], nz[0]), (oz[1], nz[1]))):
        blocks[k] = face_block(plan, own, other, -1.0 if k % 2 == 0 else 1.0, 0.5)


def xface_kernel(plan, diag, yz, ox, nx, blocks):
    blocks[0] = diag[...]
    for k in range(2):
        blocks[1 + k] = face_block(plan, ox[k], nx[k], -1.0 if k == 0 else 1.0, 1.0)
    blocks[3:] = yz[...]


def near(*shape):
    return pltpu.VMEM(shape, F32)


def far(*shape):
    return jax.ShapeDtypeStruct(shape, F32)


def call(kernel, outs, args, scratch=(), flops=0, limit=24, aliases=None, far_in=(), far_out=()):
    def place(a, where):
        return pltpu.with_memory_space_constraint(jnp.asarray(a), where)

    placed = [jax.tree.map(lambda b: place(b, pltpu.HBM if i in far_in else pltpu.VMEM), a) for i, a in enumerate(args)]
    space, apart = pl.BlockSpec(memory_space=pltpu.VMEM), pl.BlockSpec(memory_space=pl.ANY)
    return pl.pallas_call(
        kernel,
        out_shape=outs,
        in_specs=[apart if i in far_in else jax.tree.map(lambda b: space, a) for i, a in enumerate(placed)],
        out_specs=[apart if i in far_out else jax.tree.map(lambda b: space, a) for i, a in enumerate(outs)],
        scratch_shapes=list(scratch),
        input_output_aliases=aliases or {},
        compiler_params=pltpu.CompilerParams(vmem_limit_bytes=limit * 1024 * 1024),
        cost_estimate=pl.CostEstimate(flops=flops, bytes_accessed=0, transcendentals=0),
    )(*placed)


def shift(array, axis, step):
    count = lax.axis_size(axis)
    return lax.ppermute(array, axis, [(i, (i + step) % count) for i in range(count)])


def shift_z(both, paired):
    if paired:
        return shift(both, "gz", 1)
    return [shift(both[1], "gz", 1), shift(both[0], "gz", -1)]


def on_device(orbitals, potential):
    cells, width = orbitals.shape[0], orbitals.shape[-1]
    plan = Plan(cells, width)
    lanes, face, strip, rows, cross = plan.lanes, plan.face, plan.strip, plan.rows, plan.cross
    g_all, inner_all, corner = plan.groups, plan.inner, plan.corner
    paired = lax.axis_size("gz") == 2
    part = functools.partial
    bf = lambda *shape: pltpu.VMEM(shape, BF)
    wide = g_all * lanes

    def two(*shape):
        return near(2, *shape) if paired else [near(*shape), near(*shape)]

    srows, rrows, yrows = BUF * strip + 8, BUF * (face // 2 - strip), inner_all * strip + cells
    orb = orbitals.reshape(cells, face, width)
    slo, shi, rlo, rhi, vt = call(
        part(packx_kernel, plan),
        [near(srows, lanes), near(srows, lanes), near(rrows, lanes), near(rrows, lanes), near(cells, face)],
        [orb, potential.reshape(face, cells)],
        [pltpu.VMEM((2 * BUF, face, width), F32), pltpu.VMEM((face, cells), F32), pltpu.SemaphoreType.DMA((2 * BUF + 1,))],
        far_in=(0, 1),
    )
    from_slo, from_shi = shift(shi, "gx", 1), shift(slo, "gx", -1)
    ylo, yhi, inner = call(
        part(packy_kernel, plan), [near(yrows, lanes), near(yrows, lanes), near(inner_all, face, lanes)], [orb, vt],
    )
    from_ylo, from_yhi = shift(yhi, "gy", 1), shift(ylo, "gy", -1)
    from_rlo, from_rhi = shift(rhi, "gx", 1), shift(rlo, "gx", -1)

    ipick = np.zeros((2, face, lanes), np.float32)
    cpick = np.zeros((2, lanes, lanes), np.float32)
    for side in range(2):
        for k in range(BUF):
            z = side * (cells - BUF) + k
            for y in range(cells):
                ipick[side, y * cells + z, k * cells + y] = 1.0
            for y in range(2 * BUF):
                cpick[side, y * cells + z, k * corner + y] = 1.0
    elo, ehi, vx = call(
        part(edge_kernel, plan), [near(srows, lanes), near(srows, lanes), near(plan.trows, face)], [vt, from_slo, from_shi, from_ylo],
        flops=10**9,
    )
    from_elo, from_ehi = shift(ehi, "gy", 1), shift(elo, "gy", -1)

    matrix = -0.5 * row_matrix(plan, plan.second, False)
    coef = folded(-0.5 * mirrored(plan, plan.second))
    vspread = np.zeros((plan.trows, 2, g_all, lanes), np.float32)
    for g in range(g_all):
        vspread[g, :, g, :] = 0.5
        vspread[plan.ext - 1 - g, 0, g, :] = 0.5
        vspread[plan.ext - 1 - g, 1, g, :] = -0.5
    vspread = np.tile(vspread.reshape(plan.trows, -1), (3, 1)).astype(ml_dtypes.bfloat16)
    inside = halves(matrix[:, :face])
    acc, vai, vdi, early = call(
        part(inside_kernel, plan),
        [near(g_all, rows, lanes), near(g_all, face, lanes), near(g_all, face, lanes), near(8, lanes)],
        [inner, vx, *inside, vspread],
        [bf(face, inner_all * lanes), bf(face, inner_all * lanes)],
        flops=0,
    )
    outer, zi = call(
        part(xhalo_kernel, plan, paired),
        [near(BUF, face, lanes), two(g_all * strip + plan.trows, lanes)],
        [inner, vx, elo, ehi, from_rlo, from_rhi, ipick, early],
    )
    zi = shift_z(zi, paired)
    acc, order = call(
        part(outside_kernel, plan),
        [near(g_all, rows, lanes), near(8, lanes)],
        [inner, outer, *inside, coef, vai, vdi, acc],
        [bf(face, BUF * lanes), bf(face, BUF * lanes)],
        aliases={7: 0},
    )

    room = 2 * strip + (corner - 2 * BUF) * cells
    yh, vy, zc = call(
        part(ypack_kernel, plan, paired),
        [near(g_all, room, lanes), near(plan.trows, lanes), two(g_all * BUF * corner + plan.trows, lanes)],
        [from_ylo, from_yhi, from_elo, from_ehi, cpick, order],
        flops=10**10,
    )
    zc = shift_z(zc, paired)
    rest = 4 * strip
    acc, xr, vah, vdh, xrh, xrl = call(
        part(halo_kernel, plan, paired),
        [near(g_all, rows, lanes), near(g_all, rest, lanes), near(g_all, rest, lanes), near(g_all, rest, lanes), bf(rest, wide), bf(rest, wide)],
        [yh, vy, zi, coef, vspread, acc],
        aliases={5 if paired else 6: 0},
    )

    p = plan.first[BUF, :g_all] + plan.first[BUF, ::-1][:g_all]
    q = plan.first[BUF, :g_all] - plan.first[BUF, ::-1][:g_all]
    dcoef = np.concatenate([np.repeat(p[:, None], width, 1), np.repeat(q[:, None], width, 1)], 1).astype(np.float32)
    msg = near(face, lanes)
    corners = 2 * BUF * corner
    filtered, mx, my, mz = call(
        part(filter_kernel, plan, paired),
        [near(g_all, cross, lanes), [msg, msg], [msg, msg], two(face, lanes)],
        [zc, inner, outer, xr, xrh, xrl, vai, vdi, vah, vdh, acc, *halves(matrix[:, face:]), *halves(matrix[:cross]), coef, dcoef, vspread],
        [bf(rest + corners, wide), bf(rest + corners, wide), near(g_all, corners, lanes),
         near(g_all, rows, lanes), bf(rows, wide), bf(rows, wide),
         near(g_all, corners, lanes), near(g_all, corners, lanes), near(2, rows, 2 * lanes)],
    )
    ny = [shift(my[1], "gy", 1), shift(my[0], "gy", -1)]
    nx = [shift(mx[1], "gx", 1), shift(mx[0], "gx", -1)]
    nz = shift_z(mz, paired)

    along = energy(plan)
    bcoef = mirrored(plan, along).reshape(-1, lanes).astype(np.float32)
    diag, basis = call(
        part(own_kernel, plan), [near(width, width), far(cells, face, width)],
        [filtered, vai, vdi, *halves(row_matrix(plan, along, True)[:cross, :cross]), bcoef],
        [near(cells, face, width), near(g_all, cross, lanes), bf(cross, inner_all * lanes), bf(cross, inner_all * lanes), bf(g_all, cross, lanes),
         near(2, cross, 2 * lanes), pltpu.SemaphoreType.DMA((cells,))],
        flops=2 * 10**9,
        far_out=(1,),
    )
    (yz,) = call(part(yzface_kernel, plan, paired), [near(4, width, width)], [my, mz, ny, nz])
    (blocks,) = call(part(xface_kernel, plan), [far(7, width, width)], [diag, yz, mx, nx])
    return basis.reshape(orbitals.shape), blocks[None, None, None]


def solution(mesh):
    return jax.shard_map(
        on_device,
        mesh=mesh,
        in_specs=(P("gx", "gy", "gz", None), P("gx", "gy", "gz")),
        out_specs=(P("gx", "gy", "gz", None), P("gx", "gy", "gz", None, None, None)),
        check_vma=False,
    )
```

```python
import functools

import jax
import jax.numpy as jnp
import ml_dtypes
import numpy as np
from jax import lax
from jax.experimental import pallas as pl
from jax.experimental.pallas import tpu as pltpu
from jax.sharding import PartitionSpec as P

BUF = 3
PENALTY = 2.0
LOW_BOUND = -1.5
CUTOFF = 8.0
HIGH_BOUND = 16.0
BF = jnp.bfloat16
F32 = jnp.float32


class Plan:
    def __init__(self, cells, width):
        self.cells, self.width = cells, width
        self.ext = cells + 2 * BUF
        self.groups = self.ext // 2
        self.inner = cells // 2
        self.lanes = 2 * width
        self.face = cells * cells
        self.strip = BUF * cells
        self.corner = -(-2 * BUF // 8) * 8
        self.yext = self.face + 2 * self.strip
        self.cross = self.yext + 2 * self.strip
        self.rows = self.cross + 2 * BUF * self.corner
        self.trows = -(-self.ext // 8) * 8
        inside = list(range(BUF, BUF + cells))
        outside = list(range(BUF)) + list(range(BUF + cells, self.ext))
        points = [(y, z) for y in inside for z in inside] + [(y, z) for y in outside for z in inside]
        points += [(y, z) for z in outside for y in inside]
        for z in outside:
            points += [(y, z) for y in outside] + [None] * (self.corner - 2 * BUF)
        self.points = points
        self.first, self.second = spectral(self.ext)
        self.inside = np.isin(np.arange(self.ext), inside)


def spectral(points):
    indices = np.arange(points)
    offsets = indices[:, None] - indices[None, :]
    first = np.zeros((points, points))
    second = np.zeros((points, points))
    for harmonic in range(1, points // 2):
        wavenum = 2.0 * np.pi * harmonic / points
        first = first - 2.0 * wavenum * np.sin(wavenum * offsets) / points
        second = second - 2.0 * wavenum * wavenum * np.cos(wavenum * offsets) / points
    second = second - np.pi * np.pi * np.cos(np.pi * offsets) / points
    return first, second


def row_matrix(plan, along, masked):
    real = np.array([p is not None for p in plan.points])
    y, z = np.array([(0, 0) if p is None else p for p in plan.points]).T
    by_y = along[y[:, None], y[None, :]] * (z[:, None] == z[None, :])
    by_z = along[z[:, None], z[None, :]] * (y[:, None] == y[None, :])
    if masked:
        by_y, by_z = by_y * plan.inside[z][:, None], by_z * plan.inside[y][:, None]
    return (by_y + by_z) * real[:, None] * real[None, :]


def mirrored(plan, along):
    g = plan.groups
    plus = along[:g, :g] + along[:g, ::-1][:, :g]
    minus = along[:g, :g] - along[:g, ::-1][:, :g]
    return np.concatenate([np.repeat(plus[:, :, None], plan.width, 2), np.repeat(minus[:, :, None], plan.width, 2)], 2)


def folded(table):
    g = table.shape[0]
    half, odd = g // 2, g % 2
    out = []
    for t in range(half + odd):
        out += [0.5 * (table[t, s] + table[t, g - 1 - s]) for s in range(half)] + [table[t, half]] * odd
        if t < half:
            out += [0.5 * (table[t, s] - table[t, g - 1 - s]) for s in range(half)]
    return np.stack(out).astype(np.float32)


def energy(plan):
    c = plan.cells
    block = plan.first[BUF : BUF + c]
    out = 0.5 * block.T @ block
    for sign, layer in ((-1.0, BUF), (1.0, BUF + c - 1)):
        unit = np.zeros(plan.ext)
        unit[layer] = 1.0
        cross = np.outer(unit, plan.first[layer])
        out = out + 0.5 * PENALTY * np.outer(unit, unit) - 0.25 * sign * (cross + cross.T)
    return out


def halves(matrix):
    high = matrix.astype(np.float32).astype(ml_dtypes.bfloat16)
    low = (matrix - high.astype(np.float64)).astype(np.float32).astype(ml_dtypes.bfloat16)
    return high, low


def split(x):
    high = x.astype(BF)
    return high, (x - high.astype(F32)).astype(BF)


def swap(x):
    return pltpu.roll(x, x.shape[-1] // 2, x.ndim - 1)


def dot(a, b):
    return jnp.dot(a, b, preferred_element_type=F32)


def dot_t(a, b):
    return lax.dot_general(a, b, (((0,), (0,)), ((), ())), preferred_element_type=F32)


def exact(a, b):
    return jnp.dot(a, b, preferred_element_type=F32, precision=lax.Precision.HIGHEST)


def three(wh, wl, sh, sl):
    return dot(wh, sh) + dot(wl, sh) + dot(wh, sl)


def low_lanes(shape):
    return lax.broadcasted_iota(jnp.int32, shape, len(shape) - 1) < shape[-1] // 2


def sides(ref, paired):
    return [ref.at[0], ref.at[1]] if paired else ref


def chunks(stop, size=16, start=0):
    return [(r, min(r + size, stop)) for r in range(start, stop, size)]


def pairs(stop, start=0):
    return [(g, min(g + 2, stop)) for g in range(start, stop, 2)]


CENTER = (HIGH_BOUND + CUTOFF) / 2.0
HALF_WIDTH = (HIGH_BOUND - CUTOFF) / 2.0
S0 = HALF_WIDTH / (LOW_BOUND - CENTER)
S1 = 1.0 / (2.0 / S0 - S0)


def mix(coef, table, items):
    total = None
    for s, item in enumerate(items):
        term = coef[table + s : table + s + 1, :] * item
        total = term if total is None else total + term
    return total


def fold_mix(coef, items):
    g = len(items)
    half, odd = g // 2, g % 2
    plus = [items[s] + items[g - 1 - s] for s in range(half)] + [items[half]] * odd
    minus = [items[s] - items[g - 1 - s] for s in range(half)]
    out, k = [None] * g, 0
    for t in range(half + odd):
        p = mix(coef, k, plus)
        k += len(plus)
        if t < half:
            q = mix(coef, k, minus)
            k += half
            out[t], out[g - 1 - t] = p + q, p - q
        else:
            out[t] = p
    return out


def spread_potential(plan, pieces, vspread, va, vd):
    turned = []
    for piece, count in pieces:
        high = piece.astype(BF).astype(F32)
        rest = piece - high
        mid = rest.astype(BF).astype(F32)
        stacked = jnp.concatenate([high, mid, rest - mid], axis=0)
        turned.append(jnp.transpose(stacked)[:count, :])
    turned = jnp.concatenate(turned, axis=0).astype(BF)
    g_all, lanes = plan.groups, plan.lanes
    for g0, g1 in pairs(g_all):
        for k, dst, less in ((0, va, CENTER), (1, vd, 0.0)):
            cols = slice((k * g_all + g0) * lanes, (k * g_all + g1) * lanes)
            both = dot(turned, vspread[:, cols]) - less
            for g in range(g0, g1):
                dst[g] = both[:, (g - g0) * lanes : (g - g0 + 1) * lanes]


def local_terms(coef, get, count, va, vd, v0):
    items = [get(g) for g in range(va.shape[0])]
    out = fold_mix(coef, items)
    for g, own in enumerate(items):
        out[g] = out[g] + va[g, v0 : v0 + count, :] * own + vd[g, v0 : v0 + count, :] * swap(own)
    return out


def strip_kernel(plan, orb_far, pot_far, slo, shi, ylo, yhi, vt, low, high, pot, sem):
    c, lanes, face, strip, w = plan.cells, plan.lanes, plan.face, plan.strip, plan.width
    copies = [
        pltpu.make_async_copy(pot_far, pot, sem.at[0]),
        pltpu.make_async_copy(orb_far.at[:, :strip], low, sem.at[1]),
        pltpu.make_async_copy(orb_far.at[:, face - strip :], high, sem.at[2]),
    ]
    for copy in copies:
        copy.start()
    copies[0].wait()
    v = jnp.concatenate([pot[pl.ds(y, c, stride=c), :] for y in range(c)], axis=1)
    vt[...] = v
    base = BUF * strip
    for out, first in ((slo, 0), (shi, c - BUF)):
        out[base:, :] = jnp.zeros((8, lanes), F32)
        for part in range(2):
            out[base + part * BUF : base + (part + 1) * BUF, :] = v[first : first + BUF, part * lanes : (part + 1) * lanes]
    ybase = plan.inner * strip
    ylo[ybase:, :] = v[:, :lanes]
    yhi[ybase:, :] = v[:, face - lanes :]
    copies[1].wait()
    copies[2].wait()
    for out, part in ((ylo, low), (yhi, high)):
        for j in range(plan.inner):
            a, b = part[j], part[c - 1 - j]
            out[j * strip : (j + 1) * strip, :] = jnp.concatenate([a + b, a - b], axis=1)
    for k in range(BUF):
        rows = slice(k * strip, (k + 1) * strip)
        slo[rows, :] = jnp.concatenate([low[k], high[k]], axis=1)
        shi[rows, :] = jnp.concatenate([low[c - BUF + k], high[c - BUF + k]], axis=1)


def pack_kernel(plan, orb, rlo, rhi, inner):
    c, strip, face = plan.cells, plan.strip, plan.face
    half, rest = face // 2, face // 2 - plan.strip
    for k in range(BUF):
        rows = slice(k * rest, (k + 1) * rest)
        for out, x in ((rlo, k), (rhi, c - BUF + k)):
            out[rows, :] = jnp.concatenate([orb[x, strip:half], orb[x, half : face - strip]], axis=1)
    for j in range(plan.inner):
        a, b = orb[j], orb[c - 1 - j]
        inner[j] = jnp.concatenate([a + b, a - b], axis=1)


def mirror(a, b):
    mask = low_lanes(a.shape)
    s, d = a + b, a - b
    return jnp.where(mask, s, swap(d)), jnp.where(mask, swap(s), d)


def edge_kernel(plan, vt, lo, hi, ahead, elo, ehi, vx):
    c, strip, lanes = plan.cells, plan.strip, plan.lanes
    for g in range(BUF):
        back = BUF - 1 - g
        top, bottom = mirror(lo[g * strip : (g + 1) * strip, :], hi[back * strip : (back + 1) * strip, :])
        elo[g * strip : (g + 1) * strip, :] = top
        ehi[g * strip : (g + 1) * strip, :] = bottom
    base = BUF * strip
    vx[...] = jnp.zeros(vx.shape, F32)
    vx[BUF : BUF + c, :] = vt[...]
    elo[base:, :] = jnp.zeros((8, lanes), F32)
    ehi[base:, :] = jnp.zeros((8, lanes), F32)
    for k, src in enumerate((lo, hi)):
        elo[base + k * BUF : base + (k + 1) * BUF, :] = src[base : base + BUF, :]
        ehi[base + k * BUF : base + (k + 1) * BUF, :] = src[base + BUF : base + 2 * BUF, :]
        at = 0 if k == 0 else BUF + c
        vx[at : at + BUF, :lanes] = src[base : base + BUF, :]
        vx[at : at + BUF, lanes:] = src[base + BUF : base + 2 * BUF, :]


def xhalo_kernel(plan, paired, inner, vx, elo, ehi, lo, hi, zpick, ahead, outer, zi):
    c, face, strip = plan.cells, plan.face, plan.strip
    half, rest = face // 2, face // 2 - strip
    for g in range(BUF):
        back = BUF - 1 - g
        top, bottom = mirror(lo[g * rest : (g + 1) * rest, :], hi[back * rest : (back + 1) * rest, :])
        outer[g, :strip] = elo[g * strip : (g + 1) * strip, :]
        outer[g, strip:half] = top
        outer[g, half : face - strip] = bottom
        outer[g, face - strip :] = ehi[g * strip : (g + 1) * strip, :]
    for side, dst in enumerate(sides(zi, paired)):
        start = side * (c - BUF)
        for g in range(plan.groups):
            src = outer.at[g] if g < BUF else inner.at[g - BUF]
            for k in range(BUF):
                at = g * strip + k * c
                dst[at : at + c, :] = src[pl.ds(start + k, c, stride=c), :]
        dst[plan.groups * strip :, :] = exact(vx[...], zpick[side])


def row_products(plan, get, first, stop, wh, wl, xh, xl, acc):
    lanes = plan.lanes
    for g in range(first, stop):
        h, l = split(get(g))
        xh[:, (g - first) * lanes : (g - first + 1) * lanes] = h
        xl[:, (g - first) * lanes : (g - first + 1) * lanes] = l
    for g0, g1 in pairs(stop, first):
        cols = slice((g0 - first) * lanes, (g1 - first) * lanes)
        total = three(wh[...], wl[...], xh[:, cols], xl[:, cols])
        for g in range(g0, g1):
            acc[g] = total[:, (g - g0) * lanes : (g - g0 + 1) * lanes]


def inside_kernel(plan, inner, vx, wh, wl, vspread, acc, va, vd, order, xh, xl):
    order[...] = jnp.zeros(order.shape, F32)
    spread_potential(plan, [(vx[...], plan.face)], vspread, va, vd)
    row_products(plan, lambda g: inner[g - BUF], BUF, plan.groups, wh, wl, xh, xl, acc)


def outside_kernel(plan, inner, outer, wh, wl, coef, va, vd, given, acc, order, xh, xl):
    order[...] = jnp.zeros(order.shape, F32)
    row_products(plan, lambda g: outer[g], 0, BUF, wh, wl, xh, xl, acc)

    def get(g, r0, r1):
        return outer[g, r0:r1, :] if g < BUF else inner[g - BUF, r0:r1, :]

    for r0, r1 in chunks(plan.face):
        local = local_terms(coef, lambda g: get(g, r0, r1), r1 - r0, va, vd, r0)
        for g in range(plan.groups):
            before = acc if g < BUF else given
            acc[g, r0:r1, :] = before[g, r0:r1, :] + local[g]


def ypack_kernel(plan, paired, ylo, yhi, elo, ehi, zpick, order, yh, vy, zc):
    c, lanes, strip, corner = plan.cells, plan.lanes, plan.strip, plan.corner
    for g in range(plan.groups):
        lo, hi, at = (elo, ehi, g * strip) if g < BUF else (ylo, yhi, (g - BUF) * strip)
        yh[g, :strip] = lo[at : at + strip, :]
        yh[g, strip : 2 * strip] = hi[at : at + strip, :]
    yh[:, 2 * strip :] = jnp.zeros((plan.groups, yh.shape[1] - 2 * strip, lanes), F32)
    ebase, ybase = BUF * strip, plan.inner * strip
    shift_in = lanes - strip
    vy[...] = jnp.zeros(vy.shape, F32)
    for e, y, cut, at in ((elo, ylo, shift_in, 0), (ehi, yhi, 0, strip)):
        cols = slice(at, at + strip)
        vy[:BUF, cols] = e[ebase : ebase + BUF, :][:, cut : cut + strip]
        vy[BUF + c : plan.ext, cols] = e[ebase + BUF : ebase + 2 * BUF, :][:, cut : cut + strip]
        vy[BUF : BUF + c, cols] = y[ybase:, :][:, cut : cut + strip]
    for side, dst in enumerate(sides(zc, paired)):
        start = side * (c - BUF)
        for g in range(plan.groups):
            for k in range(BUF):
                at = (g * BUF + k) * corner
                dst[at : at + corner, :] = yh[g, pl.ds(start + k, corner, stride=c), :]
        dst[plan.groups * BUF * corner :, :] = exact(vy[...], zpick[side])


def halo_kernel(plan, paired, yh, vy, zi, coef, vspread, given, acc, xr, va, vd, xh, xl):
    g_all, lanes, strip, face = plan.groups, plan.lanes, plan.strip, plan.face
    zlo, zhi = sides(zi, paired)[::-1] if paired else zi
    pots = [(vy[...], 2 * strip)] + [(piece[g_all * strip :, :], strip) for piece in (zlo, zhi)]
    spread_potential(plan, pots, vspread, va, vd)
    for k, piece in enumerate((zlo, zhi)):
        at = (2 + k) * strip
        for g in range(g_all):
            xr[g, at : at + strip, :] = piece[g * strip : (g + 1) * strip, :]
    for g in range(g_all):
        xr[g, : 2 * strip, :] = yh[g, : 2 * strip, :]
        h, l = split(xr[g])
        xh[:, g * lanes : (g + 1) * lanes] = h
        xl[:, g * lanes : (g + 1) * lanes] = l
    for r0, r1 in chunks(4 * strip):
        local = local_terms(coef, lambda g: xr[g, r0:r1, :], r1 - r0, va, vd, r0)
        for g in range(g_all):
            acc[g, face + r0 : face + r1, :] = given[g, face + r0 : face + r1, :] + local[g]


def filter_kernel(plan, paired, zc, inner, outer, xr, xrh, xrl, vai, vdi, vah, vdh, given, wrh, wrl, wh, wl, coef, dcoef,
                  vspread, out, mx, my, mz, xh, xl, xc, y, yh, yl, va, vd, acc):
    g_all, lanes, rows, face, cross, c = plan.groups, plan.lanes, plan.rows, plan.face, plan.cross, plan.cells
    strip = plan.strip
    span = BUF * plan.corner
    mz = sides(mz, paired)
    zlo, zhi = sides(zc, paired)[::-1] if paired else zc
    rest = 4 * strip
    xh[:rest, :] = xrh[...]
    xl[:rest, :] = xrl[...]
    spread_potential(plan, [(piece[g_all * span :, :], span) for piece in (zlo, zhi)], vspread, va, vd)
    for k, piece in enumerate((zlo, zhi)):
        for g in range(g_all):
            xc[g, k * span : (k + 1) * span, :] = piece[g * span : (g + 1) * span, :]
    for g in range(g_all):
        h, l = split(xc[g])
        xh[rest:, g * lanes : (g + 1) * lanes] = h
        xl[rest:, g * lanes : (g + 1) * lanes] = l

    def put(g, r0, r1, value):
        y[g, r0:r1, :] = value
        h, l = split(value)
        yh[r0:r1, g * lanes : (g + 1) * lanes] = h
        yl[r0:r1, g * lanes : (g + 1) * lanes] = l

    corners = {}
    for r0, r1 in chunks(2 * span):
        corners[r0] = local_terms(coef, lambda g: xc[g, r0:r1, :], r1 - r0, va, vd, r0)
        for g in range(g_all):
            y[g, cross + r0 : cross + r1, :] = corners[r0][g]
    for n, (g0, g1) in enumerate(pairs(g_all)):
        slot = n % 2
        cols = slice(g0 * lanes, g1 * lanes)
        acc[slot, :, : (g1 - g0) * lanes] = three(wrh[...], wrl[...], xh[:, cols], xl[:, cols])
        for g in range(g0, g1):
            mine = slice((g - g0) * lanes, (g - g0 + 1) * lanes)
            for r0, r1 in chunks(rows):
                value = given[g, r0:r1, :] + acc[slot, r0:r1, mine]
                if r0 >= cross:
                    value = value + y[g, r0:r1, :]
                put(g, r0, r1, value * (S0 / HALF_WIDTH))

    for r0, r1 in chunks(cross):
        v, d, at = (vai, vdi, r0) if r0 < face else (vah, vdh, r0 - face)
        local = local_terms(coef, lambda g: y[g, r0:r1, :], r1 - r0, v, d, at)
        for g in range(g_all):
            if g >= BUF or r0 < face:
                if r0 >= face:
                    x = xr[g, r0 - face : r1 - face, :]
                else:
                    x = outer[g, r0:r1, :] if g < BUF else inner[g - BUF, r0:r1, :]
                out[g, r0:r1, :] = local[g] * (2.0 * S1 / HALF_WIDTH) - (S0 * S1) * x
    for n, (g0, g1) in enumerate(pairs(g_all)):
        slot = n % 2
        top = face if g1 <= BUF else cross
        cols = slice(g0 * lanes, g1 * lanes)
        acc[slot, :top, : (g1 - g0) * lanes] = three(wh[:top], wl[:top], yh[:, cols], yl[:, cols])
        for g in range(g0, g1):
            mine = slice((g - g0) * lanes, (g - g0 + 1) * lanes)
            for r0, r1 in chunks(face if g < BUF else cross):
                out[g, r0:r1, :] = out[g, r0:r1, :] + acc[slot, r0:r1, mine] * (2.0 * S1 / HALF_WIDTH)

    for r0, r1 in chunks(face):
        mask = low_lanes((r1 - r0, lanes))
        e = out[BUF, r0:r1, :]
        d = mix(dcoef, 0, [out[g, r0:r1, :] for g in range(g_all)])
        te, td = swap(e), swap(d)
        mx[0][r0:r1, :] = 0.5 * jnp.where(mask, e + te, d + td)
        mx[1][r0:r1, :] = 0.5 * jnp.where(mask, e - te, d - td)
    part = plan.inner * c
    order = list(range(BUF, BUF + c)) + list(range(BUF)) + list(range(BUF + c, plan.ext))
    mask = low_lanes((c, lanes))
    for j in range(plan.inner):
        g = BUF + j
        ylayers = [out[g, k * c : (k + 1) * c, :] for k in range(plan.ext)]
        zlayers = [out[g, pl.ds(k, c, stride=c), :] for k in range(c)]
        zlayers += [out[g, plan.yext + k * c : plan.yext + (k + 1) * c, :] for k in range(2 * BUF)]
        for layers, message in ((ylayers, my), (zlayers, mz)):
            for side, layer in enumerate((0, c - 1)):
                total = None
                for k, t in enumerate(order):
                    weight = float(plan.first[BUF + layer, t])
                    if t != BUF + layer:
                        term = weight * layers[k]
                        total = term if total is None else total + term
                value = layers[layer]
                message[side][j * c : (j + 1) * c, :] = jnp.where(mask, value, swap(total))
                message[side][part + j * c : part + (j + 1) * c, :] = jnp.where(mask, swap(value), total)


def own_kernel(plan, f, va, vd, bh, bl, coef, diag, basis, local, f2, f2h, f2l, fhi, acc, sem):
    g_all, lanes, face, cross, c = plan.groups, plan.lanes, plan.face, plan.cross, plan.cells
    copies = []
    for j in range(plan.inner):
        for r0, r1 in chunks(face, 64):
            e = f[BUF + j, r0:r1, :]
            t = swap(e)
            local[j, r0:r1, :] = (0.5 * (e + t))[:, : plan.width]
            local[c - 1 - j, r0:r1, :] = (0.5 * (e - t))[:, : plan.width]
        for x in (j, c - 1 - j):
            copies.append(pltpu.make_async_copy(local.at[x], basis.at[x], sem.at[x]))
            copies[-1].start()
    for g in range(g_all):
        top = face if g < BUF else cross
        for r0, r1 in chunks(top):
            value = f[g, r0:r1, :]
            high = value.astype(BF)
            fhi[g, r0:r1, :] = high
            twice = 2.0 * value - high.astype(F32)
            f2[g, r0:r1, :] = twice
            if g >= BUF:
                h, l = split(twice)
                f2h[r0:r1, (g - BUF) * lanes : (g - BUF + 1) * lanes] = h
                f2l[r0:r1, (g - BUF) * lanes : (g - BUF + 1) * lanes] = l
    total = jnp.zeros((lanes, 2 * lanes), F32)

    def fold(total, g, top, value):
        h, l = split(value)
        return total + dot_t(fhi[g, :top, :], jnp.concatenate([h, l], axis=1))

    def mixed(g, r0, r1):
        return mix(coef, g * g_all, [f2[s, r0:r1, :] for s in range(g_all)])

    for g in range(BUF):
        total = fold(total, g, face, jnp.concatenate([mixed(g, r0, r1) for r0, r1 in chunks(face)], axis=0))
    for n, (j0, j1) in enumerate(pairs(plan.inner)):
        slot = n % 2
        cols = slice(j0 * lanes, j1 * lanes)
        acc[slot] = three(bh[...], bl[...], f2h[:, cols], f2l[:, cols])
        for j in range(j0, j1):
            g = BUF + j
            mine = slice((j - j0) * lanes, (j - j0 + 1) * lanes)
            parts = []
            for r0, r1 in chunks(face):
                own = f2[g, r0:r1, :]
                value = acc[slot, r0:r1, mine] + mixed(g, r0, r1)
                parts.append(value + (va[g, r0:r1, :] + CENTER) * own + vd[g, r0:r1, :] * swap(own))
            parts.append(acc[slot, face:, mine])
            total = fold(total, g, cross, jnp.concatenate(parts, axis=0))
    both = total[:, :lanes] + total[:, lanes:]
    w = plan.width
    block = both[:w, :w] + both[w:, w:]
    diag[...] = 0.25 * (block + jnp.transpose(block))
    for copy in copies:
        copy.wait()


def face_block(plan, own, other, sign, scale):
    w, lanes = plan.width, plan.lanes
    ah, al = split(own[...])
    bh, bl = split(other[...])
    first = dot_t(ah, jnp.concatenate([bh, bl], axis=1))
    m = first[:, :lanes] + first[:, lanes:] + dot_t(al, bh)
    return scale * (0.25 * sign * (m[w:, :w] - m[:w, w:]) - 0.5 * PENALTY * m[:w, :w])


def yzface_kernel(plan, paired, oy, oz, ny, nz, blocks):
    oz, nz = sides(oz, paired), sides(nz, paired)[::-1] if paired else nz
    for k, (own, other) in enumerate(((oy[0], ny[0]), (oy[1], ny[1]), (oz[0], nz[0]), (oz[1], nz[1]))):
        blocks[k] = face_block(plan, own, other, -1.0 if k % 2 == 0 else 1.0, 0.5)


def xface_kernel(plan, diag, yz, ox, nx, blocks, local, sem):
    copies = [
        pltpu.make_async_copy(diag, blocks.at[0], sem.at[0]),
        pltpu.make_async_copy(yz, blocks.at[3:7], sem.at[1]),
        pltpu.make_async_copy(local, blocks.at[1:3], sem.at[2]),
    ]
    copies[0].start()
    copies[1].start()
    for k in range(2):
        local[k] = face_block(plan, ox[k], nx[k], -1.0 if k == 0 else 1.0, 1.0)
    copies[2].start()
    for copy in copies:
        copy.wait()


def near(*shape):
    return pltpu.VMEM(shape, F32)


def far(*shape):
    return jax.ShapeDtypeStruct(shape, F32)


def call(kernel, outs, args, scratch=(), flops=0, limit=24, aliases=None, far_in=(), far_out=()):
    def place(a, where):
        return pltpu.with_memory_space_constraint(jnp.asarray(a), where)

    placed = [jax.tree.map(lambda b: place(b, pltpu.HBM if i in far_in else pltpu.VMEM), a) for i, a in enumerate(args)]
    space, apart = pl.BlockSpec(memory_space=pltpu.VMEM), pl.BlockSpec(memory_space=pl.ANY)
    return pl.pallas_call(
        kernel,
        out_shape=outs,
        in_specs=[apart if i in far_in else jax.tree.map(lambda b: space, a) for i, a in enumerate(placed)],
        out_specs=[apart if i in far_out else jax.tree.map(lambda b: space, a) for i, a in enumerate(outs)],
        scratch_shapes=list(scratch),
        input_output_aliases=aliases or {},
        compiler_params=pltpu.CompilerParams(vmem_limit_bytes=limit * 1024 * 1024),
        cost_estimate=pl.CostEstimate(flops=flops, bytes_accessed=0, transcendentals=0),
    )(*placed)


def shift(array, axis, step):
    count = lax.axis_size(axis)
    return lax.ppermute(array, axis, [(i, (i + step) % count) for i in range(count)])


def shift_z(both, paired):
    if paired:
        return shift(both, "gz", 1)
    return [shift(both[1], "gz", 1), shift(both[0], "gz", -1)]


def on_device(orbitals, potential):
    cells, width = orbitals.shape[0], orbitals.shape[-1]
    plan = Plan(cells, width)
    lanes, face, strip, rows, cross = plan.lanes, plan.face, plan.strip, plan.rows, plan.cross
    g_all, inner_all, corner = plan.groups, plan.inner, plan.corner
    paired = lax.axis_size("gz") == 2
    part = functools.partial
    bf = lambda *shape: pltpu.VMEM(shape, BF)
    wide = g_all * lanes

    def two(*shape):
        return near(2, *shape) if paired else [near(*shape), near(*shape)]

    srows, rrows, yrows = BUF * strip + 8, BUF * (face // 2 - strip), inner_all * strip + cells
    orb = orbitals.reshape(cells, face, width)
    slo, shi, ylo, yhi, vt = call(
        part(strip_kernel, plan),
        [near(srows, lanes), near(srows, lanes), near(yrows, lanes), near(yrows, lanes), near(cells, face)],
        [orb, potential.reshape(face, cells)],
        [near(cells, strip, width), near(cells, strip, width), near(face, cells), pltpu.SemaphoreType.DMA((3,))],
        far_in=(0, 1),
    )
    from_ylo, from_yhi = shift(yhi, "gy", 1), shift(ylo, "gy", -1)
    from_slo, from_shi = shift(shi, "gx", 1), shift(slo, "gx", -1)
    rlo, rhi, inner = call(
        part(pack_kernel, plan), [near(rrows, lanes), near(rrows, lanes), near(inner_all, face, lanes)], [orb],
    )
    from_rlo, from_rhi = shift(rhi, "gx", 1), shift(rlo, "gx", -1)

    ipick = np.zeros((2, face, lanes), np.float32)
    cpick = np.zeros((2, lanes, lanes), np.float32)
    for side in range(2):
        for k in range(BUF):
            z = side * (cells - BUF) + k
            for y in range(cells):
                ipick[side, y * cells + z, k * cells + y] = 1.0
            for y in range(2 * BUF):
                cpick[side, y * cells + z, k * corner + y] = 1.0
    elo, ehi, vx = call(
        part(edge_kernel, plan), [near(srows, lanes), near(srows, lanes), near(plan.trows, face)], [vt, from_slo, from_shi, from_ylo],
        flops=2*10**9,
    )
    from_elo, from_ehi = shift(ehi, "gy", 1), shift(elo, "gy", -1)

    matrix = -0.5 * row_matrix(plan, plan.second, False)
    coef = folded(-0.5 * mirrored(plan, plan.second))
    vspread = np.zeros((plan.trows, 2, g_all, lanes), np.float32)
    for g in range(g_all):
        vspread[g, :, g, :] = 0.5
        vspread[plan.ext - 1 - g, 0, g, :] = 0.5
        vspread[plan.ext - 1 - g, 1, g, :] = -0.5
    vspread = np.tile(vspread.reshape(plan.trows, -1), (3, 1)).astype(ml_dtypes.bfloat16)
    inside = halves(matrix[:, :face])
    acc, vai, vdi, early = call(
        part(inside_kernel, plan),
        [near(g_all, rows, lanes), near(g_all, face, lanes), near(g_all, face, lanes), near(8, lanes)],
        [inner, vx, *inside, vspread],
        [bf(face, inner_all * lanes), bf(face, inner_all * lanes)],
        flops=0,
    )
    outer, zi = call(
        part(xhalo_kernel, plan, paired),
        [near(BUF, face, lanes), two(g_all * strip + plan.trows, lanes)],
        [inner, vx, elo, ehi, from_rlo, from_rhi, ipick, early],
    )
    zi = shift_z(zi, paired)
    acc, order = call(
        part(outside_kernel, plan),
        [near(g_all, rows, lanes), near(8, lanes)],
        [inner, outer, *inside, coef, vai, vdi, acc],
        [bf(face, BUF * lanes), bf(face, BUF * lanes)],
        aliases={7: 0},
    )

    room = 2 * strip + (corner - 2 * BUF) * cells
    yh, vy, zc = call(
        part(ypack_kernel, plan, paired),
        [near(g_all, room, lanes), near(plan.trows, lanes), two(g_all * BUF * corner + plan.trows, lanes)],
        [from_ylo, from_yhi, from_elo, from_ehi, cpick, order],
        flops=10**10,
    )
    zc = shift_z(zc, paired)
    rest = 4 * strip
    acc, xr, vah, vdh, xrh, xrl = call(
        part(halo_kernel, plan, paired),
        [near(g_all, rows, lanes), near(g_all, rest, lanes), near(g_all, rest, lanes), near(g_all, rest, lanes), bf(rest, wide), bf(rest, wide)],
        [yh, vy, zi, coef, vspread, acc],
        aliases={5 if paired else 6: 0},
    )

    p = plan.first[BUF, :g_all] + plan.first[BUF, ::-1][:g_all]
    q = plan.first[BUF, :g_all] - plan.first[BUF, ::-1][:g_all]
    dcoef = np.concatenate([np.repeat(p[:, None], width, 1), np.repeat(q[:, None], width, 1)], 1).astype(np.float32)
    msg = near(face, lanes)
    corners = 2 * BUF * corner
    filtered, mx, my, mz = call(
        part(filter_kernel, plan, paired),
        [near(g_all, cross, lanes), [msg, msg], [msg, msg], two(face, lanes)],
        [zc, inner, outer, xr, xrh, xrl, vai, vdi, vah, vdh, acc, *halves(matrix[:, face:]), *halves(matrix[:cross]), coef, dcoef, vspread],
        [bf(rest + corners, wide), bf(rest + corners, wide), near(g_all, corners, lanes),
         near(g_all, rows, lanes), bf(rows, wide), bf(rows, wide),
         near(g_all, corners, lanes), near(g_all, corners, lanes), near(2, rows, 2 * lanes)],
    )
    ny = [shift(my[1], "gy", 1), shift(my[0], "gy", -1)]
    nx = [shift(mx[1], "gx", 1), shift(mx[0], "gx", -1)]
    nz = shift_z(mz, paired)

    along = energy(plan)
    bcoef = mirrored(plan, along).reshape(-1, lanes).astype(np.float32)
    diag, basis = call(
        part(own_kernel, plan), [near(width, width), far(cells, face, width)],
        [filtered, vai, vdi, *halves(row_matrix(plan, along, True)[:cross, :cross]), bcoef],
        [near(cells, face, width), near(g_all, cross, lanes), bf(cross, inner_all * lanes), bf(cross, inner_all * lanes), bf(g_all, cross, lanes),
         near(2, cross, 2 * lanes), pltpu.SemaphoreType.DMA((cells,))],
        flops=2 * 10**9,
        far_out=(1,),
    )
    (yz,) = call(part(yzface_kernel, plan, paired), [near(4, width, width)], [my, mz, ny, nz])
    (blocks,) = call(
        part(xface_kernel, plan), [far(7, width, width)], [diag, yz, mx, nx],
        [near(2, width, width), pltpu.SemaphoreType.DMA((3,))], far_out=(0,),
    )
    return basis.reshape(orbitals.shape), blocks[None, None, None]


def solution(mesh):
    return jax.shard_map(
        on_device,
        mesh=mesh,
        in_specs=(P("gx", "gy", "gz", None), P("gx", "gy", "gz")),
        out_specs=(P("gx", "gy", "gz", None), P("gx", "gy", "gz", None, None, None)),
        check_vma=False,
    )
```

```python
import functools

import jax
import jax.numpy as jnp
import ml_dtypes
import numpy as np
from jax import lax
from jax.experimental import pallas as pl
from jax.experimental.pallas import tpu as pltpu
from jax.sharding import PartitionSpec as P

BUF = 3
PENALTY = 2.0
LOW_BOUND = -1.5
CUTOFF = 8.0
HIGH_BOUND = 16.0
BF = jnp.bfloat16
F32 = jnp.float32


class Plan:
    def __init__(self, cells, width):
        self.cells, self.width = cells, width
        self.ext = cells + 2 * BUF
        self.groups = self.ext // 2
        self.inner = cells // 2
        self.lanes = 2 * width
        self.face = cells * cells
        self.strip = BUF * cells
        self.corner = -(-2 * BUF // 8) * 8
        self.yext = self.face + 2 * self.strip
        self.cross = self.yext + 2 * self.strip
        self.rows = self.cross + 2 * BUF * self.corner
        self.trows = -(-self.ext // 8) * 8
        inside = list(range(BUF, BUF + cells))
        outside = list(range(BUF)) + list(range(BUF + cells, self.ext))
        points = [(y, z) for y in inside for z in inside] + [(y, z) for y in outside for z in inside]
        points += [(y, z) for z in outside for y in inside]
        gap = self.corner - 2 * BUF
        for z in outside:
            points += [(y, z) for y in outside[:BUF]] + [None] * gap + [(y, z) for y in outside[BUF:]]
        self.fold = self.rows // 2
        self.flat = self.cross // 2
        self.lot = -(-self.fold // 16) * 16
        self.points = points
        self.first, self.second = spectral(self.ext)
        self.inside = np.isin(np.arange(self.ext), inside)


def spectral(points):
    indices = np.arange(points)
    offsets = indices[:, None] - indices[None, :]
    first = np.zeros((points, points))
    second = np.zeros((points, points))
    for harmonic in range(1, points // 2):
        wavenum = 2.0 * np.pi * harmonic / points
        first = first - 2.0 * wavenum * np.sin(wavenum * offsets) / points
        second = second - 2.0 * wavenum * wavenum * np.cos(wavenum * offsets) / points
    second = second - np.pi * np.pi * np.cos(np.pi * offsets) / points
    return first, second


def row_matrix(plan, along, masked):
    real = np.array([p is not None for p in plan.points])
    y, z = np.array([(0, 0) if p is None else p for p in plan.points]).T
    by_y = along[y[:, None], y[None, :]] * (z[:, None] == z[None, :])
    by_z = along[z[:, None], z[None, :]] * (y[:, None] == y[None, :])
    if masked:
        by_y, by_z = by_y * plan.inside[z][:, None], by_z * plan.inside[y][:, None]
    return (by_y + by_z) * real[:, None] * real[None, :]


def mirror_basis(plan):
    c, face, strip = plan.cells, plan.face, plan.strip
    kept = [(y * c + z, (c - 1 - y) * c + z) for y in range(c // 2) for z in range(c)]
    kept += [(face + k * c + z, face + (2 * BUF - 1 - k) * c + z) for k in range(BUF) for z in range(c)]
    kept += [(plan.yext + k * c + y, plan.yext + k * c + c - 1 - y) for k in range(2 * BUF) for y in range(c // 2)]
    for m in range(BUF):
        for r in range(plan.corner):
            at = plan.cross + (2 * m + (r >= plan.corner // 2)) * plan.corner
            kept.append((at + r, at + plan.corner - 1 - r))
    out = np.zeros((2, plan.lot, plan.rows))
    for i, (a, b) in enumerate(kept):
        out[:, i, a] += 1.0
        out[0, i, b] += 1.0
        out[1, i, b] -= 1.0
    return out


def folded_rows(plan, matrix):
    basis = mirror_basis(plan)
    return 0.25 * np.einsum("pia,ab,pjb->pij", basis, matrix, basis, optimize=True)


def mirrored(plan, along):
    g = plan.groups
    plus = along[:g, :g] + along[:g, ::-1][:, :g]
    minus = along[:g, :g] - along[:g, ::-1][:, :g]
    return np.concatenate([np.repeat(plus[:, :, None], plan.width, 2), np.repeat(minus[:, :, None], plan.width, 2)], 2)


def folded(table):
    g = table.shape[0]
    half, odd = g // 2, g % 2
    out = []
    for t in range(half + odd):
        out += [0.5 * (table[t, s] + table[t, g - 1 - s]) for s in range(half)] + [table[t, half]] * odd
        if t < half:
            out += [0.5 * (table[t, s] - table[t, g - 1 - s]) for s in range(half)]
    return np.stack(out).astype(np.float32)


def energy(plan):
    c = plan.cells
    block = plan.first[BUF : BUF + c]
    out = 0.5 * block.T @ block
    for sign, layer in ((-1.0, BUF), (1.0, BUF + c - 1)):
        unit = np.zeros(plan.ext)
        unit[layer] = 1.0
        cross = np.outer(unit, plan.first[layer])
        out = out + 0.5 * PENALTY * np.outer(unit, unit) - 0.25 * sign * (cross + cross.T)
    return out


def halves(matrix):
    high = matrix.astype(np.float32).astype(ml_dtypes.bfloat16)
    low = (matrix - high.astype(np.float64)).astype(np.float32).astype(ml_dtypes.bfloat16)
    return high, low


def split(x):
    high = x.astype(BF)
    return high, (x - high.astype(F32)).astype(BF)


def swap(x):
    return pltpu.roll(x, x.shape[-1] // 2, x.ndim - 1)


def dot(a, b):
    return jnp.dot(a, b, preferred_element_type=F32)


def dot_t(a, b):
    return lax.dot_general(a, b, (((0,), (0,)), ((), ())), preferred_element_type=F32)


def exact(a, b):
    return jnp.dot(a, b, preferred_element_type=F32, precision=lax.Precision.HIGHEST)


def three(wh, wl, sh, sl):
    return dot(wh, sh) + dot(wl, sh) + dot(wh, sl)


def flip(x):
    row = lax.broadcasted_iota(jnp.int32, x.shape, 0)
    x = pltpu.roll(x, 4, 0)
    x = jnp.where(lax.rem(row, 4) < 2, pltpu.roll(x, 6, 0), pltpu.roll(x, 2, 0))
    return jnp.where(lax.rem(row, 2) < 1, pltpu.roll(x, 7, 0), pltpu.roll(x, 1, 0))


def put_folded(sh, sl, lot, at, cols, plus, minus):
    for p, value in enumerate((plus, minus)):
        h, l = split(value)
        sh[p * lot + at : p * lot + at + value.shape[0], cols] = h
        sl[p * lot + at : p * lot + at + value.shape[0], cols] = l


def fold_blocks(blocks, put, at):
    a, b = blocks
    put(at, a + b, a - b)


def fold_planes(blocks, put, at):
    firsts, lasts = [p[:8] for p in blocks], [flip(p[8:]) for p in blocks]
    put(at, jnp.concatenate([a + b for a, b in zip(firsts, lasts)], axis=0),
        jnp.concatenate([a - b for a, b in zip(firsts, lasts)], axis=0))


def fold_corners(blocks, put, at):
    plus, minus = [], []
    for block in blocks:
        a, b = block[:8], block[8:]
        fa, fb = flip(a), flip(b)
        first = lax.broadcasted_iota(jnp.int32, a.shape, 0) < 4
        plus.append(jnp.where(first, a + fa, b + fb))
        minus.append(jnp.where(first, a - fa, b - fb))
    zero = jnp.zeros_like(plus[0])
    put(at, jnp.concatenate(plus + [zero], axis=0), jnp.concatenate(minus + [zero], axis=0))


def fold_inside(plan, get, put):
    c = plan.cells
    for y in range(c // 2):
        fold_blocks([get(y * c, c), get((c - 1 - y) * c, c)], put, y * c)


def fold_halo(plan, get, put):
    c = plan.cells
    for k in range(BUF):
        fold_blocks([get(k * c, c), get((2 * BUF - 1 - k) * c, c)], put, plan.face // 2 + k * c)
    at = 2 * plan.strip
    for k in range(0, 2 * BUF, 2):
        fold_planes([get(at + k * c, c), get(at + (k + 1) * c, c)], put, plan.yext // 2 + k * 8)


def unfold(plan, v0, v1, corners):
    c = plan.cells

    def both(at, n):
        a, b = v0(at, n), v1(at, n)
        return a + b, a - b

    for y in range(c // 2):
        a, b = both(y * c, c)
        yield fold_blocks, y * c, [(y * c, a), ((c - 1 - y) * c, b)]
    at = plan.face // 2
    for k in range(BUF):
        a, b = both(at + k * c, c)
        yield fold_blocks, at + k * c, [(plan.face + k * c, a), (plan.face + (2 * BUF - 1 - k) * c, b)]
    at = plan.yext // 2
    for k in range(0, 2 * BUF, 2):
        made = []
        for m in (k, k + 1):
            a, b = both(at + m * 8, 8)
            made.append((plan.yext + m * c, jnp.concatenate([a, flip(b)], axis=0)))
        yield fold_planes, at + k * 8, made
    if corners:
        at, made = plan.cross // 2, []
        for m in range(BUF):
            a, b = both(at + m * 8, 8)
            first = lax.broadcasted_iota(jnp.int32, a.shape, 0) < 4
            b = flip(b)
            made.append((plan.cross + m * 16, jnp.concatenate([jnp.where(first, a, b), jnp.where(first, b, a)], axis=0)))
        yield fold_corners, at, made


def low_lanes(shape):
    return lax.broadcasted_iota(jnp.int32, shape, len(shape) - 1) < shape[-1] // 2


def sides(ref, paired):
    return [ref.at[0], ref.at[1]] if paired else ref


def chunks(stop, size=16, start=0):
    return [(r, min(r + size, stop)) for r in range(start, stop, size)]


def pairs(stop, start=0):
    return [(g, min(g + 2, stop)) for g in range(start, stop, 2)]


CENTER = (HIGH_BOUND + CUTOFF) / 2.0
HALF_WIDTH = (HIGH_BOUND - CUTOFF) / 2.0
S0 = HALF_WIDTH / (LOW_BOUND - CENTER)
S1 = 1.0 / (2.0 / S0 - S0)


def mix(coef, table, items):
    total = None
    for s, item in enumerate(items):
        term = coef[table + s : table + s + 1, :] * item
        total = term if total is None else total + term
    return total


def fold_mix(coef, items):
    g = len(items)
    half, odd = g // 2, g % 2
    plus = [items[s] + items[g - 1 - s] for s in range(half)] + [items[half]] * odd
    minus = [items[s] - items[g - 1 - s] for s in range(half)]
    out, k = [None] * g, 0
    for t in range(half + odd):
        p = mix(coef, k, plus)
        k += len(plus)
        if t < half:
            q = mix(coef, k, minus)
            k += half
            out[t], out[g - 1 - t] = p + q, p - q
        else:
            out[t] = p
    return out


def spread_potential(plan, pieces, vspread, va, vd):
    turned = []
    for piece, start, stop in pieces:
        high = piece.astype(BF).astype(F32)
        rest = piece - high
        mid = rest.astype(BF).astype(F32)
        stacked = jnp.concatenate([high, mid, rest - mid], axis=0)
        turned.append(jnp.transpose(stacked)[start:stop, :])
    turned = jnp.concatenate(turned, axis=0).astype(BF)
    g_all, lanes = plan.groups, plan.lanes
    for g0, g1 in pairs(g_all):
        for k, dst, less in ((0, va, CENTER), (1, vd, 0.0)):
            cols = slice((k * g_all + g0) * lanes, (k * g_all + g1) * lanes)
            both = dot(turned, vspread[:, cols]) - less
            for g in range(g0, g1):
                dst[g] = both[:, (g - g0) * lanes : (g - g0 + 1) * lanes]


def local_terms(coef, get, count, va, vd, v0):
    items = [get(g) for g in range(va.shape[0])]
    out = fold_mix(coef, items)
    for g, own in enumerate(items):
        out[g] = out[g] + va[g, v0 : v0 + count, :] * own + vd[g, v0 : v0 + count, :] * swap(own)
    return out


def strip_kernel(plan, orb_far, pot_far, slo, shi, ylo, yhi, vt, low, high, pot, sem):
    c, lanes, face, strip, w = plan.cells, plan.lanes, plan.face, plan.strip, plan.width
    copies = [
        pltpu.make_async_copy(pot_far, pot, sem.at[0]),
        pltpu.make_async_copy(orb_far.at[:, :strip], low, sem.at[1]),
        pltpu.make_async_copy(orb_far.at[:, face - strip :], high, sem.at[2]),
    ]
    for copy in copies:
        copy.start()
    copies[0].wait()
    v = jnp.concatenate([pot[pl.ds(y, c, stride=c), :] for y in range(c)], axis=1)
    vt[...] = v
    base = BUF * strip
    for out, first in ((slo, 0), (shi, c - BUF)):
        out[base:, :] = jnp.zeros((8, lanes), F32)
        for part in range(2):
            out[base + part * BUF : base + (part + 1) * BUF, :] = v[first : first + BUF, part * lanes : (part + 1) * lanes]
    ybase = plan.inner * strip
    ylo[ybase:, :] = v[:, :lanes]
    yhi[ybase:, :] = v[:, face - lanes :]
    copies[1].wait()
    copies[2].wait()
    for out, part in ((ylo, low), (yhi, high)):
        for j in range(plan.inner):
            a, b = part[j], part[c - 1 - j]
            out[j * strip : (j + 1) * strip, :] = jnp.concatenate([a + b, a - b], axis=1)
    for k in range(BUF):
        rows = slice(k * strip, (k + 1) * strip)
        slo[rows, :] = jnp.concatenate([low[k], high[k]], axis=1)
        shi[rows, :] = jnp.concatenate([low[c - BUF + k], high[c - BUF + k]], axis=1)


def pack_kernel(plan, orb, rlo, rhi, inner):
    c, strip, face = plan.cells, plan.strip, plan.face
    half, rest = face // 2, face // 2 - plan.strip
    for k in range(BUF):
        rows = slice(k * rest, (k + 1) * rest)
        for out, x in ((rlo, k), (rhi, c - BUF + k)):
            out[rows, :] = jnp.concatenate([orb[x, strip:half], orb[x, half : face - strip]], axis=1)
    for j in range(plan.inner):
        a, b = orb[j], orb[c - 1 - j]
        inner[j] = jnp.concatenate([a + b, a - b], axis=1)


def mirror(a, b):
    mask = low_lanes(a.shape)
    s, d = a + b, a - b
    return jnp.where(mask, s, swap(d)), jnp.where(mask, swap(s), d)


def edge_kernel(plan, vt, lo, hi, ahead, elo, ehi, vx):
    c, strip, lanes = plan.cells, plan.strip, plan.lanes
    for g in range(BUF):
        back = BUF - 1 - g
        top, bottom = mirror(lo[g * strip : (g + 1) * strip, :], hi[back * strip : (back + 1) * strip, :])
        elo[g * strip : (g + 1) * strip, :] = top
        ehi[g * strip : (g + 1) * strip, :] = bottom
    base = BUF * strip
    vx[...] = jnp.zeros(vx.shape, F32)
    vx[BUF : BUF + c, :] = vt[...]
    elo[base:, :] = jnp.zeros((8, lanes), F32)
    ehi[base:, :] = jnp.zeros((8, lanes), F32)
    for k, src in enumerate((lo, hi)):
        elo[base + k * BUF : base + (k + 1) * BUF, :] = src[base : base + BUF, :]
        ehi[base + k * BUF : base + (k + 1) * BUF, :] = src[base + BUF : base + 2 * BUF, :]
        at = 0 if k == 0 else BUF + c
        vx[at : at + BUF, :lanes] = src[base : base + BUF, :]
        vx[at : at + BUF, lanes:] = src[base + BUF : base + 2 * BUF, :]


def xhalo_kernel(plan, paired, inner, vx, elo, ehi, lo, hi, zpick, ahead, outer, zi):
    c, face, strip = plan.cells, plan.face, plan.strip
    half, rest = face // 2, face // 2 - strip
    for g in range(BUF):
        back = BUF - 1 - g
        top, bottom = mirror(lo[g * rest : (g + 1) * rest, :], hi[back * rest : (back + 1) * rest, :])
        outer[g, :strip] = elo[g * strip : (g + 1) * strip, :]
        outer[g, strip:half] = top
        outer[g, half : face - strip] = bottom
        outer[g, face - strip :] = ehi[g * strip : (g + 1) * strip, :]
    for side, dst in enumerate(sides(zi, paired)):
        start = side * (c - BUF)
        for g in range(plan.groups):
            src = outer.at[g] if g < BUF else inner.at[g - BUF]
            for k in range(BUF):
                at = g * strip + k * c
                dst[at : at + c, :] = src[pl.ds(start + k, c, stride=c), :]
        dst[plan.groups * strip :, :] = exact(vx[...], zpick[side])


def inside_kernel(plan, vx, vspread, va, vd, order):
    order[...] = jnp.zeros(order.shape, F32)
    spread_potential(plan, [(vx[...], 0, plan.face)], vspread, va, vd)


def outside_kernel(plan, inner, outer, coef, va, vd, acc, order, sh, sl):
    order[...] = jnp.zeros(order.shape, F32)
    lanes = plan.lanes

    def get(g, r0, r1):
        return outer[g, r0:r1, :] if g < BUF else inner[g - BUF, r0:r1, :]

    for g in range(plan.groups):
        put = functools.partial(put_folded, sh, sl, plan.lot)
        cols = slice(g * lanes, (g + 1) * lanes)
        fold_inside(plan, lambda r, n: get(g, r, r + n), lambda at, a, b: put(at, cols, a, b))
    for r0, r1 in chunks(plan.face):
        local = local_terms(coef, lambda g: get(g, r0, r1), r1 - r0, va, vd, r0)
        for g in range(plan.groups):
            acc[g, r0:r1, :] = local[g]


def ypack_kernel(plan, paired, ylo, yhi, elo, ehi, zpick, order, yh, vy, zc):
    c, lanes, strip, corner = plan.cells, plan.lanes, plan.strip, plan.corner
    last = yh.shape[1] - strip
    for g in range(plan.groups):
        lo, hi, at = (elo, ehi, g * strip) if g < BUF else (ylo, yhi, (g - BUF) * strip)
        yh[g, :strip] = lo[at : at + strip, :]
        yh[g, last:] = hi[at : at + strip, :]
    yh[:, strip:last] = jnp.zeros((plan.groups, last - strip, lanes), F32)
    ebase, ybase = BUF * strip, plan.inner * strip
    shift_in = lanes - strip
    vy[...] = jnp.zeros(vy.shape, F32)
    for e, y, cut, at in ((elo, ylo, shift_in, 0), (ehi, yhi, 0, last)):
        cols = slice(at, at + strip)
        vy[:BUF, cols] = e[ebase : ebase + BUF, :][:, cut : cut + strip]
        vy[BUF + c : plan.ext, cols] = e[ebase + BUF : ebase + 2 * BUF, :][:, cut : cut + strip]
        vy[BUF : BUF + c, cols] = y[ybase:, :][:, cut : cut + strip]
    for side, dst in enumerate(sides(zc, paired)):
        start = side * (c - BUF)
        for g in range(plan.groups):
            for k in range(BUF):
                at = (g * BUF + k) * corner
                dst[at : at + corner, :] = yh[g, pl.ds(start + k, corner, stride=c), :]
        dst[plan.groups * BUF * corner :, :] = exact(vy[...], zpick[side])


def halo_kernel(plan, paired, yh, vy, zi, coef, vspread, given, sh_in, sl_in, acc, sh, sl, xr, va, vd):
    g_all, lanes, strip, face = plan.groups, plan.lanes, plan.strip, plan.face
    last = yh.shape[1] - strip
    zlo, zhi = sides(zi, paired)[::-1] if paired else zi
    pots = [(vy[...], 0, strip), (vy[...], last, last + strip)]
    spread_potential(plan, pots + [(piece[g_all * strip :, :], 0, strip) for piece in (zlo, zhi)], vspread, va, vd)
    for g in range(g_all):
        xr[g, :strip, :] = yh[g, :strip, :]
        xr[g, strip : 2 * strip, :] = yh[g, last:, :]
        for k, piece in enumerate((zlo, zhi)):
            xr[g, (2 + k) * strip : (3 + k) * strip, :] = piece[g * strip : (g + 1) * strip, :]
    for g in range(g_all):
        cols = slice(g * lanes, (g + 1) * lanes)
        put = lambda at, a, b: put_folded(sh, sl, plan.lot, at, cols, a, b)
        fold_halo(plan, lambda r, n: xr[g, r : r + n, :], put)
    for r0, r1 in chunks(4 * strip):
        local = local_terms(coef, lambda g: xr[g, r0:r1, :], r1 - r0, va, vd, r0)
        for g in range(g_all):
            acc[g, face + r0 : face + r1, :] = local[g]


def filter_kernel(plan, paired, zc, inner, outer, xr, vai, vdi, vah, vdh, given, sh_in, sl_in, w1h, w1l, w2h, w2l, coef, dcoef,
                  vspread, out, mx, my, mz, sh, sl, xc, y, th, tl, va, vd, acc):
    g_all, lanes, rows, face, cross, c = plan.groups, plan.lanes, plan.rows, plan.face, plan.cross, plan.cells
    strip, lot, corner = plan.strip, plan.lot, plan.corner
    span = BUF * corner
    mz = sides(mz, paired)
    zlo, zhi = sides(zc, paired)[::-1] if paired else zc
    spread_potential(plan, [(piece[g_all * span :, :], 0, span) for piece in (zlo, zhi)], vspread, va, vd)
    for g in range(g_all):
        cols = slice(g * lanes, (g + 1) * lanes)
        for k, piece in enumerate((zlo, zhi)):
            xc[g, k * span : (k + 1) * span, :] = piece[g * span : (g + 1) * span, :]
        put = lambda at, a, b: put_folded(sh, sl, lot, at, cols, a, b)
        fold_corners([xc[g, k * 2 * corner : (k + 1) * 2 * corner, :] for k in range(BUF)], put, cross // 2)

    for r0, r1 in chunks(2 * span):
        local = local_terms(coef, lambda g: xc[g, r0:r1, :], r1 - r0, va, vd, r0)
        for g in range(g_all):
            y[g, cross + r0 : cross + r1, :] = local[g]
    for n, (g0, g1) in enumerate(pairs(g_all)):
        cols = slice(g0 * lanes, g1 * lanes)
        for p in range(2):
            own = slice(p * lot, (p + 1) * lot)
            acc[n % 2, own, : (g1 - g0) * lanes] = three(w1h[p], w1l[p], sh[own, cols], sl[own, cols])
        for g in range(g0, g1):
            mine = slice((g - g0) * lanes, (g - g0 + 1) * lanes)
            to = slice(g * lanes, (g + 1) * lanes)
            put = lambda at, a, b: put_folded(th, tl, lot, at, to, a, b)
            product = unfold(plan, lambda at, k: acc[n % 2, at : at + k, mine], lambda at, k: acc[n % 2, lot + at : lot + at + k, mine], True)
            for again, at, blocks in product:
                values = []
                for r0, block in blocks:
                    local = given[g, r0 : r0 + 16, :] if r0 < cross else y[g, r0 : r0 + 16, :]
                    values.append((local + block) * (S0 / HALF_WIDTH))
                    y[g, r0 : r0 + 16, :] = values[-1]
                again(values, put, at)

    for r0, r1 in chunks(cross):
        v, d, at = (vai, vdi, r0) if r0 < face else (vah, vdh, r0 - face)
        local = local_terms(coef, lambda g: y[g, r0:r1, :], r1 - r0, v, d, at)
        for g in range(g_all):
            if g >= BUF or r0 < face:
                if r0 >= face:
                    x = xr[g, r0 - face : r1 - face, :]
                else:
                    x = outer[g, r0:r1, :] if g < BUF else inner[g - BUF, r0:r1, :]
                out[g, r0:r1, :] = local[g] * (2.0 * S1 / HALF_WIDTH) - (S0 * S1) * x
    flat = plan.flat
    for n, (g0, g1) in enumerate(pairs(g_all)):
        cols = slice(g0 * lanes, g1 * lanes)
        for p in range(2):
            own = slice(p * lot, (p + 1) * lot)
            acc[n % 2, p * lot : p * lot + flat, : (g1 - g0) * lanes] = three(w2h[p], w2l[p], th[own, cols], tl[own, cols])
        for g in range(g0, g1):
            mine = slice((g - g0) * lanes, (g - g0 + 1) * lanes)
            product = unfold(plan, lambda at, k: acc[n % 2, at : at + k, mine], lambda at, k: acc[n % 2, lot + at : lot + at + k, mine], False)
            for _, _, blocks in product:
                for r0, block in blocks:
                    if r0 < face or g >= BUF:
                        out[g, r0 : r0 + 16, :] = out[g, r0 : r0 + 16, :] + block

    for r0, r1 in chunks(face):
        mask = low_lanes((r1 - r0, lanes))
        e = out[BUF, r0:r1, :]
        d = mix(dcoef, 0, [out[g, r0:r1, :] for g in range(g_all)])
        te, td = swap(e), swap(d)
        mx[0][r0:r1, :] = 0.5 * jnp.where(mask, e + te, d + td)
        mx[1][r0:r1, :] = 0.5 * jnp.where(mask, e - te, d - td)
    part = plan.inner * c
    order = list(range(BUF, BUF + c)) + list(range(BUF)) + list(range(BUF + c, plan.ext))
    mask = low_lanes((c, lanes))
    for j in range(plan.inner):
        g = BUF + j
        ylayers = [out[g, k * c : (k + 1) * c, :] for k in range(plan.ext)]
        zlayers = [out[g, pl.ds(k, c, stride=c), :] for k in range(c)]
        zlayers += [out[g, plan.yext + k * c : plan.yext + (k + 1) * c, :] for k in range(2 * BUF)]
        for layers, message in ((ylayers, my), (zlayers, mz)):
            for side, layer in enumerate((0, c - 1)):
                total = None
                for k, t in enumerate(order):
                    weight = float(plan.first[BUF + layer, t])
                    if t != BUF + layer:
                        term = weight * layers[k]
                        total = term if total is None else total + term
                value = layers[layer]
                message[side][j * c : (j + 1) * c, :] = jnp.where(mask, value, swap(total))
                message[side][part + j * c : part + (j + 1) * c, :] = jnp.where(mask, swap(value), total)


def own_kernel(plan, f, va, vd, bh, bl, coef, diag, basis, local, f2, f2h, f2l, fhi, acc, sem):
    g_all, lanes, face, cross, c = plan.groups, plan.lanes, plan.face, plan.cross, plan.cells
    copies = []
    for j in range(plan.inner):
        for r0, r1 in chunks(face, 64):
            e = f[BUF + j, r0:r1, :]
            t = swap(e)
            local[j, r0:r1, :] = (0.5 * (e + t))[:, : plan.width]
            local[c - 1 - j, r0:r1, :] = (0.5 * (e - t))[:, : plan.width]
        for x in (j, c - 1 - j):
            copies.append(pltpu.make_async_copy(local.at[x], basis.at[x], sem.at[x]))
            copies[-1].start()
    for g in range(g_all):
        top = face if g < BUF else cross
        for r0, r1 in chunks(top):
            value = f[g, r0:r1, :]
            high = value.astype(BF)
            fhi[g, r0:r1, :] = high
            f2[g, r0:r1, :] = 2.0 * value - high.astype(F32)
        if g >= BUF:
            to = slice((g - BUF) * lanes, (g - BUF + 1) * lanes)
            put = lambda at, a, b: put_folded(f2h, f2l, plan.flat, at, to, a, b)
            fold_inside(plan, lambda r, n: f2[g, r : r + n, :], put)
            fold_halo(plan, lambda r, n: f2[g, face + r : face + r + n, :], put)
    total = jnp.zeros((lanes, 2 * lanes), F32)

    def fold(total, g, top, value):
        h, l = split(value)
        return total + dot_t(fhi[g, :top, :], jnp.concatenate([h, l], axis=1))

    def mixed(g, r0, r1):
        return mix(coef, g * g_all, [f2[s, r0:r1, :] for s in range(g_all)])

    for g in range(BUF):
        total = fold(total, g, face, jnp.concatenate([mixed(g, r0, r1) for r0, r1 in chunks(face)], axis=0))
    for n, (j0, j1) in enumerate(pairs(plan.inner)):
        slot = n % 2
        cols = slice(j0 * lanes, j1 * lanes)
        for p in range(2):
            half = slice(p * plan.flat, (p + 1) * plan.flat)
            acc[slot, half] = three(bh[p], bl[p], f2h[half, cols], f2l[half, cols])
        for j in range(j0, j1):
            g = BUF + j
            mine = slice((j - j0) * lanes, (j - j0 + 1) * lanes)
            flat = plan.flat
            product = unfold(plan, lambda at, k: acc[slot, at : at + k, mine], lambda at, k: acc[slot, flat + at : flat + at + k, mine], False)
            product = {r0: block for _, _, blocks in product for r0, block in blocks}
            parts = []
            for r0, r1 in chunks(face):
                own = f2[g, r0:r1, :]
                value = product[r0] + mixed(g, r0, r1)
                parts.append(value + (va[g, r0:r1, :] + CENTER) * own + vd[g, r0:r1, :] * swap(own))
            parts += [product[r0] for r0 in range(face, cross, 16)]
            total = fold(total, g, cross, jnp.concatenate(parts, axis=0))
    both = total[:, :lanes] + total[:, lanes:]
    w = plan.width
    block = both[:w, :w] + both[w:, w:]
    diag[...] = 0.25 * (block + jnp.transpose(block))
    for copy in copies:
        copy.wait()


def face_block(plan, own, other, sign, scale):
    w, lanes = plan.width, plan.lanes
    ah, al = split(own[...])
    bh, bl = split(other[...])
    first = dot_t(ah, jnp.concatenate([bh, bl], axis=1))
    m = first[:, :lanes] + first[:, lanes:] + dot_t(al, bh)
    return scale * (0.25 * sign * (m[w:, :w] - m[:w, w:]) - 0.5 * PENALTY * m[:w, :w])


def yzface_kernel(plan, paired, oy, oz, ny, nz, blocks):
    oz, nz = sides(oz, paired), sides(nz, paired)[::-1] if paired else nz
    for k, (own, other) in enumerate(((oy[0], ny[0]), (oy[1], ny[1]), (oz[0], nz[0]), (oz[1], nz[1]))):
        blocks[k] = face_block(plan, own, other, -1.0 if k % 2 == 0 else 1.0, 0.5)


def xface_kernel(plan, diag, yz, ox, nx, blocks, local, sem):
    copies = [
        pltpu.make_async_copy(diag, blocks.at[0], sem.at[0]),
        pltpu.make_async_copy(yz, blocks.at[3:7], sem.at[1]),
        pltpu.make_async_copy(local, blocks.at[1:3], sem.at[2]),
    ]
    copies[0].start()
    copies[1].start()
    for k in range(2):
        local[k] = face_block(plan, ox[k], nx[k], -1.0 if k == 0 else 1.0, 1.0)
    copies[2].start()
    for copy in copies:
        copy.wait()


def near(*shape):
    return pltpu.VMEM(shape, F32)


def far(*shape):
    return jax.ShapeDtypeStruct(shape, F32)


def call(kernel, outs, args, scratch=(), flops=0, limit=24, aliases=None, far_in=(), far_out=()):
    def place(a, where):
        return pltpu.with_memory_space_constraint(jnp.asarray(a), where)

    placed = [jax.tree.map(lambda b: place(b, pltpu.HBM if i in far_in else pltpu.VMEM), a) for i, a in enumerate(args)]
    space, apart = pl.BlockSpec(memory_space=pltpu.VMEM), pl.BlockSpec(memory_space=pl.ANY)
    return pl.pallas_call(
        kernel,
        out_shape=outs,
        in_specs=[apart if i in far_in else jax.tree.map(lambda b: space, a) for i, a in enumerate(placed)],
        out_specs=[apart if i in far_out else jax.tree.map(lambda b: space, a) for i, a in enumerate(outs)],
        scratch_shapes=list(scratch),
        input_output_aliases=aliases or {},
        compiler_params=pltpu.CompilerParams(vmem_limit_bytes=limit * 1024 * 1024),
        cost_estimate=pl.CostEstimate(flops=flops, bytes_accessed=0, transcendentals=0),
    )(*placed)


def shift(array, axis, step):
    count = lax.axis_size(axis)
    return lax.ppermute(array, axis, [(i, (i + step) % count) for i in range(count)])


def shift_z(both, paired):
    if paired:
        return shift(both, "gz", 1)
    return [shift(both[1], "gz", 1), shift(both[0], "gz", -1)]


def on_device(orbitals, potential):
    cells, width = orbitals.shape[0], orbitals.shape[-1]
    plan = Plan(cells, width)
    lanes, face, strip, rows, cross = plan.lanes, plan.face, plan.strip, plan.rows, plan.cross
    g_all, inner_all, corner = plan.groups, plan.inner, plan.corner
    paired = lax.axis_size("gz") == 2
    part = functools.partial
    bf = lambda *shape: pltpu.VMEM(shape, BF)
    wide = g_all * lanes

    def two(*shape):
        return near(2, *shape) if paired else [near(*shape), near(*shape)]

    srows, rrows, yrows = BUF * strip + 8, BUF * (face // 2 - strip), inner_all * strip + cells
    orb = orbitals.reshape(cells, face, width)
    slo, shi, ylo, yhi, vt = call(
        part(strip_kernel, plan),
        [near(srows, lanes), near(srows, lanes), near(yrows, lanes), near(yrows, lanes), near(cells, face)],
        [orb, potential.reshape(face, cells)],
        [near(cells, strip, width), near(cells, strip, width), near(face, cells), pltpu.SemaphoreType.DMA((3,))],
        far_in=(0, 1),
    )
    from_ylo, from_yhi = shift(yhi, "gy", 1), shift(ylo, "gy", -1)
    from_slo, from_shi = shift(shi, "gx", 1), shift(slo, "gx", -1)
    rlo, rhi, inner = call(
        part(pack_kernel, plan), [near(rrows, lanes), near(rrows, lanes), near(inner_all, face, lanes)], [orb],
    )
    from_rlo, from_rhi = shift(rhi, "gx", 1), shift(rlo, "gx", -1)

    ipick = np.zeros((2, face, lanes), np.float32)
    cpick = np.zeros((2, lanes, lanes), np.float32)
    for side in range(2):
        for k in range(BUF):
            z = side * (cells - BUF) + k
            for y in range(cells):
                ipick[side, y * cells + z, k * cells + y] = 1.0
            for y in range(corner):
                cpick[side, y * cells + z, k * corner + y] = 1.0
    elo, ehi, vx = call(
        part(edge_kernel, plan), [near(srows, lanes), near(srows, lanes), near(plan.trows, face)], [vt, from_slo, from_shi, from_ylo],
        flops=2*10**9,
    )
    from_elo, from_ehi = shift(ehi, "gy", 1), shift(elo, "gy", -1)

    matrix = -0.5 * row_matrix(plan, plan.second, False)
    coef = folded(-0.5 * mirrored(plan, plan.second))
    vspread = np.zeros((plan.trows, 2, g_all, lanes), np.float32)
    for g in range(g_all):
        vspread[g, :, g, :] = 0.5
        vspread[plan.ext - 1 - g, 0, g, :] = 0.5
        vspread[plan.ext - 1 - g, 1, g, :] = -0.5
    vspread = np.tile(vspread.reshape(plan.trows, -1), (3, 1)).astype(ml_dtypes.bfloat16)
    vai, vdi, early = call(
        part(inside_kernel, plan), [near(g_all, face, lanes), near(g_all, face, lanes), near(8, lanes)], [vx, vspread],
    )
    outer, zi = call(
        part(xhalo_kernel, plan, paired),
        [near(BUF, face, lanes), two(g_all * strip + plan.trows, lanes)],
        [inner, vx, elo, ehi, from_rlo, from_rhi, ipick, early],
    )
    zi = shift_z(zi, paired)
    both = pltpu.VMEM((2 * plan.lot, wide), BF)
    acc, order, sh, sl = call(
        part(outside_kernel, plan), [near(g_all, cross, lanes), near(8, lanes), both, both], [inner, outer, coef, vai, vdi],
    )

    room = 2 * strip + (corner - 2 * BUF) * cells
    yh, vy, zc = call(
        part(ypack_kernel, plan, paired),
        [near(g_all, room, lanes), near(plan.trows, lanes), two(g_all * BUF * corner + plan.trows, lanes)],
        [from_ylo, from_yhi, from_elo, from_ehi, cpick, order],
        flops=10**10,
    )
    zc = shift_z(zc, paired)
    rest = 4 * strip
    base = 5 if paired else 6
    acc, sh, sl, xr, vah, vdh = call(
        part(halo_kernel, plan, paired),
        [near(g_all, cross, lanes), both, both, near(g_all, rest, lanes), near(g_all, rest, lanes), near(g_all, rest, lanes)],
        [yh, vy, zi, coef, vspread, acc, sh, sl],
        aliases={base: 0, base + 1: 1, base + 2: 2},
    )

    p = plan.first[BUF, :g_all] + plan.first[BUF, ::-1][:g_all]
    q = plan.first[BUF, :g_all] - plan.first[BUF, ::-1][:g_all]
    dcoef = np.concatenate([np.repeat(p[:, None], width, 1), np.repeat(q[:, None], width, 1)], 1).astype(np.float32)
    msg = near(face, lanes)
    corners = 2 * BUF * corner
    product = folded_rows(plan, matrix)
    second = 2.0 * S1 / HALF_WIDTH * product[:, : plan.flat]
    base = 9 if paired else 10
    filtered, mx, my, mz, _, _ = call(
        part(filter_kernel, plan, paired),
        [near(g_all, cross, lanes), [msg, msg], [msg, msg], two(face, lanes), both, both],
        [zc, inner, outer, xr, vai, vdi, vah, vdh, acc, sh, sl, *halves(product), *halves(second), coef, dcoef, vspread],
        [near(g_all, corners, lanes), near(g_all, rows, lanes), both, both,
         near(g_all, corners, lanes), near(g_all, corners, lanes), near(2, 2 * plan.lot, 2 * lanes)],
        aliases={base: 6 if paired else 7, base + 1: 7 if paired else 8},
    )
    ny = [shift(my[1], "gy", 1), shift(my[0], "gy", -1)]
    nx = [shift(mx[1], "gx", 1), shift(mx[0], "gx", -1)]
    nz = shift_z(mz, paired)

    along = energy(plan)
    bcoef = mirrored(plan, along).reshape(-1, lanes).astype(np.float32)
    diag, basis = call(
        part(own_kernel, plan), [near(width, width), far(cells, face, width)],
        [filtered, vai, vdi, *halves(folded_rows(plan, row_matrix(plan, along, True))[:, : plan.flat, : plan.flat]), bcoef],
        [near(cells, face, width), near(g_all, cross, lanes), bf(cross, inner_all * lanes), bf(cross, inner_all * lanes), bf(g_all, cross, lanes),
         near(2, cross, 2 * lanes), pltpu.SemaphoreType.DMA((cells,))],
        flops=2 * 10**9,
        far_out=(1,),
    )
    (yz,) = call(part(yzface_kernel, plan, paired), [near(4, width, width)], [my, mz, ny, nz])
    (blocks,) = call(
        part(xface_kernel, plan), [far(7, width, width)], [diag, yz, mx, nx],
        [near(2, width, width), pltpu.SemaphoreType.DMA((3,))], far_out=(0,),
    )
    return basis.reshape(orbitals.shape), blocks[None, None, None]


def solution(mesh):
    return jax.shard_map(
        on_device,
        mesh=mesh,
        in_specs=(P("gx", "gy", "gz", None), P("gx", "gy", "gz")),
        out_specs=(P("gx", "gy", "gz", None), P("gx", "gy", "gz", None, None, None)),
        check_vma=False,
    )
```

```python
import functools

import jax
import jax.numpy as jnp
import ml_dtypes
import numpy as np
from jax import lax
from jax.experimental import pallas as pl
from jax.experimental.pallas import tpu as pltpu
from jax.sharding import PartitionSpec as P

BUF = 3
PENALTY = 2.0
LOW_BOUND = -1.5
CUTOFF = 8.0
HIGH_BOUND = 16.0
BF = jnp.bfloat16
F32 = jnp.float32


class Plan:
    def __init__(self, cells, width):
        self.cells, self.width = cells, width
        self.ext = cells + 2 * BUF
        self.groups = self.ext // 2
        self.inner = cells // 2
        self.lanes = 2 * width
        self.face = cells * cells
        self.strip = BUF * cells
        self.corner = -(-2 * BUF // 8) * 8
        self.yext = self.face + 2 * self.strip
        self.cross = self.yext + 2 * self.strip
        self.rows = self.cross + 2 * BUF * self.corner
        self.trows = -(-self.ext // 8) * 8
        inside = list(range(BUF, BUF + cells))
        outside = list(range(BUF)) + list(range(BUF + cells, self.ext))
        points = [(y, z) for y in inside for z in inside] + [(y, z) for y in outside for z in inside]
        points += [(y, z) for z in outside for y in inside]
        gap = self.corner - 2 * BUF
        for z in outside:
            points += [(y, z) for y in outside[:BUF]] + [None] * gap + [(y, z) for y in outside[BUF:]]
        self.fold = self.rows // 2
        self.flat = self.cross // 2
        self.lot = -(-self.fold // 16) * 16
        self.points = points
        self.first, self.second = spectral(self.ext)
        self.inside = np.isin(np.arange(self.ext), inside)


def spectral(points):
    indices = np.arange(points)
    offsets = indices[:, None] - indices[None, :]
    first = np.zeros((points, points))
    second = np.zeros((points, points))
    for harmonic in range(1, points // 2):
        wavenum = 2.0 * np.pi * harmonic / points
        first = first - 2.0 * wavenum * np.sin(wavenum * offsets) / points
        second = second - 2.0 * wavenum * wavenum * np.cos(wavenum * offsets) / points
    second = second - np.pi * np.pi * np.cos(np.pi * offsets) / points
    return first, second


def row_matrix(plan, along, masked):
    real = np.array([p is not None for p in plan.points])
    y, z = np.array([(0, 0) if p is None else p for p in plan.points]).T
    by_y = along[y[:, None], y[None, :]] * (z[:, None] == z[None, :])
    by_z = along[z[:, None], z[None, :]] * (y[:, None] == y[None, :])
    if masked:
        by_y, by_z = by_y * plan.inside[z][:, None], by_z * plan.inside[y][:, None]
    return (by_y + by_z) * real[:, None] * real[None, :]


def mirror_basis(plan):
    c, face, strip = plan.cells, plan.face, plan.strip
    kept = [(y * c + z, (c - 1 - y) * c + z) for y in range(c // 2) for z in range(c)]
    kept += [(face + k * c + z, face + (2 * BUF - 1 - k) * c + z) for k in range(BUF) for z in range(c)]
    kept += [(plan.yext + k * c + y, plan.yext + k * c + c - 1 - y) for k in range(2 * BUF) for y in range(c // 2)]
    for m in range(BUF):
        for r in range(plan.corner):
            at = plan.cross + (2 * m + (r >= plan.corner // 2)) * plan.corner
            kept.append((at + r, at + plan.corner - 1 - r))
    out = np.zeros((2, plan.lot, plan.rows))
    for i, (a, b) in enumerate(kept):
        out[:, i, a] += 1.0
        out[0, i, b] += 1.0
        out[1, i, b] -= 1.0
    return out


def folded_rows(plan, matrix):
    basis = mirror_basis(plan)
    return 0.25 * np.einsum("pia,ab,pjb->pij", basis, matrix, basis, optimize=True)


def mirrored(plan, along):
    g = plan.groups
    plus = along[:g, :g] + along[:g, ::-1][:, :g]
    minus = along[:g, :g] - along[:g, ::-1][:, :g]
    return np.concatenate([np.repeat(plus[:, :, None], plan.width, 2), np.repeat(minus[:, :, None], plan.width, 2)], 2)


def folded(table):
    g = table.shape[0]
    half, odd = g // 2, g % 2
    out = []
    for t in range(half + odd):
        out += [0.5 * (table[t, s] + table[t, g - 1 - s]) for s in range(half)] + [table[t, half]] * odd
        if t < half:
            out += [0.5 * (table[t, s] - table[t, g - 1 - s]) for s in range(half)]
    return np.stack(out).astype(np.float32)


def energy(plan):
    c = plan.cells
    block = plan.first[BUF : BUF + c]
    out = 0.5 * block.T @ block
    for sign, layer in ((-1.0, BUF), (1.0, BUF + c - 1)):
        unit = np.zeros(plan.ext)
        unit[layer] = 1.0
        cross = np.outer(unit, plan.first[layer])
        out = out + 0.5 * PENALTY * np.outer(unit, unit) - 0.25 * sign * (cross + cross.T)
    return out


def halves(matrix):
    high = matrix.astype(np.float32).astype(ml_dtypes.bfloat16)
    low = (matrix - high.astype(np.float64)).astype(np.float32).astype(ml_dtypes.bfloat16)
    return high, low


def split(x):
    high = x.astype(BF)
    return high, (x - high.astype(F32)).astype(BF)


def swap(x):
    return pltpu.roll(x, x.shape[-1] // 2, x.ndim - 1)


def dot(a, b):
    return jnp.dot(a, b, preferred_element_type=F32)


def dot_t(a, b):
    return lax.dot_general(a, b, (((0,), (0,)), ((), ())), preferred_element_type=F32)


def exact(a, b):
    return jnp.dot(a, b, preferred_element_type=F32, precision=lax.Precision.HIGHEST)


def three(wh, wl, sh, sl):
    return dot(wh, sh) + dot(wl, sh) + dot(wh, sl)


def flip(x):
    row = lax.broadcasted_iota(jnp.int32, x.shape, 0)
    x = pltpu.roll(x, 4, 0)
    x = jnp.where(lax.rem(row, 4) < 2, pltpu.roll(x, 6, 0), pltpu.roll(x, 2, 0))
    return jnp.where(lax.rem(row, 2) < 1, pltpu.roll(x, 7, 0), pltpu.roll(x, 1, 0))


def put_folded(sh, sl, lot, at, cols, plus, minus):
    for p, value in enumerate((plus, minus)):
        h, l = split(value)
        sh[p * lot + at : p * lot + at + value.shape[0], cols] = h
        sl[p * lot + at : p * lot + at + value.shape[0], cols] = l


def fold_blocks(blocks, put, at):
    a, b = blocks
    put(at, a + b, a - b)


def fold_planes(blocks, put, at):
    firsts, lasts = [p[:8] for p in blocks], [flip(p[8:]) for p in blocks]
    put(at, jnp.concatenate([a + b for a, b in zip(firsts, lasts)], axis=0),
        jnp.concatenate([a - b for a, b in zip(firsts, lasts)], axis=0))


def fold_corners(blocks, put, at):
    plus, minus = [], []
    for block in blocks:
        a, b = block[:8], block[8:]
        fa, fb = flip(a), flip(b)
        first = lax.broadcasted_iota(jnp.int32, a.shape, 0) < 4
        plus.append(jnp.where(first, a + fa, b + fb))
        minus.append(jnp.where(first, a - fa, b - fb))
    zero = jnp.zeros_like(plus[0])
    put(at, jnp.concatenate(plus + [zero], axis=0), jnp.concatenate(minus + [zero], axis=0))


def fold_inside(plan, get, put):
    c = plan.cells
    for y in range(c // 2):
        fold_blocks([get(y * c, c), get((c - 1 - y) * c, c)], put, y * c)


def fold_halo(plan, get, put):
    c = plan.cells
    for k in range(BUF):
        fold_blocks([get(k * c, c), get((2 * BUF - 1 - k) * c, c)], put, plan.face // 2 + k * c)
    at = 2 * plan.strip
    for k in range(0, 2 * BUF, 2):
        fold_planes([get(at + k * c, c), get(at + (k + 1) * c, c)], put, plan.yext // 2 + k * 8)


def unfold(plan, v0, v1, corners):
    c = plan.cells

    def both(at, n):
        a, b = v0(at, n), v1(at, n)
        return a + b, a - b

    for y in range(c // 2):
        a, b = both(y * c, c)
        yield fold_blocks, y * c, [(y * c, a), ((c - 1 - y) * c, b)]
    at = plan.face // 2
    for k in range(BUF):
        a, b = both(at + k * c, c)
        yield fold_blocks, at + k * c, [(plan.face + k * c, a), (plan.face + (2 * BUF - 1 - k) * c, b)]
    at = plan.yext // 2
    for k in range(0, 2 * BUF, 2):
        made = []
        for m in (k, k + 1):
            a, b = both(at + m * 8, 8)
            made.append((plan.yext + m * c, jnp.concatenate([a, flip(b)], axis=0)))
        yield fold_planes, at + k * 8, made
    if corners:
        at, made = plan.cross // 2, []
        for m in range(BUF):
            a, b = both(at + m * 8, 8)
            first = lax.broadcasted_iota(jnp.int32, a.shape, 0) < 4
            b = flip(b)
            made.append((plan.cross + m * 16, jnp.concatenate([jnp.where(first, a, b), jnp.where(first, b, a)], axis=0)))
        yield fold_corners, at, made


def low_lanes(shape):
    return lax.broadcasted_iota(jnp.int32, shape, len(shape) - 1) < shape[-1] // 2


def sides(ref, paired):
    return [ref.at[0], ref.at[1]] if paired else ref


def chunks(stop, size=16, start=0):
    return [(r, min(r + size, stop)) for r in range(start, stop, size)]


def pairs(stop, start=0):
    return [(g, min(g + 2, stop)) for g in range(start, stop, 2)]


CENTER = (HIGH_BOUND + CUTOFF) / 2.0
HALF_WIDTH = (HIGH_BOUND - CUTOFF) / 2.0
S0 = HALF_WIDTH / (LOW_BOUND - CENTER)
S1 = 1.0 / (2.0 / S0 - S0)


def mix(coef, table, items):
    total = None
    for s, item in enumerate(items):
        term = coef[table + s : table + s + 1, :] * item
        total = term if total is None else total + term
    return total


def fold_mix(coef, items):
    g = len(items)
    half, odd = g // 2, g % 2
    plus = [items[s] + items[g - 1 - s] for s in range(half)] + [items[half]] * odd
    minus = [items[s] - items[g - 1 - s] for s in range(half)]
    out, k = [None] * g, 0
    for t in range(half + odd):
        p = mix(coef, k, plus)
        k += len(plus)
        if t < half:
            q = mix(coef, k, minus)
            k += half
            out[t], out[g - 1 - t] = p + q, p - q
        else:
            out[t] = p
    return out


def spread_potential(plan, pieces, vspread, va, vd):
    turned = []
    for piece, start, stop in pieces:
        high = piece.astype(BF).astype(F32)
        rest = piece - high
        mid = rest.astype(BF).astype(F32)
        stacked = jnp.concatenate([high, mid, rest - mid], axis=0)
        turned.append(jnp.transpose(stacked)[start:stop, :])
    turned = jnp.concatenate(turned, axis=0).astype(BF)
    g_all, lanes = plan.groups, plan.lanes
    for g0, g1 in pairs(g_all):
        for k, dst, less in ((0, va, CENTER), (1, vd, 0.0)):
            cols = slice((k * g_all + g0) * lanes, (k * g_all + g1) * lanes)
            both = dot(turned, vspread[:, cols]) - less
            for g in range(g0, g1):
                dst[g] = both[:, (g - g0) * lanes : (g - g0 + 1) * lanes]


def local_terms(coef, get, count, va, vd, v0):
    items = [get(g) for g in range(va.shape[0])]
    out = fold_mix(coef, items)
    for g, own in enumerate(items):
        out[g] = out[g] + va[g, v0 : v0 + count, :] * own + vd[g, v0 : v0 + count, :] * swap(own)
    return out


def strip_kernel(plan, orb_far, pot_far, slo, shi, ylo, yhi, vt, low, high, pot, sem):
    c, lanes, face, strip, w = plan.cells, plan.lanes, plan.face, plan.strip, plan.width
    copies = [
        pltpu.make_async_copy(pot_far, pot, sem.at[0]),
        pltpu.make_async_copy(orb_far.at[:, :strip], low, sem.at[1]),
        pltpu.make_async_copy(orb_far.at[:, face - strip :], high, sem.at[2]),
    ]
    for copy in copies:
        copy.start()
    copies[0].wait()
    v = jnp.concatenate([pot[pl.ds(y, c, stride=c), :] for y in range(c)], axis=1)
    vt[...] = v
    base = BUF * strip
    for out, first in ((slo, 0), (shi, c - BUF)):
        out[base:, :] = jnp.zeros((8, lanes), F32)
        for part in range(2):
            out[base + part * BUF : base + (part + 1) * BUF, :] = v[first : first + BUF, part * lanes : (part + 1) * lanes]
    ybase = plan.inner * strip
    ylo[ybase:, :] = v[:, :lanes]
    yhi[ybase:, :] = v[:, face - lanes :]
    copies[1].wait()
    copies[2].wait()
    for out, part in ((ylo, low), (yhi, high)):
        for j in range(plan.inner):
            a, b = part[j], part[c - 1 - j]
            out[j * strip : (j + 1) * strip, :] = jnp.concatenate([a + b, a - b], axis=1)
    for k in range(BUF):
        rows = slice(k * strip, (k + 1) * strip)
        slo[rows, :] = jnp.concatenate([low[k], high[k]], axis=1)
        shi[rows, :] = jnp.concatenate([low[c - BUF + k], high[c - BUF + k]], axis=1)


def pack_kernel(plan, orb, rlo, rhi, inner):
    c, strip, face = plan.cells, plan.strip, plan.face
    half, rest = face // 2, face // 2 - plan.strip
    for k in range(BUF):
        rows = slice(k * rest, (k + 1) * rest)
        for out, x in ((rlo, k), (rhi, c - BUF + k)):
            out[rows, :] = jnp.concatenate([orb[x, strip:half], orb[x, half : face - strip]], axis=1)
    for j in range(plan.inner):
        a, b = orb[j], orb[c - 1 - j]
        inner[j] = jnp.concatenate([a + b, a - b], axis=1)


def mirror(a, b):
    mask = low_lanes(a.shape)
    s, d = a + b, a - b
    return jnp.where(mask, s, swap(d)), jnp.where(mask, swap(s), d)


def edge_kernel(plan, vt, lo, hi, ahead, elo, ehi, vx):
    c, strip, lanes = plan.cells, plan.strip, plan.lanes
    for g in range(BUF):
        back = BUF - 1 - g
        top, bottom = mirror(lo[g * strip : (g + 1) * strip, :], hi[back * strip : (back + 1) * strip, :])
        elo[g * strip : (g + 1) * strip, :] = top
        ehi[g * strip : (g + 1) * strip, :] = bottom
    base = BUF * strip
    vx[...] = jnp.zeros(vx.shape, F32)
    vx[BUF : BUF + c, :] = vt[...]
    elo[base:, :] = jnp.zeros((8, lanes), F32)
    ehi[base:, :] = jnp.zeros((8, lanes), F32)
    for k, src in enumerate((lo, hi)):
        elo[base + k * BUF : base + (k + 1) * BUF, :] = src[base : base + BUF, :]
        ehi[base + k * BUF : base + (k + 1) * BUF, :] = src[base + BUF : base + 2 * BUF, :]
        at = 0 if k == 0 else BUF + c
        vx[at : at + BUF, :lanes] = src[base : base + BUF, :]
        vx[at : at + BUF, lanes:] = src[base + BUF : base + 2 * BUF, :]


def xhalo_kernel(plan, paired, inner, vx, elo, ehi, lo, hi, zpick, ahead, outer, zi):
    c, face, strip = plan.cells, plan.face, plan.strip
    half, rest = face // 2, face // 2 - strip
    for g in range(BUF):
        back = BUF - 1 - g
        top, bottom = mirror(lo[g * rest : (g + 1) * rest, :], hi[back * rest : (back + 1) * rest, :])
        outer[g, :strip] = elo[g * strip : (g + 1) * strip, :]
        outer[g, strip:half] = top
        outer[g, half : face - strip] = bottom
        outer[g, face - strip :] = ehi[g * strip : (g + 1) * strip, :]
    for side, dst in enumerate(sides(zi, paired)):
        start = side * (c - BUF)
        for g in range(plan.groups):
            src = outer.at[g] if g < BUF else inner.at[g - BUF]
            for k in range(BUF):
                at = g * strip + k * c
                dst[at : at + c, :] = src[pl.ds(start + k, c, stride=c), :]
        dst[plan.groups * strip :, :] = exact(vx[...], zpick[side])


def inside_kernel(plan, vx, vspread, va, vd, order):
    order[...] = jnp.zeros(order.shape, F32)
    spread_potential(plan, [(vx[...], 0, plan.face)], vspread, va, vd)


def outside_kernel(plan, inner, outer, coef, va, vd, acc, order, sh, sl):
    order[...] = jnp.zeros(order.shape, F32)
    lanes = plan.lanes

    def get(g, r0, r1):
        return outer[g, r0:r1, :] if g < BUF else inner[g - BUF, r0:r1, :]

    for g in range(plan.groups):
        put = functools.partial(put_folded, sh, sl, plan.lot)
        cols = slice(g * lanes, (g + 1) * lanes)
        fold_inside(plan, lambda r, n: get(g, r, r + n), lambda at, a, b: put(at, cols, a, b))
    for r0, r1 in chunks(plan.face):
        local = local_terms(coef, lambda g: get(g, r0, r1), r1 - r0, va, vd, r0)
        for g in range(plan.groups):
            acc[g, r0:r1, :] = local[g]


def ypack_kernel(plan, paired, ylo, yhi, elo, ehi, zpick, order, yh, vy, zc):
    c, lanes, strip, corner = plan.cells, plan.lanes, plan.strip, plan.corner
    last = yh.shape[1] - strip
    for g in range(plan.groups):
        lo, hi, at = (elo, ehi, g * strip) if g < BUF else (ylo, yhi, (g - BUF) * strip)
        yh[g, :strip] = lo[at : at + strip, :]
        yh[g, last:] = hi[at : at + strip, :]
    yh[:, strip:last] = jnp.zeros((plan.groups, last - strip, lanes), F32)
    ebase, ybase = BUF * strip, plan.inner * strip
    shift_in = lanes - strip
    vy[...] = jnp.zeros(vy.shape, F32)
    for e, y, cut, at in ((elo, ylo, shift_in, 0), (ehi, yhi, 0, last)):
        cols = slice(at, at + strip)
        vy[:BUF, cols] = e[ebase : ebase + BUF, :][:, cut : cut + strip]
        vy[BUF + c : plan.ext, cols] = e[ebase + BUF : ebase + 2 * BUF, :][:, cut : cut + strip]
        vy[BUF : BUF + c, cols] = y[ybase:, :][:, cut : cut + strip]
    for side, dst in enumerate(sides(zc, paired)):
        start = side * (c - BUF)
        for g in range(plan.groups):
            for k in range(BUF):
                at = (g * BUF + k) * corner
                dst[at : at + corner, :] = yh[g, pl.ds(start + k, corner, stride=c), :]
        dst[plan.groups * BUF * corner :, :] = exact(vy[...], zpick[side])


def halo_kernel(plan, paired, yh, vy, zi, coef, vspread, given, sh_in, sl_in, acc, sh, sl, xr, va, vd):
    g_all, lanes, strip, face = plan.groups, plan.lanes, plan.strip, plan.face
    last = yh.shape[1] - strip
    zlo, zhi = sides(zi, paired)[::-1] if paired else zi
    pots = [(vy[...], 0, strip), (vy[...], last, last + strip)]
    spread_potential(plan, pots + [(piece[g_all * strip :, :], 0, strip) for piece in (zlo, zhi)], vspread, va, vd)
    for g in range(g_all):
        xr[g, :strip, :] = yh[g, :strip, :]
        xr[g, strip : 2 * strip, :] = yh[g, last:, :]
        for k, piece in enumerate((zlo, zhi)):
            xr[g, (2 + k) * strip : (3 + k) * strip, :] = piece[g * strip : (g + 1) * strip, :]
    for g in range(g_all):
        cols = slice(g * lanes, (g + 1) * lanes)
        put = lambda at, a, b: put_folded(sh, sl, plan.lot, at, cols, a, b)
        fold_halo(plan, lambda r, n: xr[g, r : r + n, :], put)
    for r0, r1 in chunks(4 * strip):
        local = local_terms(coef, lambda g: xr[g, r0:r1, :], r1 - r0, va, vd, r0)
        for g in range(g_all):
            acc[g, face + r0 : face + r1, :] = local[g]


def filter_kernel(plan, paired, zc, inner, outer, xr, vai, vdi, vah, vdh, given, sh_in, sl_in, w1h, w1l, w2h, w2l, coef, dcoef,
                  vspread, out, mx, my, mz, sh, sl, xc, y, th, tl, va, vd, acc):
    g_all, lanes, rows, face, cross, c = plan.groups, plan.lanes, plan.rows, plan.face, plan.cross, plan.cells
    strip, lot, corner = plan.strip, plan.lot, plan.corner
    span = BUF * corner
    mz = sides(mz, paired)
    zlo, zhi = sides(zc, paired)[::-1] if paired else zc
    spread_potential(plan, [(piece[g_all * span :, :], 0, span) for piece in (zlo, zhi)], vspread, va, vd)
    for g in range(g_all):
        cols = slice(g * lanes, (g + 1) * lanes)
        for k, piece in enumerate((zlo, zhi)):
            xc[g, k * span : (k + 1) * span, :] = piece[g * span : (g + 1) * span, :]
        put = lambda at, a, b: put_folded(sh, sl, lot, at, cols, a, b)
        fold_corners([xc[g, k * 2 * corner : (k + 1) * 2 * corner, :] for k in range(BUF)], put, cross // 2)

    for r0, r1 in chunks(2 * span):
        local = local_terms(coef, lambda g: xc[g, r0:r1, :], r1 - r0, va, vd, r0)
        for g in range(g_all):
            y[g, cross + r0 : cross + r1, :] = local[g]
    for n, (g0, g1) in enumerate(pairs(g_all)):
        cols = slice(g0 * lanes, g1 * lanes)
        for p in range(2):
            own = slice(p * lot, (p + 1) * lot)
            acc[n % 2, own, : (g1 - g0) * lanes] = three(w1h[p], w1l[p], sh[own, cols], sl[own, cols])
        for g in range(g0, g1):
            mine = slice((g - g0) * lanes, (g - g0 + 1) * lanes)
            to = slice(g * lanes, (g + 1) * lanes)
            put = lambda at, a, b: put_folded(th, tl, lot, at, to, a, b)
            product = unfold(plan, lambda at, k: acc[n % 2, at : at + k, mine], lambda at, k: acc[n % 2, lot + at : lot + at + k, mine], True)
            for again, at, blocks in product:
                values = []
                for r0, block in blocks:
                    local = given[g, r0 : r0 + 16, :] if r0 < cross else y[g, r0 : r0 + 16, :]
                    values.append((local + block) * (S0 / HALF_WIDTH))
                    y[g, r0 : r0 + 16, :] = values[-1]
                again(values, put, at)

    for r0, r1 in chunks(cross):
        v, d, at = (vai, vdi, r0) if r0 < face else (vah, vdh, r0 - face)
        local = local_terms(coef, lambda g: y[g, r0:r1, :], r1 - r0, v, d, at)
        for g in range(g_all):
            if g >= BUF or r0 < face:
                if r0 >= face:
                    x = xr[g, r0 - face : r1 - face, :]
                else:
                    x = outer[g, r0:r1, :] if g < BUF else inner[g - BUF, r0:r1, :]
                out[g, r0:r1, :] = local[g] * (2.0 * S1 / HALF_WIDTH) - (S0 * S1) * x
    flat = plan.flat
    for n, (g0, g1) in enumerate(pairs(g_all)):
        cols = slice(g0 * lanes, g1 * lanes)
        for p in range(2):
            own = slice(p * lot, (p + 1) * lot)
            acc[n % 2, p * lot : p * lot + flat, : (g1 - g0) * lanes] = three(w2h[p], w2l[p], th[own, cols], tl[own, cols])
        for g in range(g0, g1):
            mine = slice((g - g0) * lanes, (g - g0 + 1) * lanes)
            product = unfold(plan, lambda at, k: acc[n % 2, at : at + k, mine], lambda at, k: acc[n % 2, lot + at : lot + at + k, mine], False)
            for _, _, blocks in product:
                for r0, block in blocks:
                    if r0 < face or g >= BUF:
                        out[g, r0 : r0 + 16, :] = out[g, r0 : r0 + 16, :] + block

    for r0, r1 in chunks(face):
        mask = low_lanes((r1 - r0, lanes))
        e = out[BUF, r0:r1, :]
        d = mix(dcoef, 0, [out[g, r0:r1, :] for g in range(g_all)])
        te, td = swap(e), swap(d)
        mx[0][r0:r1, :] = 0.5 * jnp.where(mask, e + te, d + td)
        mx[1][r0:r1, :] = 0.5 * jnp.where(mask, e - te, d - td)
    part = plan.inner * c
    order = list(range(BUF, BUF + c)) + list(range(BUF)) + list(range(BUF + c, plan.ext))
    mask = low_lanes((c, lanes))
    for j in range(plan.inner):
        g = BUF + j
        ylayers = [out[g, k * c : (k + 1) * c, :] for k in range(plan.ext)]
        zlayers = [out[g, pl.ds(k, c, stride=c), :] for k in range(c)]
        zlayers += [out[g, plan.yext + k * c : plan.yext + (k + 1) * c, :] for k in range(2 * BUF)]
        for layers, message in ((ylayers, my), (zlayers, mz)):
            for side, layer in enumerate((0, c - 1)):
                total = None
                for k, t in enumerate(order):
                    weight = float(plan.first[BUF + layer, t])
                    if t != BUF + layer:
                        term = weight * layers[k]
                        total = term if total is None else total + term
                value = layers[layer]
                message[side][j * c : (j + 1) * c, :] = jnp.where(mask, value, swap(total))
                message[side][part + j * c : part + (j + 1) * c, :] = jnp.where(mask, swap(value), total)


def own_kernel(plan, f, va, vd, bh, bl, coef, diag, basis, local, f2, f2h, f2l, fhi, acc, sem):
    g_all, lanes, face, cross, c = plan.groups, plan.lanes, plan.face, plan.cross, plan.cells
    copies = []
    for j in range(plan.inner):
        for r0, r1 in chunks(face, 64):
            e = f[BUF + j, r0:r1, :]
            t = swap(e)
            local[j, r0:r1, :] = (0.5 * (e + t))[:, : plan.width]
            local[c - 1 - j, r0:r1, :] = (0.5 * (e - t))[:, : plan.width]
        for x in (j, c - 1 - j):
            copies.append(pltpu.make_async_copy(local.at[x], basis.at[x], sem.at[x]))
            copies[-1].start()
    for g in range(g_all):
        top = face if g < BUF else cross
        for r0, r1 in chunks(top):
            value = f[g, r0:r1, :]
            high = value.astype(BF)
            fhi[g, r0:r1, :] = high
            f2[g, r0:r1, :] = 2.0 * value - high.astype(F32)
        if g >= BUF:
            to = slice((g - BUF) * lanes, (g - BUF + 1) * lanes)
            put = lambda at, a, b: put_folded(f2h, f2l, plan.flat, at, to, a, b)
            fold_inside(plan, lambda r, n: f2[g, r : r + n, :], put)
            fold_halo(plan, lambda r, n: f2[g, face + r : face + r + n, :], put)
    total = jnp.zeros((lanes, 2 * lanes), F32)

    def fold(total, g, top, value):
        h, l = split(value)
        return total + dot_t(fhi[g, :top, :], jnp.concatenate([h, l], axis=1))

    def mixed(g, r0, r1):
        return mix(coef, g * g_all, [f2[s, r0:r1, :] for s in range(g_all)])

    for g in range(BUF):
        total = fold(total, g, face, jnp.concatenate([mixed(g, r0, r1) for r0, r1 in chunks(face)], axis=0))
    for n, (j0, j1) in enumerate(pairs(plan.inner)):
        slot = n % 2
        cols = slice(j0 * lanes, j1 * lanes)
        for p in range(2):
            half = slice(p * plan.flat, (p + 1) * plan.flat)
            acc[slot, half] = three(bh[p], bl[p], f2h[half, cols], f2l[half, cols])
        for j in range(j0, j1):
            g = BUF + j
            mine = slice((j - j0) * lanes, (j - j0 + 1) * lanes)
            flat = plan.flat
            product = unfold(plan, lambda at, k: acc[slot, at : at + k, mine], lambda at, k: acc[slot, flat + at : flat + at + k, mine], False)
            product = {r0: block for _, _, blocks in product for r0, block in blocks}
            parts = []
            for r0, r1 in chunks(face):
                own = f2[g, r0:r1, :]
                value = product[r0] + mixed(g, r0, r1)
                parts.append(value + (va[g, r0:r1, :] + CENTER) * own + vd[g, r0:r1, :] * swap(own))
            parts += [product[r0] for r0 in range(face, cross, 16)]
            total = fold(total, g, cross, jnp.concatenate(parts, axis=0))
    both = total[:, :lanes] + total[:, lanes:]
    w = plan.width
    block = both[:w, :w] + both[w:, w:]
    diag[...] = 0.25 * (block + jnp.transpose(block))
    for copy in copies:
        copy.wait()


def face_block(plan, own, other, sign, scale):
    w, lanes = plan.width, plan.lanes
    ah, al = split(own[...])
    bh, bl = split(other[...])
    first = dot_t(ah, jnp.concatenate([bh, bl], axis=1))
    m = first[:, :lanes] + first[:, lanes:] + dot_t(al, bh)
    return scale * (0.25 * sign * (m[w:, :w] - m[:w, w:]) - 0.5 * PENALTY * m[:w, :w])


def early_faces_kernel(plan, paired, ox, oy, oz, nx, ny, nz, blocks):
    oz, nz = sides(oz, paired), sides(nz, paired)[::-1] if paired else nz
    blocks[0] = face_block(plan, ox, nx, -1.0, 1.0)
    for k, (own, other, sign) in enumerate(((oy, ny, 1.0), (oz[0], nz[0], -1.0), (oz[1], nz[1], 1.0))):
        blocks[1 + k] = face_block(plan, own, other, sign, 0.5)


def late_faces_kernel(plan, diag, early, ox, oy, nx, ny, blocks, local, sem):
    copies = [
        pltpu.make_async_copy(diag, blocks.at[0], sem.at[0]),
        pltpu.make_async_copy(early.at[0], blocks.at[1], sem.at[1]),
        pltpu.make_async_copy(early.at[1:4], blocks.at[4:7], sem.at[2]),
        pltpu.make_async_copy(local, blocks.at[2:4], sem.at[3]),
    ]
    for copy in copies[:3]:
        copy.start()
    local[0] = face_block(plan, ox, nx, 1.0, 1.0)
    local[1] = face_block(plan, oy, ny, -1.0, 0.5)
    copies[3].start()
    for copy in copies:
        copy.wait()


def near(*shape):
    return pltpu.VMEM(shape, F32)


def far(*shape):
    return jax.ShapeDtypeStruct(shape, F32)


def call(kernel, outs, args, scratch=(), flops=0, limit=24, aliases=None, far_in=(), far_out=()):
    def place(a, where):
        return pltpu.with_memory_space_constraint(jnp.asarray(a), where)

    placed = [jax.tree.map(lambda b: place(b, pltpu.HBM if i in far_in else pltpu.VMEM), a) for i, a in enumerate(args)]
    space, apart = pl.BlockSpec(memory_space=pltpu.VMEM), pl.BlockSpec(memory_space=pl.ANY)
    return pl.pallas_call(
        kernel,
        out_shape=outs,
        in_specs=[apart if i in far_in else jax.tree.map(lambda b: space, a) for i, a in enumerate(placed)],
        out_specs=[apart if i in far_out else jax.tree.map(lambda b: space, a) for i, a in enumerate(outs)],
        scratch_shapes=list(scratch),
        input_output_aliases=aliases or {},
        compiler_params=pltpu.CompilerParams(vmem_limit_bytes=limit * 1024 * 1024),
        cost_estimate=pl.CostEstimate(flops=flops, bytes_accessed=0, transcendentals=0),
    )(*placed)


def shift(array, axis, step):
    count = lax.axis_size(axis)
    return lax.ppermute(array, axis, [(i, (i + step) % count) for i in range(count)])


def shift_z(both, paired):
    if paired:
        return shift(both, "gz", 1)
    return [shift(both[1], "gz", 1), shift(both[0], "gz", -1)]


def on_device(orbitals, potential):
    cells, width = orbitals.shape[0], orbitals.shape[-1]
    plan = Plan(cells, width)
    lanes, face, strip, rows, cross = plan.lanes, plan.face, plan.strip, plan.rows, plan.cross
    g_all, inner_all, corner = plan.groups, plan.inner, plan.corner
    paired = lax.axis_size("gz") == 2
    part = functools.partial
    bf = lambda *shape: pltpu.VMEM(shape, BF)
    wide = g_all * lanes

    def two(*shape):
        return near(2, *shape) if paired else [near(*shape), near(*shape)]

    srows, rrows, yrows = BUF * strip + 8, BUF * (face // 2 - strip), inner_all * strip + cells
    orb = orbitals.reshape(cells, face, width)
    slo, shi, ylo, yhi, vt = call(
        part(strip_kernel, plan),
        [near(srows, lanes), near(srows, lanes), near(yrows, lanes), near(yrows, lanes), near(cells, face)],
        [orb, potential.reshape(face, cells)],
        [near(cells, strip, width), near(cells, strip, width), near(face, cells), pltpu.SemaphoreType.DMA((3,))],
        far_in=(0, 1),
    )
    from_ylo, from_yhi = shift(yhi, "gy", 1), shift(ylo, "gy", -1)
    from_slo, from_shi = shift(shi, "gx", 1), shift(slo, "gx", -1)
    rlo, rhi, inner = call(
        part(pack_kernel, plan), [near(rrows, lanes), near(rrows, lanes), near(inner_all, face, lanes)], [orb],
    )
    from_rlo, from_rhi = shift(rhi, "gx", 1), shift(rlo, "gx", -1)

    ipick = np.zeros((2, face, lanes), np.float32)
    cpick = np.zeros((2, lanes, lanes), np.float32)
    for side in range(2):
        for k in range(BUF):
            z = side * (cells - BUF) + k
            for y in range(cells):
                ipick[side, y * cells + z, k * cells + y] = 1.0
            for y in range(corner):
                cpick[side, y * cells + z, k * corner + y] = 1.0
    elo, ehi, vx = call(
        part(edge_kernel, plan), [near(srows, lanes), near(srows, lanes), near(plan.trows, face)], [vt, from_slo, from_shi, from_ylo],
        flops=2*10**9,
    )
    from_elo, from_ehi = shift(ehi, "gy", 1), shift(elo, "gy", -1)

    matrix = -0.5 * row_matrix(plan, plan.second, False)
    coef = folded(-0.5 * mirrored(plan, plan.second))
    vspread = np.zeros((plan.trows, 2, g_all, lanes), np.float32)
    for g in range(g_all):
        vspread[g, :, g, :] = 0.5
        vspread[plan.ext - 1 - g, 0, g, :] = 0.5
        vspread[plan.ext - 1 - g, 1, g, :] = -0.5
    vspread = np.tile(vspread.reshape(plan.trows, -1), (3, 1)).astype(ml_dtypes.bfloat16)
    vai, vdi, early = call(
        part(inside_kernel, plan), [near(g_all, face, lanes), near(g_all, face, lanes), near(8, lanes)], [vx, vspread],
    )
    outer, zi = call(
        part(xhalo_kernel, plan, paired),
        [near(BUF, face, lanes), two(g_all * strip + plan.trows, lanes)],
        [inner, vx, elo, ehi, from_rlo, from_rhi, ipick, early],
    )
    zi = shift_z(zi, paired)
    both = pltpu.VMEM((2 * plan.lot, wide), BF)
    acc, order, sh, sl = call(
        part(outside_kernel, plan), [near(g_all, cross, lanes), near(8, lanes), both, both], [inner, outer, coef, vai, vdi],
    )

    room = 2 * strip + (corner - 2 * BUF) * cells
    yh, vy, zc = call(
        part(ypack_kernel, plan, paired),
        [near(g_all, room, lanes), near(plan.trows, lanes), two(g_all * BUF * corner + plan.trows, lanes)],
        [from_ylo, from_yhi, from_elo, from_ehi, cpick, order],
        flops=10**10,
    )
    zc = shift_z(zc, paired)
    rest = 4 * strip
    base = 5 if paired else 6
    acc, sh, sl, xr, vah, vdh = call(
        part(halo_kernel, plan, paired),
        [near(g_all, cross, lanes), both, both, near(g_all, rest, lanes), near(g_all, rest, lanes), near(g_all, rest, lanes)],
        [yh, vy, zi, coef, vspread, acc, sh, sl],
        aliases={base: 0, base + 1: 1, base + 2: 2},
    )

    p = plan.first[BUF, :g_all] + plan.first[BUF, ::-1][:g_all]
    q = plan.first[BUF, :g_all] - plan.first[BUF, ::-1][:g_all]
    dcoef = np.concatenate([np.repeat(p[:, None], width, 1), np.repeat(q[:, None], width, 1)], 1).astype(np.float32)
    msg = near(face, lanes)
    corners = 2 * BUF * corner
    product = folded_rows(plan, matrix)
    second = 2.0 * S1 / HALF_WIDTH * product[:, : plan.flat]
    base = 9 if paired else 10
    filtered, mx, my, mz, _, _ = call(
        part(filter_kernel, plan, paired),
        [near(g_all, cross, lanes), [msg, msg], [msg, msg], two(face, lanes), both, both],
        [zc, inner, outer, xr, vai, vdi, vah, vdh, acc, sh, sl, *halves(product), *halves(second), coef, dcoef, vspread],
        [near(g_all, corners, lanes), near(g_all, rows, lanes), both, both,
         near(g_all, corners, lanes), near(g_all, corners, lanes), near(2, 2 * plan.lot, 2 * lanes)],
        aliases={base: 6 if paired else 7, base + 1: 7 if paired else 8},
    )
    ny = [shift(my[1], "gy", 1), shift(my[0], "gy", -1)]
    nx = [shift(mx[1], "gx", 1), shift(mx[0], "gx", -1)]
    nz = shift_z(mz, paired)

    along = energy(plan)
    bcoef = mirrored(plan, along).reshape(-1, lanes).astype(np.float32)
    diag, basis = call(
        part(own_kernel, plan), [near(width, width), far(cells, face, width)],
        [filtered, vai, vdi, *halves(folded_rows(plan, row_matrix(plan, along, True))[:, : plan.flat, : plan.flat]), bcoef],
        [near(cells, face, width), near(g_all, cross, lanes), bf(cross, inner_all * lanes), bf(cross, inner_all * lanes), bf(g_all, cross, lanes),
         near(2, cross, 2 * lanes), pltpu.SemaphoreType.DMA((cells,))],
        flops=2 * 10**9,
        far_out=(1,),
    )
    (first_faces,) = call(
        part(early_faces_kernel, plan, paired), [near(4, width, width)], [mx[0], my[1], mz, nx[0], ny[1], nz],
    )
    (blocks,) = call(
        part(late_faces_kernel, plan), [far(7, width, width)], [diag, first_faces, mx[1], my[0], nx[1], ny[0]],
        [near(2, width, width), pltpu.SemaphoreType.DMA((4,))], far_out=(0,),
    )
    return basis.reshape(orbitals.shape), blocks[None, None, None]


def solution(mesh):
    return jax.shard_map(
        on_device,
        mesh=mesh,
        in_specs=(P("gx", "gy", "gz", None), P("gx", "gy", "gz")),
        out_specs=(P("gx", "gy", "gz", None), P("gx", "gy", "gz", None, None, None)),
        check_vma=False,
    )
```

```python
import functools

import jax
import jax.numpy as jnp
import ml_dtypes
import numpy as np
from jax import lax
from jax.experimental import pallas as pl
from jax.experimental.pallas import tpu as pltpu
from jax.sharding import PartitionSpec as P

BUF = 3
PENALTY = 2.0
LOW_BOUND = -1.5
CUTOFF = 8.0
HIGH_BOUND = 16.0
BF = jnp.bfloat16
F32 = jnp.float32


class Plan:
    def __init__(self, cells, width):
        self.cells, self.width = cells, width
        self.ext = cells + 2 * BUF
        self.groups = self.ext // 2
        self.inner = cells // 2
        self.lanes = 2 * width
        self.face = cells * cells
        self.strip = BUF * cells
        self.corner = -(-2 * BUF // 8) * 8
        self.yext = self.face + 2 * self.strip
        self.cross = self.yext + 2 * self.strip
        self.rows = self.cross + 2 * BUF * self.corner
        self.trows = -(-self.ext // 8) * 8
        inside = list(range(BUF, BUF + cells))
        outside = list(range(BUF)) + list(range(BUF + cells, self.ext))
        points = [(y, z) for y in inside for z in inside] + [(y, z) for y in outside for z in inside]
        points += [(y, z) for z in outside for y in inside]
        gap = self.corner - 2 * BUF
        for z in outside:
            points += [(y, z) for y in outside[:BUF]] + [None] * gap + [(y, z) for y in outside[BUF:]]
        self.fold = self.rows // 2
        self.flat = self.cross // 2
        self.lot = -(-self.fold // 16) * 16
        self.points = points
        self.first, self.second = spectral(self.ext)
        self.inside = np.isin(np.arange(self.ext), inside)


def spectral(points):
    indices = np.arange(points)
    offsets = indices[:, None] - indices[None, :]
    first = np.zeros((points, points))
    second = np.zeros((points, points))
    for harmonic in range(1, points // 2):
        wavenum = 2.0 * np.pi * harmonic / points
        first = first - 2.0 * wavenum * np.sin(wavenum * offsets) / points
        second = second - 2.0 * wavenum * wavenum * np.cos(wavenum * offsets) / points
    second = second - np.pi * np.pi * np.cos(np.pi * offsets) / points
    return first, second


def row_matrix(plan, along, masked):
    real = np.array([p is not None for p in plan.points])
    y, z = np.array([(0, 0) if p is None else p for p in plan.points]).T
    by_y = along[y[:, None], y[None, :]] * (z[:, None] == z[None, :])
    by_z = along[z[:, None], z[None, :]] * (y[:, None] == y[None, :])
    if masked:
        by_y, by_z = by_y * plan.inside[z][:, None], by_z * plan.inside[y][:, None]
    return (by_y + by_z) * real[:, None] * real[None, :]


def mirror_basis(plan):
    c, face, strip = plan.cells, plan.face, plan.strip
    kept = [(y * c + z, (c - 1 - y) * c + z) for y in range(c // 2) for z in range(c)]
    kept += [(face + k * c + z, face + (2 * BUF - 1 - k) * c + z) for k in range(BUF) for z in range(c)]
    kept += [(plan.yext + k * c + y, plan.yext + k * c + c - 1 - y) for k in range(2 * BUF) for y in range(c // 2)]
    for m in range(BUF):
        for r in range(plan.corner):
            at = plan.cross + (2 * m + (r >= plan.corner // 2)) * plan.corner
            kept.append((at + r, at + plan.corner - 1 - r))
    out = np.zeros((2, plan.lot, plan.rows))
    for i, (a, b) in enumerate(kept):
        out[:, i, a] += 1.0
        out[0, i, b] += 1.0
        out[1, i, b] -= 1.0
    return out


def folded_rows(plan, matrix):
    basis = mirror_basis(plan)
    return 0.25 * np.einsum("pia,ab,pjb->pij", basis, matrix, basis, optimize=True)


def mirrored(plan, along):
    g = plan.groups
    plus = along[:g, :g] + along[:g, ::-1][:, :g]
    minus = along[:g, :g] - along[:g, ::-1][:, :g]
    return np.concatenate([np.repeat(plus[:, :, None], plan.width, 2), np.repeat(minus[:, :, None], plan.width, 2)], 2)


def folded(table):
    g = table.shape[0]
    half, odd = g // 2, g % 2
    out = []
    for t in range(half + odd):
        out += [0.5 * (table[t, s] + table[t, g - 1 - s]) for s in range(half)] + [table[t, half]] * odd
        if t < half:
            out += [0.5 * (table[t, s] - table[t, g - 1 - s]) for s in range(half)]
    return np.stack(out).astype(np.float32)


def energy(plan):
    c = plan.cells
    block = plan.first[BUF : BUF + c]
    out = 0.5 * block.T @ block
    for sign, layer in ((-1.0, BUF), (1.0, BUF + c - 1)):
        unit = np.zeros(plan.ext)
        unit[layer] = 1.0
        cross = np.outer(unit, plan.first[layer])
        out = out + 0.5 * PENALTY * np.outer(unit, unit) - 0.25 * sign * (cross + cross.T)
    return out


def halves(matrix):
    high = matrix.astype(np.float32).astype(ml_dtypes.bfloat16)
    low = (matrix - high.astype(np.float64)).astype(np.float32).astype(ml_dtypes.bfloat16)
    return high, low


def split(x):
    high = x.astype(BF)
    return high, (x - high.astype(F32)).astype(BF)


def swap(x):
    return pltpu.roll(x, x.shape[-1] // 2, x.ndim - 1)


def dot(a, b):
    return jnp.dot(a, b, preferred_element_type=F32)


def dot_t(a, b):
    return lax.dot_general(a, b, (((0,), (0,)), ((), ())), preferred_element_type=F32)


def exact(a, b):
    return jnp.dot(a, b, preferred_element_type=F32, precision=lax.Precision.HIGHEST)


def three(wh, wl, sh, sl):
    return dot(wh, sh) + dot(wl, sh) + dot(wh, sl)


def flip(x):
    row = lax.broadcasted_iota(jnp.int32, x.shape, 0)
    x = pltpu.roll(x, 4, 0)
    x = jnp.where(lax.rem(row, 4) < 2, pltpu.roll(x, 6, 0), pltpu.roll(x, 2, 0))
    return jnp.where(lax.rem(row, 2) < 1, pltpu.roll(x, 7, 0), pltpu.roll(x, 1, 0))


def put_folded(sh, sl, lot, at, cols, plus, minus):
    for p, value in enumerate((plus, minus)):
        h, l = split(value)
        sh[p * lot + at : p * lot + at + value.shape[0], cols] = h
        sl[p * lot + at : p * lot + at + value.shape[0], cols] = l


def fold_blocks(blocks, put, at):
    a, b = blocks
    put(at, a + b, a - b)


def fold_planes(blocks, put, at):
    firsts, lasts = [p[:8] for p in blocks], [flip(p[8:]) for p in blocks]
    put(at, jnp.concatenate([a + b for a, b in zip(firsts, lasts)], axis=0),
        jnp.concatenate([a - b for a, b in zip(firsts, lasts)], axis=0))


def fold_corners(blocks, put, at):
    plus, minus = [], []
    for block in blocks:
        a, b = block[:8], block[8:]
        fa, fb = flip(a), flip(b)
        first = lax.broadcasted_iota(jnp.int32, a.shape, 0) < 4
        plus.append(jnp.where(first, a + fa, b + fb))
        minus.append(jnp.where(first, a - fa, b - fb))
    zero = jnp.zeros_like(plus[0])
    put(at, jnp.concatenate(plus + [zero], axis=0), jnp.concatenate(minus + [zero], axis=0))


def fold_inside(plan, get, put):
    c = plan.cells
    for y in range(c // 2):
        fold_blocks([get(y * c, c), get((c - 1 - y) * c, c)], put, y * c)


def fold_halo(plan, get, put):
    c = plan.cells
    for k in range(BUF):
        fold_blocks([get(k * c, c), get((2 * BUF - 1 - k) * c, c)], put, plan.face // 2 + k * c)
    at = 2 * plan.strip
    for k in range(0, 2 * BUF, 2):
        fold_planes([get(at + k * c, c), get(at + (k + 1) * c, c)], put, plan.yext // 2 + k * 8)


def unfold(plan, v0, v1, corners):
    c = plan.cells

    def both(at, n):
        a, b = v0(at, n), v1(at, n)
        return a + b, a - b

    for y in range(c // 2):
        a, b = both(y * c, c)
        yield fold_blocks, y * c, [(y * c, a), ((c - 1 - y) * c, b)]
    at = plan.face // 2
    for k in range(BUF):
        a, b = both(at + k * c, c)
        yield fold_blocks, at + k * c, [(plan.face + k * c, a), (plan.face + (2 * BUF - 1 - k) * c, b)]
    at = plan.yext // 2
    for k in range(0, 2 * BUF, 2):
        made = []
        for m in (k, k + 1):
            a, b = both(at + m * 8, 8)
            made.append((plan.yext + m * c, jnp.concatenate([a, flip(b)], axis=0)))
        yield fold_planes, at + k * 8, made
    if corners:
        at, made = plan.cross // 2, []
        for m in range(BUF):
            a, b = both(at + m * 8, 8)
            first = lax.broadcasted_iota(jnp.int32, a.shape, 0) < 4
            b = flip(b)
            made.append((plan.cross + m * 16, jnp.concatenate([jnp.where(first, a, b), jnp.where(first, b, a)], axis=0)))
        yield fold_corners, at, made


def low_lanes(shape):
    return lax.broadcasted_iota(jnp.int32, shape, len(shape) - 1) < shape[-1] // 2


def sides(ref, paired):
    return [ref.at[0], ref.at[1]] if paired else ref


def chunks(stop, size=16, start=0):
    return [(r, min(r + size, stop)) for r in range(start, stop, size)]


def pairs(stop, start=0):
    return [(g, min(g + 2, stop)) for g in range(start, stop, 2)]


CENTER = (HIGH_BOUND + CUTOFF) / 2.0
HALF_WIDTH = (HIGH_BOUND - CUTOFF) / 2.0
S0 = HALF_WIDTH / (LOW_BOUND - CENTER)
S1 = 1.0 / (2.0 / S0 - S0)
SECOND = (2.0 * S1 / HALF_WIDTH) * (S0 / HALF_WIDTH)


def mix(coef, table, items):
    total = None
    for s, item in enumerate(items):
        term = coef[table + s : table + s + 1, :] * item
        total = term if total is None else total + term
    return total


def fold_mix(coef, items):
    g = len(items)
    half, odd = g // 2, g % 2
    plus = [items[s] + items[g - 1 - s] for s in range(half)] + [items[half]] * odd
    minus = [items[s] - items[g - 1 - s] for s in range(half)]
    out, k = [None] * g, 0
    for t in range(half + odd):
        p = mix(coef, k, plus)
        k += len(plus)
        if t < half:
            q = mix(coef, k, minus)
            k += half
            out[t], out[g - 1 - t] = p + q, p - q
        else:
            out[t] = p
    return out


def spread_potential(plan, pieces, vspread, va, vd):
    turned = []
    for piece, start, stop in pieces:
        high = piece.astype(BF).astype(F32)
        rest = piece - high
        mid = rest.astype(BF).astype(F32)
        stacked = jnp.concatenate([high, mid, rest - mid], axis=0)
        turned.append(jnp.transpose(stacked)[start:stop, :])
    turned = jnp.concatenate(turned, axis=0).astype(BF)
    g_all, lanes = plan.groups, plan.lanes
    for g0, g1 in pairs(g_all):
        for k, dst, less in ((0, va, CENTER), (1, vd, 0.0)):
            cols = slice((k * g_all + g0) * lanes, (k * g_all + g1) * lanes)
            both = dot(turned, vspread[:, cols]) - less
            for g in range(g0, g1):
                dst[g] = both[:, (g - g0) * lanes : (g - g0 + 1) * lanes]


def local_terms(coef, get, count, va, vd, v0):
    items = [get(g) for g in range(va.shape[0])]
    out = fold_mix(coef, items)
    for g, own in enumerate(items):
        out[g] = out[g] + va[g, v0 : v0 + count, :] * own + vd[g, v0 : v0 + count, :] * swap(own)
    return out


def strip_kernel(plan, orb_far, pot_far, slo, shi, ylo, yhi, vt, low, high, pot, sem):
    c, lanes, face, strip, w = plan.cells, plan.lanes, plan.face, plan.strip, plan.width
    copies = [
        pltpu.make_async_copy(pot_far, pot, sem.at[0]),
        pltpu.make_async_copy(orb_far.at[:, :strip], low, sem.at[1]),
        pltpu.make_async_copy(orb_far.at[:, face - strip :], high, sem.at[2]),
    ]
    for copy in copies:
        copy.start()
    copies[0].wait()
    v = jnp.concatenate([pot[pl.ds(y, c, stride=c), :] for y in range(c)], axis=1)
    vt[...] = v
    base = BUF * strip
    for out, first in ((slo, 0), (shi, c - BUF)):
        out[base:, :] = jnp.zeros((8, lanes), F32)
        for part in range(2):
            out[base + part * BUF : base + (part + 1) * BUF, :] = v[first : first + BUF, part * lanes : (part + 1) * lanes]
    ybase = plan.inner * strip
    ylo[ybase:, :] = v[:, :lanes]
    yhi[ybase:, :] = v[:, face - lanes :]
    copies[1].wait()
    copies[2].wait()
    for out, part in ((ylo, low), (yhi, high)):
        for j in range(plan.inner):
            a, b = part[j], part[c - 1 - j]
            out[j * strip : (j + 1) * strip, :] = jnp.concatenate([a + b, a - b], axis=1)
    for k in range(BUF):
        rows = slice(k * strip, (k + 1) * strip)
        slo[rows, :] = jnp.concatenate([low[k], high[k]], axis=1)
        shi[rows, :] = jnp.concatenate([low[c - BUF + k], high[c - BUF + k]], axis=1)


def pack_kernel(plan, orb, rlo, rhi, inner):
    c, strip, face = plan.cells, plan.strip, plan.face
    half, rest = face // 2, face // 2 - plan.strip
    for k in range(BUF):
        rows = slice(k * rest, (k + 1) * rest)
        for out, x in ((rlo, k), (rhi, c - BUF + k)):
            out[rows, :] = jnp.concatenate([orb[x, strip:half], orb[x, half : face - strip]], axis=1)
    for j in range(plan.inner):
        a, b = orb[j], orb[c - 1 - j]
        inner[j] = jnp.concatenate([a + b, a - b], axis=1)


def mirror(a, b):
    mask = low_lanes(a.shape)
    s, d = a + b, a - b
    return jnp.where(mask, s, swap(d)), jnp.where(mask, swap(s), d)


def edge_kernel(plan, vt, lo, hi, ahead, elo, ehi, vx):
    c, strip, lanes = plan.cells, plan.strip, plan.lanes
    for g in range(BUF):
        back = BUF - 1 - g
        top, bottom = mirror(lo[g * strip : (g + 1) * strip, :], hi[back * strip : (back + 1) * strip, :])
        elo[g * strip : (g + 1) * strip, :] = top
        ehi[g * strip : (g + 1) * strip, :] = bottom
    base = BUF * strip
    vx[...] = jnp.zeros(vx.shape, F32)
    vx[BUF : BUF + c, :] = vt[...]
    elo[base:, :] = jnp.zeros((8, lanes), F32)
    ehi[base:, :] = jnp.zeros((8, lanes), F32)
    for k, src in enumerate((lo, hi)):
        elo[base + k * BUF : base + (k + 1) * BUF, :] = src[base : base + BUF, :]
        ehi[base + k * BUF : base + (k + 1) * BUF, :] = src[base + BUF : base + 2 * BUF, :]
        at = 0 if k == 0 else BUF + c
        vx[at : at + BUF, :lanes] = src[base : base + BUF, :]
        vx[at : at + BUF, lanes:] = src[base + BUF : base + 2 * BUF, :]


def xhalo_kernel(plan, paired, inner, vx, elo, ehi, lo, hi, zpick, ahead, outer, zi):
    c, face, strip = plan.cells, plan.face, plan.strip
    half, rest = face // 2, face // 2 - strip
    for g in range(BUF):
        back = BUF - 1 - g
        top, bottom = mirror(lo[g * rest : (g + 1) * rest, :], hi[back * rest : (back + 1) * rest, :])
        outer[g, :strip] = elo[g * strip : (g + 1) * strip, :]
        outer[g, strip:half] = top
        outer[g, half : face - strip] = bottom
        outer[g, face - strip :] = ehi[g * strip : (g + 1) * strip, :]
    for side, dst in enumerate(sides(zi, paired)):
        start = side * (c - BUF)
        for g in range(plan.groups):
            src = outer.at[g] if g < BUF else inner.at[g - BUF]
            for k in range(BUF):
                at = g * strip + k * c
                dst[at : at + c, :] = src[pl.ds(start + k, c, stride=c), :]
        dst[plan.groups * strip :, :] = exact(vx[...], zpick[side])


def inside_kernel(plan, vx, vspread, va, vd, order):
    order[...] = jnp.zeros(order.shape, F32)
    spread_potential(plan, [(vx[...], 0, plan.face)], vspread, va, vd)


def outside_kernel(plan, inner, outer, coef, va, vd, acc, order, sh, sl):
    order[...] = jnp.zeros(order.shape, F32)
    lanes = plan.lanes

    def get(g, r0, r1):
        return outer[g, r0:r1, :] if g < BUF else inner[g - BUF, r0:r1, :]

    for g in range(plan.groups):
        put = functools.partial(put_folded, sh, sl, plan.lot)
        cols = slice(g * lanes, (g + 1) * lanes)
        fold_inside(plan, lambda r, n: get(g, r, r + n), lambda at, a, b: put(at, cols, a, b))
    for r0, r1 in chunks(plan.face):
        local = local_terms(coef, lambda g: get(g, r0, r1), r1 - r0, va, vd, r0)
        for g in range(plan.groups):
            acc[g, r0:r1, :] = local[g]


def ypack_kernel(plan, paired, ylo, yhi, elo, ehi, zpick, order, yh, vy, zc):
    c, lanes, strip, corner = plan.cells, plan.lanes, plan.strip, plan.corner
    last = yh.shape[1] - strip
    for g in range(plan.groups):
        lo, hi, at = (elo, ehi, g * strip) if g < BUF else (ylo, yhi, (g - BUF) * strip)
        yh[g, :strip] = lo[at : at + strip, :]
        yh[g, last:] = hi[at : at + strip, :]
    yh[:, strip:last] = jnp.zeros((plan.groups, last - strip, lanes), F32)
    ebase, ybase = BUF * strip, plan.inner * strip
    shift_in = lanes - strip
    vy[...] = jnp.zeros(vy.shape, F32)
    for e, y, cut, at in ((elo, ylo, shift_in, 0), (ehi, yhi, 0, last)):
        cols = slice(at, at + strip)
        vy[:BUF, cols] = e[ebase : ebase + BUF, :][:, cut : cut + strip]
        vy[BUF + c : plan.ext, cols] = e[ebase + BUF : ebase + 2 * BUF, :][:, cut : cut + strip]
        vy[BUF : BUF + c, cols] = y[ybase:, :][:, cut : cut + strip]
    for side, dst in enumerate(sides(zc, paired)):
        start = side * (c - BUF)
        for g in range(plan.groups):
            for k in range(BUF):
                at = (g * BUF + k) * corner
                dst[at : at + corner, :] = yh[g, pl.ds(start + k, corner, stride=c), :]
        dst[plan.groups * BUF * corner :, :] = exact(vy[...], zpick[side])


def halo_kernel(plan, paired, yh, vy, zi, coef, vspread, given, sh_in, sl_in, acc, sh, sl, xr, va, vd):
    g_all, lanes, strip, face = plan.groups, plan.lanes, plan.strip, plan.face
    last = yh.shape[1] - strip
    zlo, zhi = sides(zi, paired)[::-1] if paired else zi
    pots = [(vy[...], 0, strip), (vy[...], last, last + strip)]
    spread_potential(plan, pots + [(piece[g_all * strip :, :], 0, strip) for piece in (zlo, zhi)], vspread, va, vd)
    for g in range(g_all):
        xr[g, :strip, :] = yh[g, :strip, :]
        xr[g, strip : 2 * strip, :] = yh[g, last:, :]
        for k, piece in enumerate((zlo, zhi)):
            xr[g, (2 + k) * strip : (3 + k) * strip, :] = piece[g * strip : (g + 1) * strip, :]
    for g in range(g_all):
        cols = slice(g * lanes, (g + 1) * lanes)
        put = lambda at, a, b: put_folded(sh, sl, plan.lot, at, cols, a, b)
        fold_halo(plan, lambda r, n: xr[g, r : r + n, :], put)
    for r0, r1 in chunks(4 * strip):
        local = local_terms(coef, lambda g: xr[g, r0:r1, :], r1 - r0, va, vd, r0)
        for g in range(g_all):
            acc[g, face + r0 : face + r1, :] = local[g]


def filter_kernel(plan, paired, zc, inner, outer, xr, vai, vdi, vah, vdh, given, sh_in, sl_in, w1h, w1l, w2h, w2l, coef, dcoef,
                  vspread, out, mx, my, mz, sh, sl, xc, y, th, tl, va, vd, acc):
    g_all, lanes, rows, face, cross, c = plan.groups, plan.lanes, plan.rows, plan.face, plan.cross, plan.cells
    strip, lot, corner = plan.strip, plan.lot, plan.corner
    span = BUF * corner
    mz = sides(mz, paired)
    zlo, zhi = sides(zc, paired)[::-1] if paired else zc
    spread_potential(plan, [(piece[g_all * span :, :], 0, span) for piece in (zlo, zhi)], vspread, va, vd)
    for g in range(g_all):
        cols = slice(g * lanes, (g + 1) * lanes)
        for k, piece in enumerate((zlo, zhi)):
            xc[g, k * span : (k + 1) * span, :] = piece[g * span : (g + 1) * span, :]
        put = lambda at, a, b: put_folded(sh, sl, lot, at, cols, a, b)
        fold_corners([xc[g, k * 2 * corner : (k + 1) * 2 * corner, :] for k in range(BUF)], put, cross // 2)

    for r0, r1 in chunks(2 * span):
        local = local_terms(coef, lambda g: xc[g, r0:r1, :], r1 - r0, va, vd, r0)
        for g in range(g_all):
            y[g, cross + r0 : cross + r1, :] = local[g]
    for n, (g0, g1) in enumerate(pairs(g_all)):
        cols = slice(g0 * lanes, g1 * lanes)
        for p in range(2):
            own = slice(p * lot, (p + 1) * lot)
            acc[n % 2, own, : (g1 - g0) * lanes] = three(w1h[p], w1l[p], sh[own, cols], sl[own, cols])
        for g in range(g0, g1):
            mine = slice((g - g0) * lanes, (g - g0 + 1) * lanes)
            to = slice(g * lanes, (g + 1) * lanes)
            put = lambda at, a, b: put_folded(th, tl, lot, at, to, a, b)
            product = unfold(plan, lambda at, k: acc[n % 2, at : at + k, mine], lambda at, k: acc[n % 2, lot + at : lot + at + k, mine], True)
            for again, at, blocks in product:
                values = []
                for r0, block in blocks:
                    local = given[g, r0 : r0 + 16, :] if r0 < cross else y[g, r0 : r0 + 16, :]
                    values.append(local + block)
                    y[g, r0 : r0 + 16, :] = values[-1]
                again(values, put, at)

    for r0, r1 in chunks(cross):
        v, d, at = (vai, vdi, r0) if r0 < face else (vah, vdh, r0 - face)
        local = local_terms(coef, lambda g: y[g, r0:r1, :], r1 - r0, v, d, at)
        for g in range(g_all):
            if g >= BUF or r0 < face:
                if r0 >= face:
                    x = xr[g, r0 - face : r1 - face, :]
                else:
                    x = outer[g, r0:r1, :] if g < BUF else inner[g - BUF, r0:r1, :]
                out[g, r0:r1, :] = local[g] * SECOND - (S0 * S1) * x
    flat = plan.flat
    for n, (g0, g1) in enumerate(pairs(g_all)):
        cols = slice(g0 * lanes, g1 * lanes)
        for p in range(2):
            own = slice(p * lot, (p + 1) * lot)
            acc[n % 2, p * lot : p * lot + flat, : (g1 - g0) * lanes] = three(w2h[p], w2l[p], th[own, cols], tl[own, cols])
        for g in range(g0, g1):
            mine = slice((g - g0) * lanes, (g - g0 + 1) * lanes)
            product = unfold(plan, lambda at, k: acc[n % 2, at : at + k, mine], lambda at, k: acc[n % 2, lot + at : lot + at + k, mine], False)
            for _, _, blocks in product:
                for r0, block in blocks:
                    if r0 < face or g >= BUF:
                        out[g, r0 : r0 + 16, :] = out[g, r0 : r0 + 16, :] + block

    for r0, r1 in chunks(face):
        mask = low_lanes((r1 - r0, lanes))
        e = out[BUF, r0:r1, :]
        d = mix(dcoef, 0, [out[g, r0:r1, :] for g in range(g_all)])
        te, td = swap(e), swap(d)
        mx[0][r0:r1, :] = 0.5 * jnp.where(mask, e + te, d + td)
        mx[1][r0:r1, :] = 0.5 * jnp.where(mask, e - te, d - td)
    part = plan.inner * c
    order = list(range(BUF, BUF + c)) + list(range(BUF)) + list(range(BUF + c, plan.ext))
    mask = low_lanes((c, lanes))
    for j in range(plan.inner):
        g = BUF + j
        ylayers = [out[g, k * c : (k + 1) * c, :] for k in range(plan.ext)]
        zlayers = [out[g, pl.ds(k, c, stride=c), :] for k in range(c)]
        zlayers += [out[g, plan.yext + k * c : plan.yext + (k + 1) * c, :] for k in range(2 * BUF)]
        for layers, message in ((ylayers, my), (zlayers, mz)):
            for side, layer in enumerate((0, c - 1)):
                total = None
                for k, t in enumerate(order):
                    weight = float(plan.first[BUF + layer, t])
                    if t != BUF + layer:
                        term = weight * layers[k]
                        total = term if total is None else total + term
                value = layers[layer]
                message[side][j * c : (j + 1) * c, :] = jnp.where(mask, value, swap(total))
                message[side][part + j * c : part + (j + 1) * c, :] = jnp.where(mask, swap(value), total)


def own_kernel(plan, f, va, vd, bh, bl, coef, diag, basis, local, f2, f2h, f2l, fhi, acc, sem):
    g_all, lanes, face, cross, c = plan.groups, plan.lanes, plan.face, plan.cross, plan.cells
    copies = []
    for j in range(plan.inner):
        for r0, r1 in chunks(face, 64):
            e = f[BUF + j, r0:r1, :]
            t = swap(e)
            local[j, r0:r1, :] = (0.5 * (e + t))[:, : plan.width]
            local[c - 1 - j, r0:r1, :] = (0.5 * (e - t))[:, : plan.width]
        for x in (j, c - 1 - j):
            copies.append(pltpu.make_async_copy(local.at[x], basis.at[x], sem.at[x]))
            copies[-1].start()
    for g in range(g_all):
        top = face if g < BUF else cross
        for r0, r1 in chunks(top):
            value = f[g, r0:r1, :]
            high = value.astype(BF)
            fhi[g, r0:r1, :] = high
            f2[g, r0:r1, :] = 2.0 * value - high.astype(F32)
        if g >= BUF:
            to = slice((g - BUF) * lanes, (g - BUF + 1) * lanes)
            put = lambda at, a, b: put_folded(f2h, f2l, plan.flat, at, to, a, b)
            fold_inside(plan, lambda r, n: f2[g, r : r + n, :], put)
            fold_halo(plan, lambda r, n: f2[g, face + r : face + r + n, :], put)
    total = jnp.zeros((lanes, 2 * lanes), F32)

    def fold(total, g, top, value):
        h, l = split(value)
        return total + dot_t(fhi[g, :top, :], jnp.concatenate([h, l], axis=1))

    def mixed(g, r0, r1):
        return mix(coef, g * g_all, [f2[s, r0:r1, :] for s in range(g_all)])

    for g in range(BUF):
        total = fold(total, g, face, jnp.concatenate([mixed(g, r0, r1) for r0, r1 in chunks(face)], axis=0))
    for n, (j0, j1) in enumerate(pairs(plan.inner)):
        slot = n % 2
        cols = slice(j0 * lanes, j1 * lanes)
        for p in range(2):
            half = slice(p * plan.flat, (p + 1) * plan.flat)
            acc[slot, half] = three(bh[p], bl[p], f2h[half, cols], f2l[half, cols])
        for j in range(j0, j1):
            g = BUF + j
            mine = slice((j - j0) * lanes, (j - j0 + 1) * lanes)
            flat = plan.flat
            product = unfold(plan, lambda at, k: acc[slot, at : at + k, mine], lambda at, k: acc[slot, flat + at : flat + at + k, mine], False)
            product = {r0: block for _, _, blocks in product for r0, block in blocks}
            parts = []
            for r0, r1 in chunks(face):
                own = f2[g, r0:r1, :]
                value = product[r0] + mixed(g, r0, r1)
                parts.append(value + (va[g, r0:r1, :] + CENTER) * own + vd[g, r0:r1, :] * swap(own))
            parts += [product[r0] for r0 in range(face, cross, 16)]
            total = fold(total, g, cross, jnp.concatenate(parts, axis=0))
    both = total[:, :lanes] + total[:, lanes:]
    w = plan.width
    block = both[:w, :w] + both[w:, w:]
    diag[...] = 0.25 * (block + jnp.transpose(block))
    for copy in copies:
        copy.wait()


def face_block(plan, own, other, sign, scale):
    w, lanes = plan.width, plan.lanes
    ah, al = split(own[...])
    bh, bl = split(other[...])
    first = dot_t(ah, jnp.concatenate([bh, bl], axis=1))
    m = first[:, :lanes] + first[:, lanes:] + dot_t(al, bh)
    return scale * (0.25 * sign * (m[w:, :w] - m[:w, w:]) - 0.5 * PENALTY * m[:w, :w])


def early_faces_kernel(plan, paired, ox, oy, oz, nx, ny, nz, blocks):
    oz, nz = sides(oz, paired), sides(nz, paired)[::-1] if paired else nz
    blocks[0] = face_block(plan, ox, nx, -1.0, 1.0)
    for k, (own, other, sign) in enumerate(((oy, ny, 1.0), (oz[0], nz[0], -1.0), (oz[1], nz[1], 1.0))):
        blocks[1 + k] = face_block(plan, own, other, sign, 0.5)


def late_faces_kernel(plan, diag, early, ox, oy, nx, ny, blocks, local, sem):
    copies = [
        pltpu.make_async_copy(diag, blocks.at[0], sem.at[0]),
        pltpu.make_async_copy(early.at[0], blocks.at[1], sem.at[1]),
        pltpu.make_async_copy(early.at[1:4], blocks.at[4:7], sem.at[2]),
        pltpu.make_async_copy(local, blocks.at[2:4], sem.at[3]),
    ]
    for copy in copies[:3]:
        copy.start()
    local[0] = face_block(plan, ox, nx, 1.0, 1.0)
    local[1] = face_block(plan, oy, ny, -1.0, 0.5)
    copies[3].start()
    for copy in copies:
        copy.wait()


def near(*shape):
    return pltpu.VMEM(shape, F32)


def far(*shape):
    return jax.ShapeDtypeStruct(shape, F32)


def call(kernel, outs, args, scratch=(), flops=0, limit=24, aliases=None, far_in=(), far_out=()):
    def place(a, where):
        return pltpu.with_memory_space_constraint(jnp.asarray(a), where)

    placed = [jax.tree.map(lambda b: place(b, pltpu.HBM if i in far_in else pltpu.VMEM), a) for i, a in enumerate(args)]
    space, apart = pl.BlockSpec(memory_space=pltpu.VMEM), pl.BlockSpec(memory_space=pl.ANY)
    return pl.pallas_call(
        kernel,
        out_shape=outs,
        in_specs=[apart if i in far_in else jax.tree.map(lambda b: space, a) for i, a in enumerate(placed)],
        out_specs=[apart if i in far_out else jax.tree.map(lambda b: space, a) for i, a in enumerate(outs)],
        scratch_shapes=list(scratch),
        input_output_aliases=aliases or {},
        compiler_params=pltpu.CompilerParams(vmem_limit_bytes=limit * 1024 * 1024),
        cost_estimate=pl.CostEstimate(flops=flops, bytes_accessed=0, transcendentals=0),
    )(*placed)


def shift(array, axis, step):
    count = lax.axis_size(axis)
    return lax.ppermute(array, axis, [(i, (i + step) % count) for i in range(count)])


def shift_z(both, paired):
    if paired:
        return shift(both, "gz", 1)
    return [shift(both[1], "gz", 1), shift(both[0], "gz", -1)]


def on_device(orbitals, potential):
    cells, width = orbitals.shape[0], orbitals.shape[-1]
    plan = Plan(cells, width)
    lanes, face, strip, rows, cross = plan.lanes, plan.face, plan.strip, plan.rows, plan.cross
    g_all, inner_all, corner = plan.groups, plan.inner, plan.corner
    paired = lax.axis_size("gz") == 2
    part = functools.partial
    bf = lambda *shape: pltpu.VMEM(shape, BF)
    wide = g_all * lanes

    def two(*shape):
        return near(2, *shape) if paired else [near(*shape), near(*shape)]

    srows, rrows, yrows = BUF * strip + 8, BUF * (face // 2 - strip), inner_all * strip + cells
    orb = orbitals.reshape(cells, face, width)
    slo, shi, ylo, yhi, vt = call(
        part(strip_kernel, plan),
        [near(srows, lanes), near(srows, lanes), near(yrows, lanes), near(yrows, lanes), near(cells, face)],
        [orb, potential.reshape(face, cells)],
        [near(cells, strip, width), near(cells, strip, width), near(face, cells), pltpu.SemaphoreType.DMA((3,))],
        far_in=(0, 1),
    )
    from_ylo, from_yhi = shift(yhi, "gy", 1), shift(ylo, "gy", -1)
    from_slo, from_shi = shift(shi, "gx", 1), shift(slo, "gx", -1)
    rlo, rhi, inner = call(
        part(pack_kernel, plan), [near(rrows, lanes), near(rrows, lanes), near(inner_all, face, lanes)], [orb],
    )
    from_rlo, from_rhi = shift(rhi, "gx", 1), shift(rlo, "gx", -1)

    ipick = np.zeros((2, face, lanes), np.float32)
    cpick = np.zeros((2, lanes, lanes), np.float32)
    for side in range(2):
        for k in range(BUF):
            z = side * (cells - BUF) + k
            for y in range(cells):
                ipick[side, y * cells + z, k * cells + y] = 1.0
            for y in range(corner):
                cpick[side, y * cells + z, k * corner + y] = 1.0
    elo, ehi, vx = call(
        part(edge_kernel, plan), [near(srows, lanes), near(srows, lanes), near(plan.trows, face)], [vt, from_slo, from_shi, from_ylo],
        flops=2*10**9,
    )
    from_elo, from_ehi = shift(ehi, "gy", 1), shift(elo, "gy", -1)

    matrix = -0.5 * row_matrix(plan, plan.second, False)
    coef = folded(-0.5 * mirrored(plan, plan.second))
    vspread = np.zeros((plan.trows, 2, g_all, lanes), np.float32)
    for g in range(g_all):
        vspread[g, :, g, :] = 0.5
        vspread[plan.ext - 1 - g, 0, g, :] = 0.5
        vspread[plan.ext - 1 - g, 1, g, :] = -0.5
    vspread = np.tile(vspread.reshape(plan.trows, -1), (3, 1)).astype(ml_dtypes.bfloat16)
    vai, vdi, early = call(
        part(inside_kernel, plan), [near(g_all, face, lanes), near(g_all, face, lanes), near(8, lanes)], [vx, vspread],
    )
    outer, zi = call(
        part(xhalo_kernel, plan, paired),
        [near(BUF, face, lanes), two(g_all * strip + plan.trows, lanes)],
        [inner, vx, elo, ehi, from_rlo, from_rhi, ipick, early],
    )
    zi = shift_z(zi, paired)
    both = pltpu.VMEM((2 * plan.lot, wide), BF)
    acc, order, sh, sl = call(
        part(outside_kernel, plan), [near(g_all, cross, lanes), near(8, lanes), both, both], [inner, outer, coef, vai, vdi],
    )

    room = 2 * strip + (corner - 2 * BUF) * cells
    yh, vy, zc = call(
        part(ypack_kernel, plan, paired),
        [near(g_all, room, lanes), near(plan.trows, lanes), two(g_all * BUF * corner + plan.trows, lanes)],
        [from_ylo, from_yhi, from_elo, from_ehi, cpick, order],
        flops=10**10,
    )
    zc = shift_z(zc, paired)
    rest = 4 * strip
    base = 5 if paired else 6
    acc, sh, sl, xr, vah, vdh = call(
        part(halo_kernel, plan, paired),
        [near(g_all, cross, lanes), both, both, near(g_all, rest, lanes), near(g_all, rest, lanes), near(g_all, rest, lanes)],
        [yh, vy, zi, coef, vspread, acc, sh, sl],
        aliases={base: 0, base + 1: 1, base + 2: 2},
    )

    p = plan.first[BUF, :g_all] + plan.first[BUF, ::-1][:g_all]
    q = plan.first[BUF, :g_all] - plan.first[BUF, ::-1][:g_all]
    dcoef = np.concatenate([np.repeat(p[:, None], width, 1), np.repeat(q[:, None], width, 1)], 1).astype(np.float32)
    msg = near(face, lanes)
    corners = 2 * BUF * corner
    product = folded_rows(plan, matrix)
    second = SECOND * product[:, : plan.flat]
    base = 9 if paired else 10
    filtered, mx, my, mz, _, _ = call(
        part(filter_kernel, plan, paired),
        [near(g_all, cross, lanes), [msg, msg], [msg, msg], two(face, lanes), both, both],
        [zc, inner, outer, xr, vai, vdi, vah, vdh, acc, sh, sl, *halves(product), *halves(second), coef, dcoef, vspread],
        [near(g_all, corners, lanes), near(g_all, rows, lanes), both, both,
         near(g_all, corners, lanes), near(g_all, corners, lanes), near(2, 2 * plan.lot, 2 * lanes)],
        aliases={base: 6 if paired else 7, base + 1: 7 if paired else 8},
    )
    ny = [shift(my[1], "gy", 1), shift(my[0], "gy", -1)]
    nx = [shift(mx[1], "gx", 1), shift(mx[0], "gx", -1)]
    nz = shift_z(mz, paired)

    along = energy(plan)
    bcoef = mirrored(plan, along).reshape(-1, lanes).astype(np.float32)
    diag, basis = call(
        part(own_kernel, plan), [near(width, width), far(cells, face, width)],
        [filtered, vai, vdi, *halves(folded_rows(plan, row_matrix(plan, along, True))[:, : plan.flat, : plan.flat]), bcoef],
        [near(cells, face, width), near(g_all, cross, lanes), bf(cross, inner_all * lanes), bf(cross, inner_all * lanes), bf(g_all, cross, lanes),
         near(2, cross, 2 * lanes), pltpu.SemaphoreType.DMA((cells,))],
        flops=2 * 10**9,
        far_out=(1,),
    )
    (first_faces,) = call(
        part(early_faces_kernel, plan, paired), [near(4, width, width)], [mx[0], my[1], mz, nx[0], ny[1], nz],
    )
    (blocks,) = call(
        part(late_faces_kernel, plan), [far(7, width, width)], [diag, first_faces, mx[1], my[0], nx[1], ny[0]],
        [near(2, width, width), pltpu.SemaphoreType.DMA((4,))], far_out=(0,),
    )
    return basis.reshape(orbitals.shape), blocks[None, None, None]


def solution(mesh):
    return jax.shard_map(
        on_device,
        mesh=mesh,
        in_specs=(P("gx", "gy", "gz", None), P("gx", "gy", "gz")),
        out_specs=(P("gx", "gy", "gz", None), P("gx", "gy", "gz", None, None, None)),
        check_vma=False,
    )
```
